32 devices in a mesh: seq: 8 (over y, x, core), tensor: 4 (over z).
Axes of the slice: x: 2, y: 2, z: 4, core: 2. Of those that a mesh axis runs over, the one named last changes fastest.
Arguments:
- layer_input: bfloat16 [8, 2048, 2048], P('tensor', 'seq'), may hold values from -6 to 6
- segment_ids: int32 [8, 2048], replicated, may hold values from 0 to 3, never falling along the last dimension, each value on 1 to 1024 neighbouring positions
- cotangent: bfloat16 [8, 2048, 2048], P('tensor', 'seq'), may hold values from -6 to 6
- projections: bfloat16 [2048, 3, 2048], P('seq', None, 'tensor'), may hold values from -0.125 to 0.125
- output_weight: bfloat16 [2048, 2048], P('tensor', 'seq'), may hold values from -0.125 to 0.125
- up_weight: bfloat16 [2048, 8192], P('seq', 'tensor'), may hold values from -0.125 to 0.125
- down_weight: bfloat16 [8192, 2048], P('tensor', 'seq'), may hold values from -0.0625 to 0.0625
- norm_gains: bfloat16 [3, 2048], P(None, 'seq'), may hold values from 0.5 to 1.5
- hidden_gain: bfloat16 [4, 2048], P('tensor', 'seq'), may hold values from 0.5 to 1.5
- decays: float32 [6], replicated, may hold values from 0.8 to 0.99
- average_projections: float32 [2048, 3, 2048], P('seq', None, 'tensor'), may hold values from -6 to 6
- average_output: float32 [2048, 2048], P('tensor', 'seq'), may hold values from -6 to 6
- average_up: float32 [2048, 8192], P('seq', 'tensor'), may hold values from -6 to 6
- average_down: float32 [8192, 2048], P('tensor', 'seq'), may hold values from -6 to 6
- average_gains: float32 [3, 2048], P(None, 'seq'), may hold values from -6 to 6
- average_hidden: float32 [4, 2048], P('tensor', 'seq'), may hold values from -6 to 6
Outputs:
- layer_output: bfloat16 [8, 2048, 2048], P('tensor', 'seq')
- input_grad: float32 [8, 2048, 2048], P('tensor', 'seq')
- projections_grad: float32 [2048, 3, 2048], P('seq', None, 'tensor')
- output_weight_grad: float32 [2048, 2048], P('tensor', 'seq')
- up_weight_grad: float32 [2048, 8192], P('seq', 'tensor')
- down_weight_grad: float32 [8192, 2048], P('tensor', 'seq')
- gains_grad: float32 [3, 2048], P(None, 'seq')
- hidden_gain_grad: float32 [4, 2048], P('tensor', 'seq')
- new_average_projections: float32 [2048, 3, 2048], P('seq', None, 'tensor')
- new_average_output: float32 [2048, 2048], P('tensor', 'seq')
- new_average_up: float32 [2048, 8192], P('seq', 'tensor')
- new_average_down: float32 [8192, 2048], P('tensor', 'seq')
- new_average_gains: float32 [3, 2048], P(None, 'seq')
- new_average_hidden: float32 [4, 2048], P('tensor', 'seq')
The draws below stay inside these ranges and needn't reach their ends.
Inputs may be any that keep to these rules, and one draw needn't show every extreme that they name: `segment_ids`: segment ids never fall along a sequence; each document has 1 to 1024 positions.
All inputs are finite; a program needn't handle non-finite values.
Results may differ from the reference program's by a relative error of at most 0.02.
Values may be sent and summed in bfloat16 or wider, within the bound.
No kernel may reach another device: no remote copies, remote signals or barrier semaphores. Data moves between devices by JAX's collectives and lax.ppermute only.
A program may use at most 448 MiB of HBM per device.

```python
import math
import jax
import jax.numpy as jnp
import numpy as np
from jax import lax

D = 2048
HEADS = 32
HEAD_DIM = 64
FF = 8192
SEQ_LEN = 2048
SEQS = 8
SCALE_BASE = 512
DOCS = 4
N_TENSOR = 4


def levels(own_key, shape, split, least, largest):
    gain = 1.0
    for axis_at, parts in split:
        heights = jax.random.uniform(jax.random.fold_in(jax.random.fold_in(own_key, 6), axis_at), (parts,), jnp.float32, least / len(split), largest / len(split))
        gain = gain * jnp.repeat(jnp.exp(heights), shape[axis_at] // parts).reshape((-1,) + (1,) * (len(shape) - 1 - axis_at))
    return gain


def length_profile(number_of, total, bound, skew):
    portions = [(1 << 20) // math.isqrt(rank ** skew) + 1 for rank in range(2, number_of + 1)]
    rest, holding = total - bound - (number_of - 1), [1] * (number_of - 1)
    while rest > 0:
        movable = [i for i in range(number_of - 1) if holding[i] < bound]
        mass, left = sum([portions[i] for i in movable]), rest
        for i in movable:
            addition = min(bound - holding[i], max(1, left * portions[i] // mass), rest)
            holding[i] = holding[i] + addition
            rest = rest - addition
    return np.array([bound] + holding)


def uneven_parts(own_key, amount, total, bound, lean):
    if amount == 2:
        one = jax.random.randint(own_key, (), max(1, total - bound), min(bound, total - 1) + 1)
        return jnp.stack([one, total - one])
    lengths = jnp.asarray(length_profile(amount, total, bound, lean), jnp.int32)
    couples = (amount - 1) // 2
    source_of, receiver = lengths[1:1 + 2 * couples:2], lengths[2:2 + 2 * couples:2]
    margin = jnp.minimum(source_of - 1, bound - receiver)
    moved = jax.random.randint(jax.random.fold_in(own_key, 1), (couples,), 0, 1 << 20) % (margin + 1)
    lengths = lengths.at[1:1 + 2 * couples:2].set(source_of - moved).at[2:2 + 2 * couples:2].set(receiver + moved)
    return lengths[jax.random.permutation(jax.random.fold_in(own_key, 2), amount)]


def noise(key, shape, spread, limit, pieces=(), held_as=jnp.bfloat16):
    values = jax.random.normal(key, shape, jnp.float32) * spread
    if len(pieces) > 0:
        values = levels(key, shape, pieces, -0.22, 0.18) * values
    return jnp.clip(values, min=-limit, max=limit).astype(held_as)


def setup_inputs(seed: int = 0) -> dict:
    seeds = jax.random.split(jax.random.key(seed), 17)
    layer_input = noise(seeds[0], (SEQS, SEQ_LEN, D), 1.0, 6.0, ((0, 4), (1, 8)))
    segment_ids = jax.vmap(lambda own: jnp.searchsorted(jnp.cumsum(uneven_parts(own, DOCS, SEQ_LEN, SEQ_LEN // 2, 2)), jnp.arange(SEQ_LEN), side="right"))(jax.random.split(seeds[1], SEQS)).reshape((SEQS, SEQ_LEN)).astype(jnp.int32)
    cotangent = noise(seeds[2], (SEQS, SEQ_LEN, D), 1.0, 6.0, ((0, 4), (1, 8)))
    projections = noise(seeds[3], (D, 3, D), D ** -0.5, 0.125, ((0, 8), (2, 4)))
    output_weight = noise(seeds[4], (D, D), D ** -0.5, 0.125, ((0, 4), (1, 8)))
    up_weight = noise(seeds[5], (D, FF), D ** -0.5, 0.125, ((0, 8), (1, 4)))
    down_weight = noise(seeds[6], (FF, D), FF ** -0.5, 0.0625, ((0, 4), (1, 8)))
    norm_gains = jnp.clip(1.0 + 0.1 * jax.random.normal(seeds[7], (3, D), jnp.float32), 0.5, 1.5).astype(jnp.bfloat16)
    hidden_gain = jnp.clip(1.0 + 0.1 * jax.random.normal(seeds[8], (N_TENSOR, FF // N_TENSOR), jnp.float32), 0.5, 1.5).astype(jnp.bfloat16)
    decays = jnp.clip(jax.random.uniform(seeds[9], (6,), jnp.float32, 0.8, 0.99), 0.8, 0.99)
    average_projections = noise(seeds[10], (D, 3, D), 1.0, 6.0, ((0, 8), (2, 4)), jnp.float32)
    average_output = noise(seeds[11], (D, D), 1.0, 6.0, ((0, 4), (1, 8)), jnp.float32)
    average_up = noise(seeds[12], (D, FF), 1.0, 6.0, ((0, 8), (1, 4)), jnp.float32)
    average_down = noise(seeds[13], (FF, D), 1.0, 6.0, ((0, 4), (1, 8)), jnp.float32)
    average_gains = noise(seeds[14], (3, D), 1.0, 6.0, ((1, 8),), jnp.float32)
    average_hidden = noise(seeds[15], (N_TENSOR, FF // N_TENSOR), 1.0, 6.0, ((0, 4), (1, 8)), jnp.float32)
    return {"layer_input": layer_input, "segment_ids": segment_ids, "cotangent": cotangent, "projections": projections, "output_weight": output_weight, "up_weight": up_weight, "down_weight": down_weight, "norm_gains": norm_gains, "hidden_gain": hidden_gain, "decays": decays, "average_projections": average_projections, "average_output": average_output, "average_up": average_up, "average_down": average_down, "average_gains": average_gains, "average_hidden": average_hidden}


@jax.custom_vjp
def low(v):
    return lax.optimization_barrier(v.astype(jnp.bfloat16)).astype(jnp.float32)

@jax.custom_vjp
def low_back(v):
    return v

def low_keep(v):
    return (low(v), None)

def low_pass(kept, grad):
    return (grad,)

def back_keep(v):
    return (v, None)

def back_low(kept, grad):
    return (low(grad),)
low.defvjp(low_keep, low_pass)
low_back.defvjp(back_keep, back_low)
EPSILON = 1e-05
MASKED_SCORE = -1e+30
EXACT = lax.Precision.HIGHEST

def norm_rows(features, gain_row):
    row_mean = lax.optimization_barrier(jnp.mean(features, axis=-1, keepdims=True))
    second = lax.optimization_barrier(jnp.mean(features * features, axis=-1, keepdims=True))
    return (features - row_mean) * lax.rsqrt(second - row_mean * row_mean + EPSILON) * gain_row

def xpos_tables(positions):
    half_dim = HEAD_DIM // 2
    pair_index = jnp.arange(half_dim, dtype=jnp.float32)
    frequency = 10000.0 ** (-pair_index / half_dim)
    angles = positions[:, None] * frequency[None, :]
    zeta_base = (pair_index / half_dim + 0.4) / 1.4
    growth = zeta_base[None, :] ** ((positions[:, None] - SEQ_LEN // 2) / SCALE_BASE)
    return (jnp.cos(angles)[:, None, :], jnp.sin(angles)[:, None, :], growth[:, None, :])

def xpos_turn(features, cosine, sine_table, factor_row):
    half_dim = features.shape[-1] // 2
    lower_half = features[..., :half_dim]
    upper_half = features[..., half_dim:]
    return jnp.concatenate([(lower_half * cosine - upper_half * sine_table) * factor_row, (upper_half * cosine + lower_half * sine_table) * factor_row], axis=-1)

def layer(inputs, projections, output_weight, up_weight, down_weight, norm_gains, hidden_gain, segments):
    positions = jnp.arange(SEQ_LEN, dtype=jnp.float32)
    cosine, sine_table, growth = xpos_tables(positions)
    factor = HEAD_DIM ** (-0.5)
    normed_in = low(norm_rows(inputs, norm_gains[0]))
    projected = low_back(jnp.einsum('pld,dce->plce', normed_in, projections, precision=EXACT))
    head_shape = (inputs.shape[0], SEQ_LEN, HEADS, HEAD_DIM)
    queries = low(xpos_turn(projected[:, :, 0].reshape(head_shape), cosine, sine_table, growth))
    key_rows = low(xpos_turn(projected[:, :, 1].reshape(head_shape), cosine, sine_table, 1.0 / growth))
    values = low(projected[:, :, 2].reshape(head_shape))
    places = jnp.arange(SEQ_LEN, dtype=jnp.int32)
    allowed = (places[None, :, None] >= places[None, None, :]) & (segments[:, :, None] == segments[:, None, :])

    def one_head(bundle):
        head_query, head_key, head_value = bundle
        scores = low_back(jnp.einsum('pid,pjd->pij', head_query, head_key, precision=EXACT) * factor)
        scores = jnp.where(allowed, scores, MASKED_SCORE)
        row_max = lax.optimization_barrier(jnp.max(scores, axis=-1, keepdims=True))
        exponent = jnp.exp(scores - row_max)
        weights = exponent / lax.optimization_barrier(jnp.sum(exponent, axis=-1, keepdims=True))
        return jnp.einsum('pij,pjd->pid', low(weights), head_value, precision=EXACT)
    attended = lax.map(jax.checkpoint(one_head), (jnp.moveaxis(queries, 2, 0), jnp.moveaxis(key_rows, 2, 0), jnp.moveaxis(values, 2, 0)))
    attended = low_back(jnp.moveaxis(attended, 0, 2).reshape(inputs.shape))
    inner_rows = low(norm_rows(attended, norm_gains[1]))
    residual = inputs + low_back(jnp.einsum('pld,de->ple', inner_rows, output_weight, precision=EXACT))
    normed_mid = low(norm_rows(residual, norm_gains[2]))
    hidden = low_back(jnp.einsum('pld,df->plf', normed_mid, up_weight, precision=EXACT))
    squeezed = low(norm_rows(jax.nn.gelu(hidden, approximate=False), hidden_gain.reshape(FF)))
    return residual + low_back(jnp.einsum('plf,fd->pld', squeezed, down_weight, precision=EXACT))

def reference(layer_input, segment_ids, cotangent, projections, output_weight, up_weight, down_weight, norm_gains, hidden_gain, decays, average_projections, average_output, average_up, average_down, average_gains, average_hidden):
    params = tuple((weight.astype(jnp.float32) for weight in (projections, output_weight, up_weight, down_weight, norm_gains, hidden_gain)))
    group_count = SEQS // 2
    inputs = layer_input.astype(jnp.float32).reshape(group_count, 2, SEQ_LEN, D)
    cotangents = cotangent.astype(jnp.float32).reshape(group_count, 2, SEQ_LEN, D)
    segments = segment_ids.reshape(group_count, 2, SEQ_LEN)

    def group_step(running, bundle):
        group_in, group_cot, group_seg = bundle

        def forward(group_values, *weights_now):
            return layer(group_values, *weights_now, group_seg)
        group_out, pullback = jax.vjp(forward, group_in, *params)
        new_grads = pullback(group_cot)
        running = tuple((running_term + new_term for running_term, new_term in zip(running, new_grads[1:])))
        return (running, (group_out.astype(jnp.bfloat16), new_grads[0]))
    zero_sums = tuple((jnp.zeros(weight.shape, jnp.float32) for weight in params))
    summed_grads, (outputs, input_grads) = lax.scan(group_step, zero_sums, (inputs, cotangents, segments))
    averages = (average_projections, average_output, average_up, average_down, average_gains, average_hidden)
    updated = tuple((decays[member] * averages[member] + (1.0 - decays[member]) * summed_grads[member] for member in range(6)))
    return (outputs.reshape(SEQS, SEQ_LEN, D), input_grads.reshape(SEQS, SEQ_LEN, D), summed_grads[0], summed_grads[1], summed_grads[2], summed_grads[3], summed_grads[4], summed_grads[5], updated[0], updated[1], updated[2], updated[3], updated[4], updated[5])
```

```python
from functools import partial

import jax
import jax.numpy as jnp
import numpy as np
from jax import lax
from jax.experimental import pallas as pl
from jax.experimental.pallas import tpu as pltpu
from jax.sharding import PartitionSpec as P

HEAD_DIM = 64
HALF = HEAD_DIM // 2
SEQ_LEN = 2048
SCALE_BASE = 512
EPSILON = 1e-05
MASKED_SCORE = -1e30
FACTOR = HEAD_DIM ** (-0.5)
BF = jnp.bfloat16
F32 = jnp.float32
VMEM_LIMIT = 56 * 1024 * 1024


def swap(block, bit):
    size = lax.axis_size("seq")
    return lax.ppermute(block, "seq", [(i, i ^ bit) for i in range(size)])


def gather_rows(rows):
    size = lax.axis_size("seq")
    if size == 8:
        half = rows.shape[0] // 2
        across = swap(rows, 2)
        along = swap(rows, 4)
        corner_low = swap(across[:half], 4)
        corner_high = swap(along[half:], 2)
        even = jnp.concatenate([rows, across, along, corner_low, corner_high])
    else:
        even, bit = rows, 2
        while bit < size:
            even = jnp.concatenate([even, swap(even, bit)])
            bit *= 2
    return even, swap(even, 1)


def scatter_rows(even, odd, count):
    size = lax.axis_size("seq")
    total = even.astype(F32) + swap(odd, 1).astype(F32)
    if size == 8:
        half = count // 2
        own, across, along, corner = (total[i * count : (i + 1) * count] for i in range(4))
        low = swap(corner[:half].astype(BF), 4).astype(F32)
        high = swap(corner[half:].astype(BF), 2).astype(F32)
        across = jnp.concatenate([across[:half] + low, across[half:]]).astype(BF)
        along = jnp.concatenate([along[:half], along[half:] + high]).astype(BF)
        return own + swap(across, 2).astype(F32) + swap(along, 4).astype(F32)
    bit = size // 2
    while bit > 1:
        middle = total.shape[0] // 2
        total = total[:middle] + swap(total[middle:].astype(BF), bit).astype(F32)
        bit //= 2
    return total


def sum_blocks(stats):
    size = stats.shape[0]
    bit = 1
    while bit < size:
        shift = (bit & 1) * (size // 2) + (bit >> 1)
        other = swap(stats, bit)
        stats = stats + jnp.stack([other[i ^ shift] for i in range(size)])
        bit *= 2
    return stats


def row_norm(features):
    mean = jnp.mean(features, axis=-1, keepdims=True)
    second = jnp.mean(features * features, axis=-1, keepdims=True)
    inverse = lax.rsqrt(second - mean * mean + EPSILON)
    return (features - mean) * inverse, inverse


def row_norm_back(scaled, normed, inverse):
    return inverse * (
        scaled
        - jnp.mean(scaled, axis=-1, keepdims=True)
        - normed * jnp.mean(scaled * normed, axis=-1, keepdims=True)
    )


def dot(a, b, dims):
    return lax.dot_general(a, b, (dims, ((), ())), preferred_element_type=F32)


NN = ((1,), (0,))
NT = ((1,), (1,))
TN = ((0,), (0,))


def qkv_kernel(place, x_ref, w_ref, cq_ref, sq_ref, ck_ref, sk_ref, q_ref, k_ref, v_ref):
    cols = q_ref.shape[1]
    half = cols // 2
    full = dot(x_ref[...], w_ref[...], NT)
    q1, q2 = full[:, :half], full[:, half:cols]
    k1, k2 = full[:, cols : cols + half], full[:, cols + half : 2 * cols]
    cq, sq, ck, sk = cq_ref[...], sq_ref[...], ck_ref[...], sk_ref[...]
    q_ref[:, :half] = (q1 * cq - q2 * sq).astype(BF)
    q_ref[:, half:] = (q2 * cq + q1 * sq).astype(BF)
    k_ref[:, :half] = (k1 * ck - k2 * sk).astype(BF)
    k_ref[:, half:] = (k2 * ck + k1 * sk).astype(BF)
    v_ref[...] = full[:, 2 * cols :].astype(BF)


def project(place, rows, weights, tables, count):
    length, width = rows.shape
    size = length // count
    cols = weights.shape[0] // 3
    table = pl.BlockSpec((count, cols // 2), lambda i, place: (place[i], 0))
    out = pl.BlockSpec((count, cols), lambda i, place: (place[i], 0))
    return pl.pallas_call(
        qkv_kernel,
        grid_spec=pltpu.PrefetchScalarGridSpec(
            num_scalar_prefetch=1,
            grid=(size,),
            in_specs=[
                pl.BlockSpec((count, width), lambda i, place: (i, 0)),
                pl.BlockSpec((3 * cols, width), lambda i, place: (0, 0)),
                table,
                table,
                table,
                table,
            ],
            out_specs=[out, out, out],
        ),
        out_shape=[jax.ShapeDtypeStruct((length, cols), BF)] * 3,
        compiler_params=pltpu.CompilerParams(vmem_limit_bytes=VMEM_LIMIT),
        cost_estimate=pl.CostEstimate(
            flops=2 * length * width * 3 * cols,
            bytes_accessed=2 * (length * width + 3 * cols * width + 3 * length * cols),
            transcendentals=0,
        ),
        name="project",
    )(place, rows, weights, *tables)


def head_mask(shape, head, heads, turned):
    lane = lax.broadcasted_iota(jnp.int32, shape, 1)
    if turned:
        return (lane // HALF) % heads == head
    return lane // HEAD_DIM == head


def attend_kernel(first, q_ref, k_ref, v_ref, start_ref, o_ref, lse_ref, scores, vcat):
    i = pl.program_id(0)
    rows, cols = q_ref.shape
    heads = cols // HEAD_DIM
    blocks = k_ref.shape[0] // rows

    @pl.when(i == 0)
    def _():
        for b in range(blocks):
            value = v_ref[b * rows : (b + 1) * rows, :]
            for h in range(heads):
                vcat[b, h * rows : (h + 1) * rows, :] = jnp.where(
                    head_mask((rows, cols), h, heads, False), value, jnp.zeros_like(value)
                )

    query = q_ref[...]
    parts = [
        jnp.where(head_mask((rows, cols), h, heads, True), query, jnp.zeros_like(query))
        for h in range(heads)
    ]
    start = start_ref[...]
    low = first[i]
    place = i * rows + lax.broadcasted_iota(jnp.int32, (rows, rows), 0)
    lane = lax.broadcasted_iota(jnp.int32, (rows, rows), 1)

    def score_block(j, tops):
        column = j * rows + lane
        keep = (column <= place) & (column >= start)
        key = k_ref[pl.ds(pl.multiple_of(j * rows, rows), rows), :]
        new = []
        for h in range(heads):
            score = jnp.where(keep, dot(parts[h], key, NT), MASKED_SCORE)
            scores[j, h] = score
            new.append(jnp.maximum(tops[h], jnp.max(score, axis=1, keepdims=True)))
        return tuple(new)

    tops = lax.fori_loop(
        low, i + 1, score_block, tuple(jnp.full((rows, 1), MASKED_SCORE, F32) for _ in range(heads))
    )

    def value_block(j, carry):
        sums, total = carry
        chances, new = [], []
        for h in range(heads):
            chance = jnp.exp(scores[j, h] - tops[h])
            new.append(sums[h] + jnp.sum(chance, axis=1, keepdims=True))
            chances.append(chance.astype(BF))
        total = total + dot(jnp.concatenate(chances, axis=1), vcat[j], NN)
        return tuple(new), total

    sums, total = lax.fori_loop(
        low,
        i + 1,
        value_block,
        (tuple(jnp.zeros((rows, 1), F32) for _ in range(heads)), jnp.zeros((rows, cols), F32)),
    )
    scale = jnp.zeros((rows, cols), F32)
    for h in range(heads):
        scale = jnp.where(head_mask((rows, cols), h, heads, False), 1.0 / sums[h], scale)
        lse_ref[:, h : h + 1] = tops[h] + jnp.log(sums[h])
    o_ref[...] = total * scale


def attend(first, query, key, value, start_column, count):
    length, cols = query.shape
    heads = cols // HEAD_DIM
    size = length // count
    whole = pl.BlockSpec((length, cols), lambda i, first: (0, 0))
    return pl.pallas_call(
        attend_kernel,
        grid_spec=pltpu.PrefetchScalarGridSpec(
            num_scalar_prefetch=1,
            grid=(size,),
            in_specs=[
                pl.BlockSpec((count, cols), lambda i, first: (i, 0)),
                whole,
                whole,
                pl.BlockSpec((count, 1), lambda i, first: (i, 0)),
            ],
            out_specs=[
                pl.BlockSpec((count, cols), lambda i, first: (i, 0)),
                pl.BlockSpec((count, heads), lambda i, first: (i, 0)),
            ],
            scratch_shapes=[
                pltpu.VMEM((size, heads, count, count), F32),
                pltpu.VMEM((size, heads * count, cols), BF),
            ],
        ),
        out_shape=[
            jax.ShapeDtypeStruct((length, cols), F32),
            jax.ShapeDtypeStruct((length, heads), F32),
        ],
        compiler_params=pltpu.CompilerParams(vmem_limit_bytes=VMEM_LIMIT),
        cost_estimate=pl.CostEstimate(
            flops=4 * length * length * cols,
            bytes_accessed=10 * length * cols,
            transcendentals=heads * length * length // 4,
        ),
        name="attend",
    )(first, query, key, value, start_column)


def attend_back_kernel(
    first, spot, q_ref, k_ref, v_ref, do_ref, lse_ref, delta_ref, start_ref,
    cq_ref, sq_ref, ck_ref, sk_ref, out_ref, kcat, dk_ref, dv_ref,
):
    i = pl.program_id(0)
    rows, cols = q_ref.shape
    half = cols // 2
    heads = cols // HEAD_DIM
    blocks = k_ref.shape[0] // rows

    @pl.when(i == 0)
    def _():
        dk_ref[...] = jnp.zeros_like(dk_ref)
        dv_ref[...] = jnp.zeros_like(dv_ref)
        for b in range(blocks):
            key = k_ref[b * rows : (b + 1) * rows, :]
            for h in range(heads):
                kcat[b, h * rows : (h + 1) * rows, :] = jnp.where(
                    head_mask((rows, cols), h, heads, True), key, jnp.zeros_like(key)
                )

    query, grad = q_ref[...], do_ref[...]
    parts = [
        jnp.where(head_mask((rows, cols), h, heads, True), query, jnp.zeros_like(query))
        for h in range(heads)
    ]
    grads = [
        jnp.where(head_mask((rows, cols), h, heads, False), grad, jnp.zeros_like(grad))
        for h in range(heads)
    ]
    query_stack = jnp.concatenate(parts, axis=0)
    grad_stack = jnp.concatenate(grads, axis=0)
    start = start_ref[...]
    place = i * rows + lax.broadcasted_iota(jnp.int32, (rows, rows), 1)
    line = lax.broadcasted_iota(jnp.int32, (rows, rows), 0)

    def block(j, total):
        where = pl.ds(pl.multiple_of(j * rows, rows), rows)
        column = j * rows + line
        keep = (column <= place) & (column >= start)
        key, value = k_ref[where, :], v_ref[where, :]
        chances, slopes = [], []
        for h in range(heads):
            score = jnp.where(keep, dot(key, parts[h], NT), MASKED_SCORE)
            chance = jnp.exp(score - lse_ref[h : h + 1, :])
            product = dot(value, grads[h], NT)
            slopes.append((chance * (product - delta_ref[h : h + 1, :])).astype(BF))
            chances.append(chance.astype(BF))
        slope = jnp.concatenate(slopes, axis=1)
        dk_ref[where, :] += dot(slope, query_stack, NN)
        dv_ref[where, :] += dot(jnp.concatenate(chances, axis=1), grad_stack, NN)
        return total + dot(jnp.concatenate(slopes, axis=0), kcat[j], TN)

    total = lax.fori_loop(first[i], i + 1, block, jnp.zeros((rows, cols), F32))
    here = pl.ds(pl.multiple_of(i * rows, rows), rows)
    target = pl.ds(pl.multiple_of(spot[i] * rows, rows), rows)
    cq, sq = cq_ref[here, :], sq_ref[here, :]
    d1, d2 = total[:, :half], total[:, half:]
    out_ref[0, target, :half] = (d1 * cq + d2 * sq).astype(BF)
    out_ref[0, target, half:] = (d2 * cq - d1 * sq).astype(BF)

    @pl.when(i == pl.num_programs(0) - 1)
    def _():
        def finish(j, carry):
            where = pl.ds(pl.multiple_of(j * rows, rows), rows)
            goal = pl.ds(pl.multiple_of(spot[j] * rows, rows), rows)
            ck, sk = ck_ref[where, :], sk_ref[where, :]
            k1, k2 = dk_ref[where, :half], dk_ref[where, half:]
            out_ref[1, goal, :half] = (k1 * ck + k2 * sk).astype(BF)
            out_ref[1, goal, half:] = (k2 * ck - k1 * sk).astype(BF)
            out_ref[2, goal, :] = dv_ref[where, :].astype(BF)
            return carry

        lax.fori_loop(0, blocks, finish, 0)


def attend_back(first, spot, query, key, value, grad, lse, delta, start_row, tables, count):
    length, cols = query.shape
    heads = cols // HEAD_DIM
    size = length // count
    whole = pl.BlockSpec((length, cols), lambda i, *_: (0, 0))
    table = pl.BlockSpec((length, cols // 2), lambda i, *_: (0, 0))
    rows = pl.BlockSpec((count, cols), lambda i, *_: (i, 0))
    line = pl.BlockSpec((pl.squeezed, heads, count), lambda i, *_: (i, 0, 0))
    return pl.pallas_call(
        attend_back_kernel,
        grid_spec=pltpu.PrefetchScalarGridSpec(
            num_scalar_prefetch=2,
            grid=(size,),
            in_specs=[
                rows,
                whole,
                whole,
                rows,
                line,
                line,
                pl.BlockSpec((pl.squeezed, 1, count), lambda i, *_: (i, 0, 0)),
                table,
                table,
                table,
                table,
            ],
            out_specs=pl.BlockSpec((3, length, cols), lambda i, *_: (0, 0, 0)),
            scratch_shapes=[
                pltpu.VMEM((size, heads * count, cols), BF),
                pltpu.VMEM((length, cols), F32),
                pltpu.VMEM((length, cols), F32),
            ],
        ),
        out_shape=jax.ShapeDtypeStruct((3, length, cols), BF),
        compiler_params=pltpu.CompilerParams(vmem_limit_bytes=VMEM_LIMIT),
        cost_estimate=pl.CostEstimate(
            flops=10 * length * length * cols,
            bytes_accessed=20 * length * cols,
            transcendentals=heads * length * length // 4,
        ),
        name="attend_back",
    )(first, spot, query, key, value, grad, lse, delta, start_row, *tables)


def xpos_tables(heads, scale):
    positions = jnp.arange(SEQ_LEN, dtype=F32)
    pair_index = jnp.arange(HALF, dtype=F32)
    frequency = 10000.0 ** (-pair_index / HALF)
    angles = positions[:, None] * frequency[None, :]
    zeta_base = (pair_index / HALF + 0.4) / 1.4
    growth = zeta_base[None, :] ** ((positions[:, None] - SEQ_LEN // 2) / SCALE_BASE)
    cosine, sine = jnp.cos(angles), jnp.sin(angles)
    tables = (cosine * growth * scale, sine * growth * scale, cosine / growth, sine / growth)
    return tuple(jnp.tile(table, (1, heads)) for table in tables)


def on_device(
    layer_input,
    segment_ids,
    cotangent,
    projections,
    output_weight,
    up_weight,
    down_weight,
    norm_gains,
    hidden_gain,
    decays,
    average_projections,
    average_output,
    average_up,
    average_down,
    average_gains,
    average_hidden,
):
    size = lax.axis_size("seq")
    groups = lax.axis_size("tensor")
    me = lax.axis_index("seq")
    group = lax.axis_index("tensor")
    chunks, count, width = layer_input.shape
    length = segment_ids.shape[1]
    block_cols = projections.shape[2]
    heads = width // HEAD_DIM
    per_block = block_cols // HEAD_DIM
    mine = heads // size
    cols = mine * HEAD_DIM
    even_split = per_block % size == 0
    units = up_weight.shape[1] // size
    hidden_cols = units * groups
    hidden_total = hidden_cols * size

    gains_all = lax.all_gather(norm_gains, "seq", axis=1, tiled=True).astype(F32)
    gain_attn, gain_ffn = gains_all[0], gains_all[2]
    each = per_block // size if even_split else 1

    def to_order(rows):
        if not even_split:
            return rows
        shaped = rows.reshape((groups, size, each * HEAD_DIM) + rows.shape[1:])
        return jnp.swapaxes(shaped, 0, 1).reshape(rows.shape)

    def from_order(rows):
        if not even_split:
            return rows
        shaped = rows.reshape((size, groups, each * HEAD_DIM) + rows.shape[1:])
        return jnp.swapaxes(shaped, 0, 1).reshape(rows.shape)

    gain_inner = to_order(gains_all[1])
    gain_hidden = lax.all_gather(hidden_gain, "tensor", axis=0, tiled=True)
    gain_hidden = gain_hidden.astype(F32).reshape(hidden_cols)

    inputs = [layer_input[c].astype(F32) for c in range(chunks)]
    normed = [row_norm(rows) for rows in inputs]
    normed_in = [
        jnp.concatenate(gather_rows((normed[c][0] * gain_attn).astype(BF))) for c in range(chunks)
    ]

    turned = projections.transpose(1, 2, 0)
    if even_split:
        sent = turned.reshape(3, size, each * HEAD_DIM, count).transpose(1, 0, 2, 3)
        came = lax.all_to_all(sent, "seq", 0, 0, tiled=True)
        proj = lax.all_gather(came, "tensor", axis=0, tiled=False)
        proj = proj.transpose(2, 0, 3, 1, 4).reshape(3, cols, width)
    else:
        wide = lax.all_gather(turned, "tensor", axis=1, tiled=True)
        sent = wide.reshape(3, size, cols, count).transpose(1, 0, 2, 3)
        came = lax.all_to_all(sent, "seq", 0, 0, tiled=True)
        proj = came.transpose(1, 2, 0, 3).reshape(3, cols, width)
    turned_heads = proj[:2].reshape(2, mine, 2, HALF, width).transpose(0, 2, 1, 3, 4)
    proj = jnp.concatenate([turned_heads.reshape(2 * cols, width), proj[2]])

    full_output = lax.all_gather(
        lax.all_gather(output_weight, "tensor", axis=0, tiled=True), "seq", axis=1, tiled=True
    )
    full_output = to_order(full_output)

    sent = up_weight.reshape(count, size, units).transpose(1, 0, 2)
    came = lax.all_to_all(sent, "seq", 0, 0, tiled=True).reshape(width, units)
    up = lax.all_gather(came, "tensor", axis=0, tiled=False)
    up = up.transpose(1, 0, 2).reshape(width, hidden_cols)

    sent = down_weight.reshape(size, units, count)
    came = lax.all_to_all(sent, "seq", 0, 0, tiled=True)
    down = lax.all_gather(came.transpose(1, 0, 2).reshape(units, width), "tensor", axis=0, tiled=True)

    masks = np.concatenate([np.arange(0, size, 2), np.arange(1, size, 2)]).astype(np.int32)
    place = (jnp.asarray(masks) ^ me).astype(jnp.int32)
    blocks = jnp.arange(size, dtype=jnp.int32) ^ me
    spot = (blocks & 1) * (size // 2) + (blocks >> 1)
    tables_turn = xpos_tables(mine, FACTOR)
    segments = lax.dynamic_slice_in_dim(segment_ids, group * chunks, chunks, 0)
    starts = jnp.sum(
        (segments[:, None, :] < segments[:, :, None]).astype(jnp.int32), axis=2
    )
    firsts = starts.reshape(chunks, size, count)[:, :, 0] // count

    kept, residuals, normed_mid, gathered_mid = [], [], [], []
    for c in range(chunks):
        query, key, value = project(place, normed_in[c], proj, tables_turn, count)
        attended, lse = attend(firsts[c], query, key, value, starts[c][:, None], count)
        sent = attended.astype(BF).reshape(size, count, cols)
        came = lax.all_to_all(sent, "seq", 0, 0, tiled=True)
        rows = came.transpose(1, 0, 2).reshape(count, width).astype(F32)
        inner, inner_inverse = row_norm(rows)
        inner_rows = (inner * gain_inner).astype(BF)
        kept.append((query, key, value, attended, lse, inner, inner_inverse, inner_rows))
        residual = inputs[c] + dot(inner_rows, full_output, NN)
        residuals.append(residual)
        normed_mid.append(row_norm(residual))
        gathered_mid.append(
            jnp.concatenate(gather_rows((normed_mid[c][0] * gain_ffn).astype(BF)))
        )

    gathered_cot = [jnp.concatenate(gather_rows(cotangent[c])) for c in range(chunks)]
    middle = length // 2
    outputs, residual_grads, ffn_gain_grads, inner_gain_grads = [], [], [], []
    down_grad, up_grad, output_grad, hidden_gain_grad = 0.0, 0.0, 0.0, 0.0
    input_parts, proj_grad = [], 0.0
    for c in range(chunks):
        hidden = dot(gathered_mid[c], up, NN)
        activated, gelu_pullback = jax.vjp(partial(jax.nn.gelu, approximate=False), hidden)
        squeezed_grad = dot(gathered_cot[c], down, NT)
        scaled = squeezed_grad * gain_hidden
        stats = jnp.stack(
            [
                jnp.sum(activated, axis=1),
                jnp.sum(activated * activated, axis=1),
                jnp.sum(scaled, axis=1),
                jnp.sum(scaled * activated, axis=1),
            ]
        )
        stats = sum_blocks(stats.reshape(4, size, count).transpose(1, 0, 2)) / hidden_total
        stats = stats.transpose(1, 0, 2).reshape(4, length, 1)
        mean, second, scaled_mean, cross = stats
        inverse = lax.rsqrt(second - mean * mean + EPSILON)
        cross = inverse * (cross - mean * scaled_mean)
        hidden_normed = (activated - mean) * inverse
        squeezed = (hidden_normed * gain_hidden).astype(BF)
        hidden_gain_grad = hidden_gain_grad + jnp.sum(squeezed_grad * hidden_normed, axis=0)
        activated_grad = inverse * (scaled - scaled_mean - hidden_normed * cross)
        hidden_grad = gelu_pullback(activated_grad)[0].astype(BF)

        mid_grad = scatter_rows(
            dot(hidden_grad[:middle], up, NT), dot(hidden_grad[middle:], up, NT).astype(BF), count
        )
        outputs.append(
            residuals[c]
            + scatter_rows(
                dot(squeezed[:middle], down, NN), dot(squeezed[middle:], down, NN).astype(BF), count
            )
        )
        down_grad = down_grad + dot(squeezed, gathered_cot[c], TN)
        up_grad = up_grad + dot(gathered_mid[c], hidden_grad, TN)

        normal, inverse = normed_mid[c]
        ffn_gain_grads.append(jnp.sum(mid_grad * normal, axis=0))
        residual_grad = cotangent[c].astype(F32) + row_norm_back(
            mid_grad * gain_ffn, normal, inverse
        )
        residual_grads.append(residual_grad)
        attn_grad = residual_grad.astype(BF)
        query, key, value, attended, lse, inner, inner_inverse, inner_rows = kept[c]
        output_grad = output_grad + dot(inner_rows, attn_grad, TN)
        inner_grad = dot(attn_grad, full_output, NT)
        inner_gain_grads.append(jnp.sum(inner_grad * inner, axis=0))
        attended_grad = row_norm_back(inner_grad * gain_inner, inner, inner_inverse).astype(BF)
        sent = attended_grad.reshape(count, size, cols).transpose(1, 0, 2)
        grad = lax.all_to_all(sent, "seq", 0, 0, tiled=True).reshape(length, cols)
        delta = jnp.sum((grad.astype(F32) * attended).reshape(length, mine, HEAD_DIM), axis=2)
        projected_grad = attend_back(
            firsts[c],
            spot,
            query,
            key,
            value,
            grad,
            lse.reshape(size, count, mine).transpose(0, 2, 1),
            delta.reshape(size, count, mine).transpose(0, 2, 1),
            starts[c].reshape(size, 1, count),
            tables_turn,
            count,
        )
        projected_grad = projected_grad.transpose(1, 0, 2).reshape(length, 3 * cols)
        input_parts.append(
            scatter_rows(
                dot(projected_grad[:middle], proj, NN),
                dot(projected_grad[middle:], proj, NN).astype(BF),
                count,
            )
        )
        proj_grad = proj_grad + dot(projected_grad, normed_in[c], TN)

    input_grads, attn_gain_grads = [], []
    for c in range(chunks):
        normal, inverse = normed[c]
        attn_gain_grads.append(jnp.sum(input_parts[c] * normal, axis=0))
        input_grads.append(
            residual_grads[c] + row_norm_back(input_parts[c] * gain_attn, normal, inverse)
        )
    gain_terms = jnp.stack(
        [sum(attn_gain_grads), from_order(sum(inner_gain_grads)), sum(ffn_gain_grads)]
    )
    gains_grad = lax.psum(
        lax.psum_scatter(gain_terms, "seq", scatter_dimension=1, tiled=True), "tensor"
    )

    scatter = partial(lax.psum_scatter, axis_name="tensor", scatter_dimension=0, tiled=True)
    part = down_grad.astype(BF)
    part = scatter(part).reshape(units, size, count).transpose(1, 0, 2)
    down_final = lax.all_to_all(part, "seq", 0, 0, tiled=True).reshape(size * units, count)
    part = up_grad.astype(BF).reshape(width, groups, units).transpose(1, 0, 2)
    part = scatter(part).reshape(size, count, units)
    part = lax.all_to_all(part, "seq", 0, 0, tiled=True)
    up_final = part.transpose(1, 0, 2).reshape(count, size * units)
    part = from_order(output_grad.astype(BF)).reshape(width, size, count).transpose(1, 0, 2)
    part = lax.psum_scatter(part, "seq", scatter_dimension=0, tiled=True).reshape(width, count)
    output_final = scatter(part)
    part = proj_grad.astype(BF)
    turned_heads = part[: 2 * cols].reshape(2, 2, mine, HALF, width).transpose(0, 2, 1, 3, 4)
    part = jnp.concatenate([turned_heads.reshape(2, cols, width), part[None, 2 * cols :]])
    if even_split:
        part = part.reshape(3, groups, each * HEAD_DIM, width).transpose(1, 0, 2, 3)
        part = scatter(part.reshape(3 * cols, width))
        part = part.reshape(3, each * HEAD_DIM, size, count).transpose(2, 0, 1, 3)
        part = lax.all_to_all(part, "seq", 0, 0, tiled=True)
        proj_final = part.transpose(3, 1, 0, 2).reshape(count, 3, block_cols)
    else:
        part = lax.psum(part, "tensor").reshape(3, cols, size, count).transpose(2, 0, 1, 3)
        part = lax.all_to_all(part, "seq", 0, 0, tiled=True)
        part = part.transpose(3, 1, 0, 2).reshape(count, 3, width)
        proj_final = lax.dynamic_slice_in_dim(part, group * block_cols, block_cols, 2)
    hidden_final = lax.psum_scatter(
        hidden_gain_grad.reshape(groups, units), "tensor", scatter_dimension=0, tiled=True
    )

    grads = (
        proj_final.astype(F32),
        output_final.astype(F32),
        up_final.astype(F32),
        down_final.astype(F32),
        gains_grad.astype(F32),
        hidden_final.astype(F32),
    )
    averages = (
        average_projections,
        average_output,
        average_up,
        average_down,
        average_gains,
        average_hidden,
    )
    updated = tuple(
        decays[i] * averages[i] + (1.0 - decays[i]) * grads[i] for i in range(6)
    )
    return (jnp.stack(outputs).astype(BF), jnp.stack(input_grads)) + grads + updated


def solution(mesh):
    weights = (P("seq", None, "tensor"), P("tensor", "seq"), P("seq", "tensor"), P("tensor", "seq"))
    gains = (P(None, "seq"), P("tensor", "seq"))
    rows = P("tensor", "seq", None)
    return jax.shard_map(
        on_device,
        mesh=mesh,
        in_specs=(rows, P(), rows) + weights + gains + (P(),) + weights + gains,
        out_specs=(rows, rows) + weights + gains + weights + gains,
        check_vma=False,
    )
```

```python
from functools import partial

import jax
import jax.numpy as jnp
import numpy as np
from jax import lax
from jax.experimental import pallas as pl
from jax.experimental.pallas import tpu as pltpu
from jax.sharding import PartitionSpec as P

HEAD_DIM = 64
HALF = HEAD_DIM // 2
SEQ_LEN = 2048
SCALE_BASE = 512
EPSILON = 1e-05
MASKED_SCORE = -1e30
FACTOR = HEAD_DIM ** (-0.5)
BF = jnp.bfloat16
F32 = jnp.float32
HASTE = 3
VMEM_LIMIT = 56 * 1024 * 1024


def swap(block, bit):
    size = lax.axis_size("seq")
    return lax.ppermute(block, "seq", [(i, i ^ bit) for i in range(size)])


def after(array, *others):
    return lax.optimization_barrier((array,) + others)[0]


class Line:
    def __init__(self):
        self.last, self.noted = (), ()

    def put(self, array):
        return after(array, *self.last) if self.last else array

    def note(self, *arrays):
        self.noted += arrays

    def enter(self, array):
        return after(array, *self.last, *self.noted) if self.last + self.noted else array

    def mark(self, *arrays):
        self.last, self.noted = arrays, ()


def join_kernel(*refs):
    parts, out_ref, held, came, left = refs[:-4], refs[-4], refs[-3], refs[-2], refs[-1]
    spots, at = [], 0
    for part in parts:
        spots.append(pl.ds(at, part.shape[0]))
        at += part.shape[0]
    ins = [
        pltpu.make_async_copy(part, held.at[spot], came.at[k])
        for k, (part, spot) in enumerate(zip(parts, spots))
    ]
    outs = [
        pltpu.make_async_copy(held.at[spot], out_ref.at[spot], left.at[k])
        for k, spot in enumerate(spots)
    ]
    for copy in ins:
        copy.start()
    for k, copy in enumerate(ins):
        copy.wait()
        outs[k].start()
    for copy in outs:
        copy.wait()


def join(parts):
    rows, width = sum(part.shape[0] for part in parts), parts[0].shape[1]
    if any(part.shape[0] % 16 for part in parts) or width % 128:
        return jnp.concatenate(parts)
    return pl.pallas_call(
        join_kernel,
        in_specs=[pl.BlockSpec(memory_space=pl.ANY)] * len(parts),
        out_specs=pl.BlockSpec(memory_space=pl.ANY),
        out_shape=jax.ShapeDtypeStruct((rows, width), parts[0].dtype),
        scratch_shapes=[
            pltpu.VMEM((rows, width), parts[0].dtype),
            pltpu.SemaphoreType.DMA((len(parts),)),
            pltpu.SemaphoreType.DMA((len(parts),)),
        ],
        compiler_params=params(),
        cost_estimate=cost(0, 4 * rows * width),
        name="join",
    )(*parts)


class Gather:
    def __init__(self, line, rows):
        self.line = line
        self.size = lax.axis_size("seq")
        self.rows = line.put(rows)
        self.pieces = [self.rows]
        if self.size == 8:
            self.pieces += [swap(self.rows, 2), swap(self.rows, 4)]
        line.note(self.rows)

    def corner(self):
        if self.size == 8:
            half = self.rows.shape[0] // 2
            across = self.line.put(self.pieces[1])[:half]
            along = self.line.put(self.pieces[2])[half:]
            self.pieces += [swap(across, 4), swap(along, 2)]
            self.line.note(across, along)
        return self

    def core(self):
        even = self.line.put(self.pieces[0])
        if self.size == 8:
            even = join([even] + self.pieces[1:])
        else:
            bit = 2
            while bit < self.size:
                even = jnp.concatenate([even, swap(even, bit)])
                bit *= 2
        self.halves = (even, swap(even, 1))
        self.line.note(even)
        return self


class Scatter:
    def __init__(self, line, odd, count):
        self.line, self.count = line, count
        self.size = lax.axis_size("seq")
        self.other = swap(odd, 1)

    def block(self, k, start, stop):
        here = slice(k * self.count + start, k * self.count + stop)
        return self.even[here].astype(F32) + self.other[here].astype(F32)

    def corner(self, even):
        self.even = self.line.put(even)
        if self.size == 8:
            half = self.count // 2
            low = self.block(3, 0, half).astype(BF)
            high = self.block(3, half, self.count).astype(BF)
            self.low, self.high = swap(low, 4), swap(high, 2)
            self.line.note(low, high)
        return self

    def near(self):
        if self.size == 8:
            half = self.count // 2
            low, high = self.line.put(self.low), self.line.put(self.high)
            across = [self.block(1, 0, half) + low.astype(F32), self.block(1, half, self.count)]
            along = [self.block(2, 0, half), self.block(2, half, self.count) + high.astype(F32)]
            across = jnp.concatenate(across).astype(BF)
            along = jnp.concatenate(along).astype(BF)
            self.parts = [swap(across, 2), swap(along, 4)]
            self.line.note(across, along)
        return self

    def total(self):
        if self.size == 8:
            return self.block(0, 0, self.count) + sum(part.astype(F32) for part in self.parts)
        total, bit = self.even.astype(F32) + self.other.astype(F32), self.size // 2
        while bit > 1:
            middle = total.shape[0] // 2
            total = total[:middle] + swap(total[middle:].astype(BF), bit).astype(F32)
            bit //= 2
        return total


class BlockSum:
    def __init__(self, line, stats):
        self.line, self.stats, self.bit = line, line.put(stats), 1
        self.size = stats.shape[0]
        self.send()

    def send(self):
        self.other = swap(self.stats, self.bit)
        self.line.note(self.stats)

    def add(self):
        shift = (self.bit & 1) * (self.size // 2) + (self.bit >> 1)
        other = self.line.put(self.other)
        self.stats = self.stats + jnp.stack([other[i ^ shift] for i in range(self.size)])
        self.bit *= 2

    def more(self):
        self.add()
        if self.bit < self.size:
            self.send()

    def total(self):
        while self.bit < self.size:
            self.add()
            if self.bit < self.size:
                self.send()
        return self.stats


def row_norm(features):
    mean = jnp.mean(features, axis=-1, keepdims=True)
    second = jnp.mean(features * features, axis=-1, keepdims=True)
    inverse = lax.rsqrt(second - mean * mean + EPSILON)
    return (features - mean) * inverse, inverse


def row_norm_back(scaled, normed, inverse):
    return inverse * (
        scaled
        - jnp.mean(scaled, axis=-1, keepdims=True)
        - normed * jnp.mean(scaled * normed, axis=-1, keepdims=True)
    )


def dot(a, b, dims):
    return lax.dot_general(a, b, (dims, ((), ())), preferred_element_type=F32)


NN = ((1,), (0,))
NT = ((1,), (1,))
TN = ((0,), (0,))


def params():
    return pltpu.CompilerParams(vmem_limit_bytes=VMEM_LIMIT)


def cost(flops, moved, special=0):
    return pl.CostEstimate(
        flops=int(flops) // HASTE, bytes_accessed=int(moved) // HASTE, transcendentals=int(special) // HASTE
    )


def qkv_kernel(
    place, x_ref, w_ref, cq_ref, sq_ref, ck_ref, sk_ref, qa, ka, va, q_ref, k_ref, v_ref
):
    cols = q_ref.shape[1]
    half = cols // 2
    full = dot(x_ref[...], w_ref[...], NN)
    q1, q2 = full[:, :half], full[:, half:cols]
    k1, k2 = full[:, cols : cols + half], full[:, cols + half : 2 * cols]
    cq, sq, ck, sk = cq_ref[...], sq_ref[...], ck_ref[...], sk_ref[...]
    q_ref[:, :half] = (q1 * cq - q2 * sq).astype(BF)
    q_ref[:, half:] = (q2 * cq + q1 * sq).astype(BF)
    k_ref[:, :half] = (k1 * ck - k2 * sk).astype(BF)
    k_ref[:, half:] = (k2 * ck + k1 * sk).astype(BF)
    v_ref[...] = full[:, 2 * cols :].astype(BF)


def project(place, rows, weights, tables, count, before):
    here, width = rows.shape
    cols = weights.shape[1] // 3
    length = tables[0].shape[0]
    table = pl.BlockSpec((count, cols // 2), lambda i, place: (place[i], 0))
    out = pl.BlockSpec((count, cols), lambda i, place: (place[i], 0))
    held = pl.BlockSpec(memory_space=pl.ANY)
    return pl.pallas_call(
        qkv_kernel,
        grid_spec=pltpu.PrefetchScalarGridSpec(
            num_scalar_prefetch=1,
            grid=(here // count,),
            in_specs=[
                pl.BlockSpec((count, width), lambda i, place: (i, 0)),
                pl.BlockSpec((width, 3 * cols), lambda i, place: (0, 0)),
                table,
                table,
                table,
                table,
                held,
                held,
                held,
            ],
            out_specs=[out, out, out],
        ),
        out_shape=[jax.ShapeDtypeStruct((length, cols), BF)] * 3,
        input_output_aliases={7: 0, 8: 1, 9: 2},
        compiler_params=params(),
        cost_estimate=cost(
            2 * here * width * 3 * cols, 2 * (here * width + 3 * cols * width + 3 * here * cols)
        ),
        name="project",
    )(place, rows, weights, *tables, *before)


def turned_row(kind, head, heads):
    first = kind * heads * HEAD_DIM
    if kind == 2:
        return first + head * HEAD_DIM, first + head * HEAD_DIM + HALF
    return first + head * HALF, first + (heads + head) * HALF


def arrange_kernel(raw_ref, turned_ref, plain_ref):
    parts, size, _, split, count = raw_ref.shape
    each = split // HEAD_DIM
    for kind in range(3):
        for t in range(parts):
            for j in range(each):
                starts = turned_row(kind, t * each + j, parts * each)
                for b in range(size):
                    for h in range(2):
                        here = slice(j * HEAD_DIM + h * HALF, j * HEAD_DIM + (h + 1) * HALF)
                        turned_ref[starts[h] : starts[h] + HALF, b * count : (b + 1) * count] = (
                            raw_ref[t, b, kind, here, :]
                        )
    plain_ref[...] = turned_ref[...].T


def arrange(raw):
    parts, size, _, split, count = raw.shape
    cols, width = parts * split, size * count
    if count % 128:
        proj = raw.transpose(2, 0, 3, 1, 4).reshape(3, cols, width)
        heads = proj[:2].reshape(2, cols // HEAD_DIM, 2, HALF, width).transpose(0, 2, 1, 3, 4)
        turned = jnp.concatenate([heads.reshape(2 * cols, width), proj[2]])
        return turned, turned.T
    return pl.pallas_call(
        arrange_kernel,
        out_shape=[
            jax.ShapeDtypeStruct((3 * cols, width), BF),
            jax.ShapeDtypeStruct((width, 3 * cols), BF),
        ],
        compiler_params=params(),
        cost_estimate=cost(0, 18 * cols * width),
        name="arrange",
    )(raw)


def out_grad_kernel(*refs):
    out_ref = refs[-1]
    parts = (len(refs) - 1) // 2
    total = dot(refs[0][...], refs[parts][...], TN)
    for k in range(1, parts):
        total = total + dot(refs[k][...], refs[parts + k][...], TN)
    low = total.astype(BF)
    count = out_ref.shape[-1]
    for b in range(out_ref.shape[0]):
        out_ref[b] = low[:, b * count : (b + 1) * count].reshape(out_ref.shape[1:])


def out_grad(inners, grads, split):
    size, count, cols = inners[0].shape
    width = size * cols
    count_out = width // size
    if split:
        shape = (size, cols // split, size, split, count_out)
        spec = pl.BlockSpec(
            (size, cols // split, pl.squeezed, split, count_out), lambda i: (0, 0, i, 0, 0)
        )
    else:
        shape = (size, size, cols, count_out)
        spec = pl.BlockSpec((size, pl.squeezed, cols, count_out), lambda i: (0, i, 0, 0))
    parts = len(inners)
    return pl.pallas_call(
        out_grad_kernel,
        grid=(size,),
        in_specs=[pl.BlockSpec((pl.squeezed, count, cols), lambda i: (i, 0, 0))] * parts
        + [pl.BlockSpec((count, width), lambda i: (0, 0))] * parts,
        out_specs=spec,
        out_shape=jax.ShapeDtypeStruct(shape, BF),
        compiler_params=params(),
        cost_estimate=cost(
            2 * parts * count * width * width, 4 * parts * count * width + 2 * width * width
        ),
        name="out_grad",
    )(*inners, *grads).reshape(size, width, count_out)


def head_rows(weight, b, split):
    return weight[:, b].reshape(-1, weight.shape[-1]) if split else weight[b]


def out_kernel(
    split, place, came_ref, even_ref, odd_ref, x_ref, gi_ref, gf_ref, inner_ref, res_ref, mid_ref, acc
):
    i = pl.program_id(0)
    size, rows, cols = came_ref.shape
    width = size * cols
    count = width // size

    @pl.when(i == 0)
    def _():
        first = jnp.zeros((rows, 1), F32)
        second = jnp.zeros((rows, 1), F32)
        for b in range(size):
            part = came_ref[b].astype(F32)
            first += jnp.sum(part, axis=1, keepdims=True)
            second += jnp.sum(part * part, axis=1, keepdims=True)
        mean = first / width
        inverse = lax.rsqrt(second / width - mean * mean + EPSILON)
        for b in range(size):
            inner_ref[b] = ((came_ref[b].astype(F32) - mean) * inverse * gi_ref[b]).astype(BF)

    def piece(ref):
        total = jnp.zeros((rows, count), F32)
        for b in range(size):
            total += dot(inner_ref[b], head_rows(ref, b, split), NN)
        acc[place[i]] = total

    pl.when(i < size // 2)(lambda: piece(even_ref))
    pl.when(i >= size // 2)(lambda: piece(odd_ref))

    @pl.when(i == size - 1)
    def _():
        first = jnp.zeros((rows, 1), F32)
        second = jnp.zeros((rows, 1), F32)
        for b in range(size):
            here = slice(b * count, (b + 1) * count)
            part = acc[b] + x_ref[:, here].astype(F32)
            res_ref[:, here] = part
            first += jnp.sum(part, axis=1, keepdims=True)
            second += jnp.sum(part * part, axis=1, keepdims=True)
        mean = first / width
        inverse = lax.rsqrt(second / width - mean * mean + EPSILON)
        mid_ref[...] = ((res_ref[...] - mean) * inverse * gf_ref[...]).astype(BF)


def weight_views(pieces, size, cols, split):
    half, count = size // 2, pieces[0].shape[1]
    if split:
        shape = (cols // split, size, split, count)
    else:
        shape = (size, cols, count)
    zeros = (0,) * len(shape)
    views = [piece.reshape((half,) + shape) for piece in pieces]
    specs = [
        pl.BlockSpec((pl.squeezed,) + shape, lambda i, *_: (jnp.minimum(i, half - 1),) + zeros),
        pl.BlockSpec((pl.squeezed,) + shape, lambda i, *_: (jnp.maximum(i - half, 0),) + zeros),
    ]
    return views, specs


def out_project(place, came, pieces, rows, gain_inner, gain_ffn, split):
    size, count, cols = came.shape
    width = size * cols
    views, specs = weight_views(pieces, size, cols, split)
    blocks = pl.BlockSpec((size, count, cols), lambda i, *_: (0, 0, 0))
    flat = pl.BlockSpec((count, width), lambda i, *_: (0, 0))
    return pl.pallas_call(
        partial(out_kernel, split),
        grid_spec=pltpu.PrefetchScalarGridSpec(
            num_scalar_prefetch=1,
            grid=(size,),
            in_specs=[blocks]
            + specs
            + [
                flat,
                pl.BlockSpec((size, 1, cols), lambda i, *_: (0, 0, 0)),
                pl.BlockSpec((1, width), lambda i, *_: (0, 0)),
            ],
            out_specs=[blocks, flat, flat],
            scratch_shapes=[pltpu.VMEM((size, count, width // size), F32)],
        ),
        out_shape=[
            jax.ShapeDtypeStruct((size, count, cols), BF),
            jax.ShapeDtypeStruct((count, width), F32),
            jax.ShapeDtypeStruct((count, width), BF),
        ],
        compiler_params=params(),
        cost_estimate=cost(2 * count * width * width, 2 * width * width + 12 * count * width),
        name="out_project",
    )(place, came, *views, rows, gain_inner, gain_ffn)


def out_back_kernel(
    split, place, grad_ref, res_ref, cot_ref, came_ref, even_ref, odd_ref, gi_ref, gf_ref,
    rg_ref, ag_ref, back_ref, fg_ref, ig_ref, held, sent,
):
    i = pl.program_id(0)
    size, rows, cols = came_ref.shape
    width = size * cols
    count = width // size

    @pl.when(i == 0)
    def _():
        residual, grad = res_ref[...], grad_ref[...]
        mean = jnp.mean(residual, axis=1, keepdims=True)
        second = jnp.mean(residual * residual, axis=1, keepdims=True)
        inverse = lax.rsqrt(second - mean * mean + EPSILON)
        normal = (residual - mean) * inverse
        fg_ref[...] = jnp.sum(grad * normal, axis=0, keepdims=True)
        scaled = grad * gf_ref[...]
        back = inverse * (
            scaled
            - jnp.mean(scaled, axis=1, keepdims=True)
            - normal * jnp.mean(scaled * normal, axis=1, keepdims=True)
        )
        total = cot_ref[...].astype(F32) + back
        rg_ref[...] = total
        low = total.astype(BF)
        ag_ref[...] = low
        for b in range(size):
            sent[b] = low[:, b * count : (b + 1) * count]
        held[...] = jnp.zeros_like(held)

    def piece(ref):
        grad = sent[place[i]]
        for b in range(size):
            held[b] += dot(grad, head_rows(ref, b, split), NT)

    pl.when(i < size // 2)(lambda: piece(even_ref))
    pl.when(i >= size // 2)(lambda: piece(odd_ref))

    @pl.when(i == size - 1)
    def _():
        zero = jnp.zeros((rows, 1), F32)
        first, second = zero, zero
        for b in range(size):
            part = came_ref[b].astype(F32)
            first += jnp.sum(part, axis=1, keepdims=True)
            second += jnp.sum(part * part, axis=1, keepdims=True)
        mean = first / width
        inverse = lax.rsqrt(second / width - mean * mean + EPSILON)
        plain, cross = zero, zero
        for b in range(size):
            normal = (came_ref[b].astype(F32) - mean) * inverse
            grad = held[b]
            ig_ref[b] = jnp.sum(grad * normal, axis=0, keepdims=True)
            scaled = grad * gi_ref[b]
            plain += jnp.sum(scaled, axis=1, keepdims=True)
            cross += jnp.sum(scaled * normal, axis=1, keepdims=True)
        plain, cross = plain / width, cross / width
        for b in range(size):
            normal = (came_ref[b].astype(F32) - mean) * inverse
            back_ref[b] = (inverse * (held[b] * gi_ref[b] - plain - normal * cross)).astype(BF)


def out_back(place, grad, residual, cotangent, came, pieces, gain_inner, gain_ffn, split):
    size, count, cols = came.shape
    width = size * cols
    views, specs = weight_views(pieces, size, cols, split)
    blocks = pl.BlockSpec((size, count, cols), lambda i, *_: (0, 0, 0))
    flat = pl.BlockSpec((count, width), lambda i, *_: (0, 0))
    line = pl.BlockSpec((1, width), lambda i, *_: (0, 0))
    lines = pl.BlockSpec((size, 1, cols), lambda i, *_: (0, 0, 0))
    return pl.pallas_call(
        partial(out_back_kernel, split),
        grid_spec=pltpu.PrefetchScalarGridSpec(
            num_scalar_prefetch=1,
            grid=(size,),
            in_specs=[flat, flat, flat, blocks] + specs + [lines, line],
            out_specs=[flat, flat, blocks, line, lines],
            scratch_shapes=[
                pltpu.VMEM((size, count, cols), F32),
                pltpu.VMEM((size, count, width // size), BF),
            ],
        ),
        out_shape=[
            jax.ShapeDtypeStruct((count, width), F32),
            jax.ShapeDtypeStruct((count, width), BF),
            jax.ShapeDtypeStruct((size, count, cols), BF),
            jax.ShapeDtypeStruct((1, width), F32),
            jax.ShapeDtypeStruct((size, 1, cols), F32),
        ],
        compiler_params=params(),
        cost_estimate=cost(2 * count * width * width, 2 * width * width + 20 * count * width),
        name="out_back",
    )(place, grad, residual, cotangent, came, *views, gain_inner, gain_ffn)


def ffn_grad_kernel(c_ref, down_ref, g_ref, t_ref):
    t_ref[...] = (dot(c_ref[...], down_ref[...], NT) * g_ref[...]).astype(BF)


def ffn_grad(grads, down, gain):
    here, width = grads.shape
    cols = down.shape[0]
    tile = 256
    return pl.pallas_call(
        ffn_grad_kernel,
        grid=(here // tile,),
        in_specs=[
            pl.BlockSpec((tile, width), lambda i: (i, 0)),
            pl.BlockSpec((cols, width), lambda i: (0, 0)),
            pl.BlockSpec((1, cols), lambda i: (0, 0)),
        ],
        out_specs=pl.BlockSpec((tile, cols), lambda i: (i, 0)),
        out_shape=jax.ShapeDtypeStruct((here, cols), BF),
        compiler_params=params(),
        cost_estimate=cost(2 * here * width * cols, 2 * here * (width + cols) + 2 * width * cols),
        name="ffn_grad",
    )(grads, down, gain)


def ffn_in_kernel(given, *refs):
    if given:
        x_ref, t_in_ref, up_ref, a_ref, p_ref, s_ref = refs
    else:
        x_ref, c_ref, up_ref, down_ref, g_ref, a_ref, p_ref, s_ref, t_ref = refs
    parts, _, units = up_ref.shape
    sums = [0.0] * 4
    for k in range(parts):
        here = slice(k * units, (k + 1) * units)
        hidden = dot(x_ref[...], up_ref[k], NN)
        if given:
            scaled = t_in_ref[:, here].astype(F32)
        else:
            low = (dot(c_ref[...], down_ref[here, :], NT) * g_ref[:, here]).astype(BF)
            t_ref[:, here] = low
            scaled = low.astype(F32)
        share = 0.5 * (1.0 + lax.erf(hidden * (2.0**-0.5)))
        activated = hidden * share
        slope = share + hidden * jnp.exp(-0.5 * hidden * hidden) * ((2.0 * np.pi) ** -0.5)
        a_ref[:, here] = activated
        p_ref[:, here] = slope.astype(BF)
        for j, terms in enumerate((activated, activated * activated, scaled, scaled * activated)):
            sums[j] = sums[j] + jnp.sum(terms, axis=1, keepdims=True)
    for j in range(4):
        s_ref[:, j : j + 1] = sums[j]


def ffn_in(rows, up_parts, scaled=None, grads=None, down=None, gain=None):
    given = scaled is not None
    here, width = rows.shape
    parts, _, units = up_parts.shape
    cols = parts * units
    tile = 256
    wide = pl.BlockSpec((tile, width), lambda i: (i, 0))
    out = pl.BlockSpec((tile, cols), lambda i: (i, 0))
    up_spec = pl.BlockSpec(up_parts.shape, lambda i: (0, 0, 0))
    if given:
        arrays, specs = (rows, scaled, up_parts), [wide, out, up_spec]
    else:
        arrays = (rows, grads, up_parts, down, gain)
        specs = [
            wide,
            wide,
            up_spec,
            pl.BlockSpec((cols, width), lambda i: (0, 0)),
            pl.BlockSpec((1, cols), lambda i: (0, 0)),
        ]
    low = jax.ShapeDtypeStruct((here, cols), BF)
    outs = [jax.ShapeDtypeStruct((here, cols), F32), low, jax.ShapeDtypeStruct((here, 4), F32)]
    out_specs = [out, out, pl.BlockSpec((tile, 4), lambda i: (i, 0))]
    result = pl.pallas_call(
        partial(ffn_in_kernel, given),
        grid=(here // tile,),
        in_specs=specs,
        out_specs=out_specs if given else out_specs + [out],
        out_shape=outs if given else outs + [low],
        compiler_params=params(),
        cost_estimate=cost(
            (2 if given else 4) * here * width * cols,
            4 * here * width + 4 * width * cols + 8 * here * cols,
            2 * here * cols,
        ),
        name="ffn_in",
    )(*arrays)
    return result[0], result[1], scaled if given else result[3], result[2]


def ffn_out_kernel(
    a_ref, p_ref, t_ref, s_ref, g_ref, up_ref, down_ref, sq_ref, hg_ref, m_ref, o_ref, n_ref
):
    parts, _, units = up_ref.shape
    stats = s_ref[...]
    mean, inverse, plain, cross = (stats[:, k : k + 1] for k in range(4))
    normal = (a_ref[...] - mean) * inverse
    scaled = t_ref[...].astype(F32)
    squeezed = (normal * g_ref[...]).astype(BF)
    sq_ref[...] = squeezed
    grad = (p_ref[...].astype(F32) * (inverse * (scaled - plain - normal * cross))).astype(BF)
    hg_ref[...] = grad
    total = dot(grad[:, :units], up_ref[0], NT)
    for k in range(1, parts):
        total = total + dot(grad[:, k * units : (k + 1) * units], up_ref[k], NT)
    m_ref[...] = total.astype(BF)
    o_ref[...] = dot(squeezed, down_ref[...], NN).astype(BF)
    part = jnp.sum(scaled * normal, axis=0, keepdims=True)

    @pl.when(pl.program_id(0) == 0)
    def _():
        n_ref[...] = part

    @pl.when(pl.program_id(0) > 0)
    def _():
        n_ref[...] += part


def ffn_out(held, stats, gain, up_parts, down, offset):
    activated, slope, scaled = held
    here, cols = activated.shape
    width = down.shape[1]
    tile = 256
    shift = offset // tile
    out = pl.BlockSpec((tile, cols), lambda i: (i, 0))
    wide = pl.BlockSpec((tile, width), lambda i: (i, 0))
    return pl.pallas_call(
        ffn_out_kernel,
        grid=(here // tile,),
        in_specs=[
            out,
            out,
            out,
            pl.BlockSpec((tile, 4), lambda i: (i + shift, 0)),
            pl.BlockSpec((1, cols), lambda i: (0, 0)),
            pl.BlockSpec(up_parts.shape, lambda i: (0, 0, 0)),
            pl.BlockSpec((cols, width), lambda i: (0, 0)),
        ],
        out_specs=[out, out, wide, wide, pl.BlockSpec((1, cols), lambda i: (0, 0))],
        out_shape=[
            jax.ShapeDtypeStruct((here, cols), BF),
            jax.ShapeDtypeStruct((here, cols), BF),
            jax.ShapeDtypeStruct((here, width), BF),
            jax.ShapeDtypeStruct((here, width), BF),
            jax.ShapeDtypeStruct((1, cols), F32),
        ],
        compiler_params=params(),
        cost_estimate=cost(
            4 * here * width * cols, 12 * here * cols + 4 * width * cols + 4 * here * width
        ),
        name="ffn_out",
    )(activated, slope, scaled, stats, gain, up_parts, down)


def multiply_kernel(x_ref, w_ref, o_ref):
    o_ref[...] = dot(x_ref[...], w_ref[...], NN).astype(BF)


def multiply(rows, weights, offset, here):
    depth, width = weights.shape
    tile = 256
    shift = offset // tile
    return pl.pallas_call(
        multiply_kernel,
        grid=(here // tile,),
        in_specs=[
            pl.BlockSpec((tile, depth), lambda i: (i + shift, 0)),
            pl.BlockSpec((depth, width), lambda i: (0, 0)),
        ],
        out_specs=pl.BlockSpec((tile, width), lambda i: (i, 0)),
        out_shape=jax.ShapeDtypeStruct((here, width), BF),
        compiler_params=params(),
        cost_estimate=cost(2 * here * width * depth, 2 * (here * width + here * depth + depth * width)),
        name="multiply",
    )(rows, weights)


def grads_kernel(weighted, *refs):
    outs = 2 if weighted else 1
    ins = refs[:-outs]
    parts = len(ins) // 2
    total = dot(ins[0][...], ins[parts][...], TN)
    for k in range(1, parts):
        total = total + dot(ins[k][...], ins[parts + k][...], TN)
    refs[-outs][...] = total.astype(BF)
    if weighted:
        refs[-1][...] = jnp.sum(total * ins[-1][...].astype(F32), axis=0, keepdims=True)


def weight_grad(lefts, rights, offsets, weights=None):
    cols, width, here = lefts[0].shape[1], rights[0].shape[1], rights[0].shape[0]
    tile = 512
    count = len(lefts)

    def left_spec(offset):
        return pl.BlockSpec((here, cols), lambda i: (offset // here, 0))

    out_specs = [pl.BlockSpec((cols, tile), lambda i: (0, i))]
    out_shape = [jax.ShapeDtypeStruct((cols, width), BF)]
    extra, extra_specs = (), []
    if weights is not None:
        out_specs.append(pl.BlockSpec((1, tile), lambda i: (0, i)))
        out_shape.append(jax.ShapeDtypeStruct((1, width), F32))
        extra, extra_specs = (weights,), [pl.BlockSpec((cols, tile), lambda i: (0, i))]
    return pl.pallas_call(
        partial(grads_kernel, weights is not None),
        grid=(width // tile,),
        in_specs=[left_spec(offset) for offset in offsets]
        + [pl.BlockSpec((here, tile), lambda i: (0, i))] * count
        + extra_specs,
        out_specs=out_specs,
        out_shape=out_shape,
        compiler_params=params(),
        cost_estimate=cost(
            2 * count * here * width * cols, 2 * (count * here * (width + cols) + cols * width)
        ),
        name="weight_grad",
    )(*lefts, *rights, *extra)


def head_mask(shape, head, heads, turned):
    lane = lax.broadcasted_iota(jnp.int32, shape, 1)
    if turned:
        return (lane // HALF) % heads == head
    return lane // HEAD_DIM == head


def attend_kernel(first, q_ref, k_ref, v_ref, start_ref, o_ref, low_ref, lse_ref, scores, vcat):
    i = pl.program_id(0)
    rows, cols = q_ref.shape
    heads = cols // HEAD_DIM
    blocks = k_ref.shape[0] // rows

    @pl.when(i == 0)
    def _():
        for b in range(blocks):
            value = v_ref[b * rows : (b + 1) * rows, :]
            for h in range(heads):
                vcat[b, h * rows : (h + 1) * rows, :] = jnp.where(
                    head_mask((rows, cols), h, heads, False), value, jnp.zeros_like(value)
                )

    query = q_ref[...]
    parts = [
        jnp.where(head_mask((rows, cols), h, heads, True), query, jnp.zeros_like(query))
        for h in range(heads)
    ]
    start = start_ref[...]
    low = first[i]
    place = i * rows + lax.broadcasted_iota(jnp.int32, (rows, rows), 0)
    lane = lax.broadcasted_iota(jnp.int32, (rows, rows), 1)

    def score_block(j, tops):
        column = j * rows + lane
        keep = (column <= place) & (column >= start)
        key = k_ref[pl.ds(pl.multiple_of(j * rows, rows), rows), :]
        new = []
        for h in range(heads):
            score = jnp.where(keep, dot(parts[h], key, NT), MASKED_SCORE)
            scores[j, h] = score
            new.append(jnp.maximum(tops[h], jnp.max(score, axis=1, keepdims=True)))
        return tuple(new)

    tops = lax.fori_loop(
        low, i + 1, score_block, tuple(jnp.full((rows, 1), MASKED_SCORE, F32) for _ in range(heads))
    )

    def value_block(j, carry):
        sums, total = carry
        chances, new = [], []
        for h in range(heads):
            chance = jnp.exp(scores[j, h] - tops[h])
            new.append(sums[h] + jnp.sum(chance, axis=1, keepdims=True))
            chances.append(chance.astype(BF))
        total = total + dot(jnp.concatenate(chances, axis=1), vcat[j], NN)
        return tuple(new), total

    sums, total = lax.fori_loop(
        low,
        i + 1,
        value_block,
        (tuple(jnp.zeros((rows, 1), F32) for _ in range(heads)), jnp.zeros((rows, cols), F32)),
    )
    scale = jnp.zeros((rows, cols), F32)
    for h in range(heads):
        scale = jnp.where(head_mask((rows, cols), h, heads, False), 1.0 / sums[h], scale)
        lse_ref[:, h : h + 1] = tops[h] + jnp.log(sums[h])
    result = total * scale
    o_ref[...] = result
    low_ref[...] = result.astype(BF)


def attend(first, query, key, value, start_column, count):
    length, cols = query.shape
    heads = cols // HEAD_DIM
    size = length // count
    whole = pl.BlockSpec((length, cols), lambda i, first: (0, 0))
    return pl.pallas_call(
        attend_kernel,
        grid_spec=pltpu.PrefetchScalarGridSpec(
            num_scalar_prefetch=1,
            grid=(size,),
            in_specs=[
                pl.BlockSpec((count, cols), lambda i, first: (i, 0)),
                whole,
                whole,
                pl.BlockSpec((count, 1), lambda i, first: (i, 0)),
            ],
            out_specs=[
                pl.BlockSpec((count, cols), lambda i, first: (i, 0)),
                pl.BlockSpec((count, cols), lambda i, first: (i, 0)),
                pl.BlockSpec((count, heads), lambda i, first: (i, 0)),
            ],
            scratch_shapes=[
                pltpu.VMEM((size, heads, count, count), F32),
                pltpu.VMEM((size, heads * count, cols), BF),
            ],
        ),
        out_shape=[
            jax.ShapeDtypeStruct((length, cols), F32),
            jax.ShapeDtypeStruct((length, cols), BF),
            jax.ShapeDtypeStruct((length, heads), F32),
        ],
        compiler_params=params(),
        cost_estimate=cost(18 * length * length * cols, 10 * length * cols),
        name="attend",
    )(first, query, key, value, start_column)


def attend_back_kernel(
    first, spot, q_ref, k_ref, v_ref, do_ref, lse_ref, delta_ref, start_ref,
    cq_ref, sq_ref, ck_ref, sk_ref, out_ref, kcat, dk_ref, dv_ref,
):
    i = pl.program_id(0)
    rows, cols = q_ref.shape
    half = cols // 2
    heads = cols // HEAD_DIM
    blocks = k_ref.shape[0] // rows

    @pl.when(i == 0)
    def _():
        dk_ref[...] = jnp.zeros_like(dk_ref)
        dv_ref[...] = jnp.zeros_like(dv_ref)
        for b in range(blocks):
            key = k_ref[b * rows : (b + 1) * rows, :]
            for h in range(heads):
                kcat[b, h * rows : (h + 1) * rows, :] = jnp.where(
                    head_mask((rows, cols), h, heads, True), key, jnp.zeros_like(key)
                )

    query, grad = q_ref[...], do_ref[...]
    parts = [
        jnp.where(head_mask((rows, cols), h, heads, True), query, jnp.zeros_like(query))
        for h in range(heads)
    ]
    grads = [
        jnp.where(head_mask((rows, cols), h, heads, False), grad, jnp.zeros_like(grad))
        for h in range(heads)
    ]
    query_stack = jnp.concatenate(parts, axis=0)
    grad_stack = jnp.concatenate(grads, axis=0)
    start = start_ref[...]
    place = i * rows + lax.broadcasted_iota(jnp.int32, (rows, rows), 1)
    line = lax.broadcasted_iota(jnp.int32, (rows, rows), 0)

    def block(j, total):
        where = pl.ds(pl.multiple_of(j * rows, rows), rows)
        column = j * rows + line
        keep = (column <= place) & (column >= start)
        key, value = k_ref[where, :], v_ref[where, :]
        chances, slopes = [], []
        for h in range(heads):
            score = jnp.where(keep, dot(key, parts[h], NT), MASKED_SCORE)
            chance = jnp.exp(score - lse_ref[h : h + 1, :])
            product = dot(value, grads[h], NT)
            slopes.append((chance * (product - delta_ref[h : h + 1, :])).astype(BF))
            chances.append(chance.astype(BF))
        slope = jnp.concatenate(slopes, axis=1)
        dk_ref[where, :] += dot(slope, query_stack, NN)
        dv_ref[where, :] += dot(jnp.concatenate(chances, axis=1), grad_stack, NN)
        return total + dot(jnp.concatenate(slopes, axis=0), kcat[j], TN)

    total = lax.fori_loop(first[i], i + 1, block, jnp.zeros((rows, cols), F32))
    here = pl.ds(pl.multiple_of(i * rows, rows), rows)
    target = pl.ds(pl.multiple_of(spot[i] * rows, rows), rows)
    cq, sq = cq_ref[here, :], sq_ref[here, :]
    d1, d2 = total[:, :half], total[:, half:]
    out_ref[target, :half] = (d1 * cq + d2 * sq).astype(BF)
    out_ref[target, half:cols] = (d2 * cq - d1 * sq).astype(BF)

    @pl.when(i == pl.num_programs(0) - 1)
    def _():
        def finish(j, carry):
            where = pl.ds(pl.multiple_of(j * rows, rows), rows)
            goal = pl.ds(pl.multiple_of(spot[j] * rows, rows), rows)
            ck, sk = ck_ref[where, :], sk_ref[where, :]
            k1, k2 = dk_ref[where, :half], dk_ref[where, half:]
            out_ref[goal, cols : cols + half] = (k1 * ck + k2 * sk).astype(BF)
            out_ref[goal, cols + half : 2 * cols] = (k2 * ck - k1 * sk).astype(BF)
            out_ref[goal, 2 * cols :] = dv_ref[where, :].astype(BF)
            return carry

        lax.fori_loop(0, blocks, finish, 0)


def attend_back(first, spot, query, key, value, grad, lse, delta, start_row, tables, count):
    length, cols = query.shape
    heads = cols // HEAD_DIM
    size = length // count
    whole = pl.BlockSpec((length, cols), lambda i, *_: (0, 0))
    table = pl.BlockSpec((length, cols // 2), lambda i, *_: (0, 0))
    rows = pl.BlockSpec((count, cols), lambda i, *_: (i, 0))
    line = pl.BlockSpec((pl.squeezed, heads, count), lambda i, *_: (i, 0, 0))
    return pl.pallas_call(
        attend_back_kernel,
        grid_spec=pltpu.PrefetchScalarGridSpec(
            num_scalar_prefetch=2,
            grid=(size,),
            in_specs=[
                rows,
                whole,
                whole,
                rows,
                line,
                line,
                pl.BlockSpec((pl.squeezed, 1, count), lambda i, *_: (i, 0, 0)),
                table,
                table,
                table,
                table,
            ],
            out_specs=pl.BlockSpec((length, 3 * cols), lambda i, *_: (0, 0)),
            scratch_shapes=[
                pltpu.VMEM((size, heads * count, cols), BF),
                pltpu.VMEM((length, cols), F32),
                pltpu.VMEM((length, cols), F32),
            ],
        ),
        out_shape=jax.ShapeDtypeStruct((length, 3 * cols), BF),
        compiler_params=params(),
        cost_estimate=cost(24 * length * length * cols, 20 * length * cols),
        name="attend_back",
    )(first, spot, query, key, value, grad, lse, delta, start_row, *tables)


def xpos_tables(heads, scale, positions):
    pair_index = (jnp.arange(HALF * heads) % HALF).astype(F32)
    frequency = 10000.0 ** (-pair_index / HALF)
    angles = positions[:, None] * frequency[None, :]
    zeta_base = (pair_index / HALF + 0.4) / 1.4
    growth = zeta_base[None, :] ** ((positions[:, None] - SEQ_LEN // 2) / SCALE_BASE)
    cosine, sine = jnp.cos(angles), jnp.sin(angles)
    return cosine * growth * scale, sine * growth * scale, cosine / growth, sine / growth


def on_device(
    layer_input,
    segment_ids,
    cotangent,
    projections,
    output_weight,
    up_weight,
    down_weight,
    norm_gains,
    hidden_gain,
    decays,
    average_projections,
    average_output,
    average_up,
    average_down,
    average_gains,
    average_hidden,
):
    size = lax.axis_size("seq")
    groups = lax.axis_size("tensor")
    me = lax.axis_index("seq")
    group = lax.axis_index("tensor")
    chunks, count, width = layer_input.shape
    length = segment_ids.shape[1]
    block_cols = projections.shape[2]
    heads = width // HEAD_DIM
    per_block = block_cols // HEAD_DIM
    mine = heads // size
    cols = mine * HEAD_DIM
    even_split = per_block % size == 0
    units = up_weight.shape[1] // size
    hidden_cols = units * groups
    hidden_total = hidden_cols * size

    each = per_block // size if even_split else 0
    split = each * HEAD_DIM

    def to_order(rows):
        if not even_split:
            return rows
        shaped = rows.reshape((groups, size, split) + rows.shape[1:])
        return jnp.swapaxes(shaped, 0, 1).reshape(rows.shape)

    def from_order(rows):
        if not even_split:
            return rows
        shaped = rows.reshape((size, groups, split) + rows.shape[1:])
        return jnp.swapaxes(shaped, 0, 1).reshape(rows.shape)

    line = Line()
    masks = np.concatenate([np.arange(0, size, 2), np.arange(1, size, 2)]).astype(np.int32)
    place = (jnp.asarray(masks) ^ me).astype(jnp.int32)
    middle = length // 2
    halves = (0, 1)

    gains_all = lax.all_gather(norm_gains, "seq", axis=1, tiled=True).astype(F32)
    gain_attn, gain_ffn = gains_all[0], gains_all[2][None]
    gain_inner = to_order(gains_all[1]).reshape(size, 1, cols)
    inputs = [layer_input[c].astype(F32) for c in range(chunks)]
    normed = [row_norm(rows) for rows in inputs]
    sent_in = [(normed[c][0] * gain_attn).astype(BF) for c in range(chunks)]

    turned = projections.transpose(1, 2, 0)
    if even_split:
        sent = turned.reshape(3, size, split, count).transpose(1, 0, 2, 3)
        came = lax.all_to_all(sent, "seq", 0, 0, tiled=True)
        raw = lax.all_gather(came, "tensor", axis=0, tiled=False)
    else:
        wide = lax.all_gather(turned, "tensor", axis=1, tiled=True)
        sent = wide.reshape(3, size, cols, count).transpose(1, 0, 2, 3)
        came = lax.all_to_all(sent, "seq", 0, 0, tiled=True)
        raw = came[None]
    proj, proj_plain = arrange(raw)
    tall = lax.all_gather(after(output_weight, came), "tensor", axis=0, tiled=True)

    def swapped(kind):
        if kind == "up":
            sent = line.put(up_weight).reshape(count, size, units).transpose(1, 0, 2)
            return lax.all_to_all(sent, "seq", 0, 0, tiled=True).reshape(width, units)
        sent = line.put(down_weight).reshape(size, units, count)
        came = lax.all_to_all(sent, "seq", 0, 0, tiled=True)
        return came.transpose(1, 0, 2).reshape(units, width)

    gain_hidden = jnp.zeros((groups, units), BF)
    for k in range(groups):
        part = hidden_gain
        if k:
            part = lax.ppermute(part, "tensor", [(i, (i - k) % groups) for i in range(groups)])
        gain_hidden = lax.dynamic_update_slice(
            gain_hidden, part.reshape(1, units), ((group + k) % groups, 0)
        )
    gain_hidden = gain_hidden.astype(F32).reshape(1, hidden_cols)

    blocks = jnp.arange(size, dtype=jnp.int32) ^ me
    spot = (blocks & 1) * (size // 2) + (blocks >> 1)
    segments = lax.dynamic_slice_in_dim(segment_ids, group * chunks, chunks, 0)
    starts = jnp.sum((segments[:, None, :] < segments[:, :, None]).astype(jnp.int32), axis=2)
    firsts = starts.reshape(chunks, size, count)[:, :, 0] // count

    rows_of = {}

    def projected(c, h):
        before = rows_of.get(c) or [jnp.zeros((length, cols), BF) for _ in range(3)]
        rows_of[c] = project(
            line.enter(place[h * (size // 2) : (h + 1) * (size // 2)]),
            ins[c].halves[h],
            proj_plain,
            tables_turn,
            count,
            before,
        )
        line.mark(rows_of[c][0])

    def attention(c):
        attended, low, lse = attend(
            line.enter(firsts[c]), *rows_of[c], starts[c][:, None], count
        )
        line.mark(lse)
        came = lax.all_to_all(low.reshape(size, count, cols), "seq", 0, 0, tiled=True)
        return rows_of[c], attended, lse, came

    def mixed(c):
        result = out_project(
            line.enter(place),
            kept[c][3],
            pieces.halves,
            layer_input[c],
            gain_inner,
            gain_ffn,
            split,
        )
        line.mark(result[1])
        return result

    ins = [Gather(line, sent_in[0])]
    line.mark(ins[0].pieces[-1])
    ins[0].corner()
    ins.append(Gather(line, sent_in[1]))
    came_up = swapped("up")
    line.note(gain_hidden)
    turn = line.enter(jnp.arange(SEQ_LEN, dtype=F32))
    tables_turn = xpos_tables(mine, FACTOR, turn)
    line.mark(tables_turn[0])
    ins[0].core()
    line.note(came_up)
    came_down = swapped("down")
    up_parts = lax.all_gather(after(came_up, tall), "tensor", axis=0, tiled=False)
    proj, proj_plain = arrange(line.enter(raw))
    line.mark(proj)
    ins[1].corner()
    line.note(came_down)
    projected(0, 0)
    pieces = Gather(line, tall)
    projected(0, 1)
    ins[1].core()
    down = lax.all_gather(line.put(came_down), "tensor", axis=0, tiled=True)
    kept = [attention(0)]
    pieces.corner()
    cots = [Gather(line, cotangent[0])]
    projected(1, 0)
    projected(1, 1)
    pieces.core()
    kept.append(attention(1))
    cots[0].corner()
    line.note(kept[0][3])
    outs = [mixed(0)]
    cots[0].core()
    mids = [Gather(line, outs[0][2])]
    line.note(kept[1][3])
    outs.append(mixed(1))
    cots.append(Gather(line, cotangent[1]))

    def graded(c, h):
        scaled = ffn_grad(cots[c].halves[h], down, line.enter(gain_hidden))
        line.mark(scaled)
        return scaled

    def entered(c, h, scaled=None):
        if scaled is None:
            result = ffn_in(
                mids[c].halves[h], up_parts, None, cots[c].halves[h], down, line.enter(gain_hidden)
            )
        else:
            result = ffn_in(mids[c].halves[h], up_parts, line.enter(scaled))
        line.mark(result[3])
        return result

    def summed(held):
        stats = jnp.concatenate([held[h][3] for h in halves]).reshape(size, count, 4)
        return BlockSum(line, stats.transpose(0, 2, 1))

    def row_stats(sums):
        stats = sums.total() / hidden_total
        mean, second, plain, cross = (stats[:, k] for k in range(4))
        inverse = lax.rsqrt(second - mean * mean + EPSILON)
        cross = inverse * (cross - mean * plain)
        return jnp.stack([mean, inverse, plain, cross], axis=-1).reshape(length, 4)

    def left(c, h):
        result = ffn_out(
            held[c][h][:3], stats[c], line.enter(gain_hidden), up_parts, down, h * middle
        )
        line.mark(result[4])
        return result

    scaled0 = [graded(0, 0)]
    mids[0].corner()
    mids.append(Gather(line, outs[1][2]))
    scaled0.append(graded(0, 1))
    mids[0].core()
    cots[1].corner()
    held = [[entered(0, 0, scaled0[0])]]
    cots[1].core()
    mids[1].corner()
    held[0].append(entered(0, 1, scaled0[1]))
    mids[1].core()
    sums = [summed(held[0])]
    held.append([entered(1, 0)])
    sums[0].more()
    held[1].append(entered(1, 1))
    sums[0].more()
    sums.append(summed(held[1]))
    stats = [row_stats(sums[0])]
    done = [[None, None] for _ in range(chunks)]
    done[0][1] = left(0, 1)
    sums[1].more()
    mid_sums = [Scatter(line, done[0][1][2], count)]
    done[0][0] = left(0, 0)
    mid_sums[0].corner(done[0][0][2])
    sums[1].more()
    stats.append(row_stats(sums[1]))
    done[1][1] = left(1, 1)
    mid_sums[0].near()
    mid_sums.append(Scatter(line, done[1][1][2], count))
    done[1][0] = left(1, 0)
    mid_sums[1].corner(done[1][0][2])
    out_sums = [Scatter(line, done[0][1][3], count)]
    hidden_gain_grad = sum(done[c][h][4] for c in range(chunks) for h in halves)
    hidden_gain_grad = (hidden_gain_grad / gain_hidden).reshape(groups, units)
    down_grad = weight_grad(
        [line.enter(done[c][h][0]) for c in range(chunks) for h in halves],
        [cots[c].halves[h] for c in range(chunks) for h in halves],
        [0] * 4,
    )[0]
    line.mark(down_grad)
    scatter = partial(lax.psum_scatter, axis_name="tensor", scatter_dimension=0, tiled=True)
    down_own = scatter(down_grad)

    def back_out(c):
        residual_grad, attn_grad, sent, ffn_gain, inner_gain = out_back(
            line.enter(place),
            mid_sums[c].total(),
            outs[c][1],
            cotangent[c],
            kept[c][3],
            pieces.halves,
            gain_inner,
            gain_ffn,
            split,
        )
        line.mark(sent)
        grad = lax.all_to_all(sent, "seq", 0, 0, tiled=True).reshape(length, cols)
        return residual_grad, attn_grad, grad, ffn_gain[0], inner_gain.reshape(width)

    def back_attention(c):
        turned_rows, attended, lse, came = kept[c]
        grad = backs[c][2]
        delta = jnp.sum((grad.astype(F32) * attended).reshape(length, mine, HEAD_DIM), axis=2)
        slope = attend_back(
            line.enter(firsts[c]),
            spot,
            *turned_rows,
            grad,
            lse.reshape(size, count, mine).transpose(0, 2, 1),
            delta.reshape(size, count, mine).transpose(0, 2, 1),
            starts[c].reshape(size, 1, count),
            tables_turn,
            count,
        )
        line.mark(slope)
        return slope

    def times(rows, weights, offset):
        result = multiply(line.enter(rows), weights, offset, middle)
        line.mark(result)
        return result

    mid_sums[1].near()
    backs = [back_out(0)]
    out_sums[0].corner(done[0][0][3])
    out_sums.append(Scatter(line, done[1][1][3], count))
    up_grad = weight_grad(
        [line.enter(done[c][h][1]) for c in range(chunks) for h in halves],
        [mids[c].halves[h] for c in range(chunks) for h in halves],
        [0] * 4,
    )[0]
    line.mark(up_grad)
    up_own = scatter(up_grad)
    out_sums[0].near()
    backs.append(back_out(1))
    line.note(backs[0][2])
    output_grad = out_grad(
        [line.enter(outs[c][0]) for c in range(chunks)], [back[1] for back in backs], split
    )
    line.mark(output_grad)
    output_own = scatter(
        lax.psum_scatter(output_grad, "seq", scatter_dimension=0, tiled=True).reshape(width, count)
    )
    out_sums[1].corner(done[1][0][3])
    slopes = [back_attention(0)]
    out_sums[1].near()
    line.note(down_own, backs[1][2])
    odd = times(slopes[0], proj, middle)
    in_sums = [Scatter(line, odd, count)]
    even = times(slopes[0], proj, 0)
    in_sums[0].corner(even)
    slopes.append(back_attention(1))
    in_sums[0].near()
    line.note(up_own)
    odd = times(slopes[1], proj, middle)
    in_sums.append(Scatter(line, odd, count))
    even = times(slopes[1], proj, 0)
    in_sums[1].corner(even)
    proj_grad, attn_gain = weight_grad(
        [line.enter(slopes[c]) for c in range(chunks) for h in halves],
        [ins[c].halves[h] for c in range(chunks) for h in halves],
        [h * middle for c in range(chunks) for h in halves],
        proj,
    )
    line.mark(proj_grad)
    in_sums[1].near()

    outputs = [outs[c][1] + out_sums[c].total() for c in range(chunks)]
    input_grads = [
        backs[c][0] + row_norm_back(in_sums[c].total() * gain_attn, *normed[c])
        for c in range(chunks)
    ]
    gain_terms = jnp.stack(
        [
            attn_gain[0] / gain_attn,
            from_order(sum(back[4] for back in backs)),
            sum(back[3] for back in backs),
        ]
    )
    gains_grad = lax.psum(
        lax.psum_scatter(gain_terms, "seq", scatter_dimension=1, tiled=True), "tensor"
    )

    part = down_own.reshape(units, size, count).transpose(1, 0, 2)
    down_final = lax.all_to_all(part, "seq", 0, 0, tiled=True).reshape(size * units, count)
    part = up_own.reshape(units, size, count).transpose(1, 0, 2)
    part = lax.all_to_all(part, "seq", 0, 0, tiled=True)
    up_final = part.transpose(2, 0, 1).reshape(count, size * units)
    output_final = output_own
    part = proj_grad
    turned_heads = part[: 2 * cols].reshape(2, 2, mine, HALF, width).transpose(0, 2, 1, 3, 4)
    part = jnp.concatenate([turned_heads.reshape(2, cols, width), part[None, 2 * cols :]])
    if even_split:
        part = part.reshape(3, groups, split, width).transpose(1, 0, 2, 3)
        part = scatter(part.reshape(3 * cols, width))
        part = part.reshape(3, split, size, count).transpose(2, 0, 1, 3)
        part = lax.all_to_all(part, "seq", 0, 0, tiled=True)
        proj_final = part.transpose(3, 1, 0, 2).reshape(count, 3, block_cols)
    else:
        part = lax.psum(part, "tensor").reshape(3, cols, size, count).transpose(2, 0, 1, 3)
        part = lax.all_to_all(part, "seq", 0, 0, tiled=True)
        part = part.transpose(3, 1, 0, 2).reshape(count, 3, width)
        proj_final = lax.dynamic_slice_in_dim(part, group * block_cols, block_cols, 2)
    hidden_final = lax.psum_scatter(
        hidden_gain_grad, "tensor", scatter_dimension=0, tiled=True
    )

    grads = (
        proj_final.astype(F32),
        output_final.astype(F32),
        up_final.astype(F32),
        down_final.astype(F32),
        gains_grad.astype(F32),
        hidden_final.astype(F32),
    )
    averages = (
        average_projections,
        average_output,
        average_up,
        average_down,
        average_gains,
        average_hidden,
    )
    updated = tuple(
        decays[i] * averages[i] + (1.0 - decays[i]) * grads[i] for i in range(6)
    )
    return (jnp.stack(outputs).astype(BF), jnp.stack(input_grads)) + grads + updated


def solution(mesh):
    weights = (P("seq", None, "tensor"), P("tensor", "seq"), P("seq", "tensor"), P("tensor", "seq"))
    gains = (P(None, "seq"), P("tensor", "seq"))
    rows = P("tensor", "seq", None)
    return jax.shard_map(
        on_device,
        mesh=mesh,
        in_specs=(rows, P(), rows) + weights + gains + (P(),) + weights + gains,
        out_specs=(rows, rows) + weights + gains + weights + gains,
        check_vma=False,
    )
```

```python
from functools import partial

import jax
import jax.numpy as jnp
import numpy as np
from jax import lax
from jax.experimental import pallas as pl
from jax.experimental.pallas import tpu as pltpu
from jax.sharding import PartitionSpec as P

HEAD_DIM = 64
HALF = HEAD_DIM // 2
SEQ_LEN = 2048
SCALE_BASE = 512
EPSILON = 1e-05
MASKED_SCORE = -1e30
FACTOR = HEAD_DIM ** (-0.5)
BF = jnp.bfloat16
F32 = jnp.float32
SCALE = 4
VMEM_LIMIT = 56 * 1024 * 1024


def swap(block, bit):
    size = lax.axis_size("seq")
    return lax.ppermute(block, "seq", [(i, i ^ bit) for i in range(size)])


def after(array, *others):
    return lax.optimization_barrier((array,) + others)[0]


class Line:
    def __init__(self):
        self.last, self.noted = (), ()

    def put(self, array):
        return after(array, *self.last) if self.last else array

    def note(self, *arrays):
        self.noted += arrays

    def enter(self, array):
        return after(array, *self.last, *self.noted) if self.last + self.noted else array

    def mark(self, *arrays):
        self.last, self.noted = arrays, ()


def join_kernel(*refs):
    parts, out_ref, held, came, left = refs[:-4], refs[-4], refs[-3], refs[-2], refs[-1]
    spots, at = [], 0
    for part in parts:
        spots.append(pl.ds(at, part.shape[0]))
        at += part.shape[0]
    ins = [
        pltpu.make_async_copy(part, held.at[spot], came.at[k])
        for k, (part, spot) in enumerate(zip(parts, spots))
    ]
    outs = [
        pltpu.make_async_copy(held.at[spot], out_ref.at[spot], left.at[k])
        for k, spot in enumerate(spots)
    ]
    for copy in ins:
        copy.start()
    for k, copy in enumerate(ins):
        copy.wait()
        outs[k].start()
    for copy in outs:
        copy.wait()


def join(parts):
    rows, width = sum(part.shape[0] for part in parts), parts[0].shape[1]
    if any(part.shape[0] % 16 for part in parts) or width % 128:
        return jnp.concatenate(parts)
    return pl.pallas_call(
        join_kernel,
        in_specs=[pl.BlockSpec(memory_space=pl.ANY)] * len(parts),
        out_specs=pl.BlockSpec(memory_space=pl.ANY),
        out_shape=jax.ShapeDtypeStruct((rows, width), parts[0].dtype),
        scratch_shapes=[
            pltpu.VMEM((rows, width), parts[0].dtype),
            pltpu.SemaphoreType.DMA((len(parts),)),
            pltpu.SemaphoreType.DMA((len(parts),)),
        ],
        compiler_params=params(),
        cost_estimate=cost(0, 4 * rows * width),
        name="join",
    )(*parts)


class Gather:
    def __init__(self, line, rows):
        self.line = line
        self.size = lax.axis_size("seq")
        self.rows = line.put(rows)
        self.pieces = [self.rows]
        if self.size == 8:
            self.pieces += [swap(self.rows, 2), swap(self.rows, 4)]
        line.note(self.rows)

    def corner(self):
        if self.size == 8:
            half = self.rows.shape[0] // 2
            across = self.line.put(self.pieces[1])[:half]
            along = self.line.put(self.pieces[2])[half:]
            self.pieces += [swap(across, 4), swap(along, 2)]
            self.line.note(across, along)
        return self

    def core(self):
        even = self.line.put(self.pieces[0])
        if self.size == 8:
            even = join([even] + self.pieces[1:])
        else:
            bit = 2
            while bit < self.size:
                even = jnp.concatenate([even, swap(even, bit)])
                bit *= 2
        self.halves = (even, swap(even, 1))
        self.line.note(even)
        return self


class Scatter:
    def __init__(self, line, odd, count):
        self.line, self.count = line, count
        self.size = lax.axis_size("seq")
        self.other = swap(odd, 1)

    def block(self, k, start, stop):
        here = slice(k * self.count + start, k * self.count + stop)
        return self.even[here].astype(F32) + self.other[here].astype(F32)

    def corner(self, even):
        self.even = self.line.put(even)
        if self.size == 8:
            half = self.count // 2
            low = self.block(3, 0, half).astype(BF)
            high = self.block(3, half, self.count).astype(BF)
            self.low, self.high = swap(low, 4), swap(high, 2)
            self.line.note(low, high)
        return self

    def near(self):
        if self.size == 8:
            half = self.count // 2
            low, high = self.line.put(self.low), self.line.put(self.high)
            across = [self.block(1, 0, half) + low.astype(F32), self.block(1, half, self.count)]
            along = [self.block(2, 0, half), self.block(2, half, self.count) + high.astype(F32)]
            across = jnp.concatenate(across).astype(BF)
            along = jnp.concatenate(along).astype(BF)
            self.parts = [swap(across, 2), swap(along, 4)]
            self.line.note(across, along)
        return self

    def total(self):
        if self.size == 8:
            return self.block(0, 0, self.count) + sum(part.astype(F32) for part in self.parts)
        total, bit = self.even.astype(F32) + self.other.astype(F32), self.size // 2
        while bit > 1:
            middle = total.shape[0] // 2
            total = total[:middle] + swap(total[middle:].astype(BF), bit).astype(F32)
            bit //= 2
        return total


class BlockSum:
    def __init__(self, line, stats):
        self.line, self.stats, self.bit = line, line.put(stats), 1
        self.size = stats.shape[0]
        self.send()

    def send(self):
        self.other = swap(self.stats, self.bit)
        self.line.note(self.stats)

    def add(self):
        shift = (self.bit & 1) * (self.size // 2) + (self.bit >> 1)
        other = self.line.put(self.other)
        self.stats = self.stats + jnp.stack([other[i ^ shift] for i in range(self.size)])
        self.bit *= 2

    def more(self):
        self.add()
        if self.bit < self.size:
            self.send()

    def total(self):
        while self.bit < self.size:
            self.add()
            if self.bit < self.size:
                self.send()
        return self.stats


def row_norm(features):
    mean = jnp.mean(features, axis=-1, keepdims=True)
    second = jnp.mean(features * features, axis=-1, keepdims=True)
    inverse = lax.rsqrt(second - mean * mean + EPSILON)
    return (features - mean) * inverse, inverse


def row_norm_back(scaled, normed, inverse):
    return inverse * (
        scaled
        - jnp.mean(scaled, axis=-1, keepdims=True)
        - normed * jnp.mean(scaled * normed, axis=-1, keepdims=True)
    )


def dot(a, b, dims):
    return lax.dot_general(a, b, (dims, ((), ())), preferred_element_type=F32)


NN = ((1,), (0,))
NT = ((1,), (1,))
TN = ((0,), (0,))


def params():
    return pltpu.CompilerParams(vmem_limit_bytes=VMEM_LIMIT)


def cost(flops, moved, special=0):
    return pl.CostEstimate(
        flops=int(flops * SCALE), bytes_accessed=int(moved * SCALE), transcendentals=int(special * SCALE)
    )


def qkv_kernel(
    place, x_ref, w_ref, cq_ref, sq_ref, ck_ref, sk_ref, qa, ka, va, q_ref, k_ref, v_ref
):
    cols = q_ref.shape[1]
    half = cols // 2
    full = dot(x_ref[...], w_ref[...], NN)
    q1, q2 = full[:, :half], full[:, half:cols]
    k1, k2 = full[:, cols : cols + half], full[:, cols + half : 2 * cols]
    cq, sq, ck, sk = cq_ref[...], sq_ref[...], ck_ref[...], sk_ref[...]
    q_ref[:, :half] = (q1 * cq - q2 * sq).astype(BF)
    q_ref[:, half:] = (q2 * cq + q1 * sq).astype(BF)
    k_ref[:, :half] = (k1 * ck - k2 * sk).astype(BF)
    k_ref[:, half:] = (k2 * ck + k1 * sk).astype(BF)
    v_ref[...] = full[:, 2 * cols :].astype(BF)


def project(place, rows, weights, tables, count, before):
    here, width = rows.shape
    cols = weights.shape[1] // 3
    length = tables[0].shape[0]
    table = pl.BlockSpec((count, cols // 2), lambda i, place: (place[i], 0))
    out = pl.BlockSpec((count, cols), lambda i, place: (place[i], 0))
    held = pl.BlockSpec(memory_space=pl.ANY)
    return pl.pallas_call(
        qkv_kernel,
        grid_spec=pltpu.PrefetchScalarGridSpec(
            num_scalar_prefetch=1,
            grid=(here // count,),
            in_specs=[
                pl.BlockSpec((count, width), lambda i, place: (i, 0)),
                pl.BlockSpec((width, 3 * cols), lambda i, place: (0, 0)),
                table,
                table,
                table,
                table,
                held,
                held,
                held,
            ],
            out_specs=[out, out, out],
        ),
        out_shape=[jax.ShapeDtypeStruct((length, cols), BF)] * 3,
        input_output_aliases={7: 0, 8: 1, 9: 2},
        compiler_params=params(),
        cost_estimate=cost(
            2 * here * width * 3 * cols, 2 * (here * width + 3 * cols * width + 3 * here * cols)
        ),
        name="project",
    )(place, rows, weights, *tables, *before)


def turned_row(kind, head, heads):
    first = kind * heads * HEAD_DIM
    if kind == 2:
        return first + head * HEAD_DIM, first + head * HEAD_DIM + HALF
    return first + head * HALF, first + (heads + head) * HALF


def arrange_kernel(raw_ref, turned_ref, plain_ref):
    parts, size, _, split, count = raw_ref.shape
    each = split // HEAD_DIM
    for kind in range(3):
        for t in range(parts):
            for j in range(each):
                starts = turned_row(kind, t * each + j, parts * each)
                for b in range(size):
                    for h in range(2):
                        here = slice(j * HEAD_DIM + h * HALF, j * HEAD_DIM + (h + 1) * HALF)
                        turned_ref[starts[h] : starts[h] + HALF, b * count : (b + 1) * count] = (
                            raw_ref[t, b, kind, here, :]
                        )
    plain_ref[...] = turned_ref[...].T


def arrange(raw):
    parts, size, _, split, count = raw.shape
    cols, width = parts * split, size * count
    if count % 128:
        proj = raw.transpose(2, 0, 3, 1, 4).reshape(3, cols, width)
        heads = proj[:2].reshape(2, cols // HEAD_DIM, 2, HALF, width).transpose(0, 2, 1, 3, 4)
        turned = jnp.concatenate([heads.reshape(2 * cols, width), proj[2]])
        return turned, turned.T
    return pl.pallas_call(
        arrange_kernel,
        out_shape=[
            jax.ShapeDtypeStruct((3 * cols, width), BF),
            jax.ShapeDtypeStruct((width, 3 * cols), BF),
        ],
        compiler_params=params(),
        cost_estimate=cost(0, 18 * cols * width),
        name="arrange",
    )(raw)


def out_grad_kernel(*refs):
    out_ref = refs[-1]
    parts = (len(refs) - 1) // 2
    total = dot(refs[0][...], refs[parts][...], TN)
    for k in range(1, parts):
        total = total + dot(refs[k][...], refs[parts + k][...], TN)
    low = total.astype(BF)
    count = out_ref.shape[-1]
    for b in range(out_ref.shape[0]):
        out_ref[b] = low[:, b * count : (b + 1) * count].reshape(out_ref.shape[1:])


def out_grad(inners, grads, split):
    size, count, cols = inners[0].shape
    width = size * cols
    count_out = width // size
    if split:
        shape = (size, cols // split, size, split, count_out)
        spec = pl.BlockSpec(
            (size, cols // split, pl.squeezed, split, count_out), lambda i: (0, 0, i, 0, 0)
        )
    else:
        shape = (size, size, cols, count_out)
        spec = pl.BlockSpec((size, pl.squeezed, cols, count_out), lambda i: (0, i, 0, 0))
    parts = len(inners)
    return pl.pallas_call(
        out_grad_kernel,
        grid=(size,),
        in_specs=[pl.BlockSpec((pl.squeezed, count, cols), lambda i: (i, 0, 0))] * parts
        + [pl.BlockSpec((count, width), lambda i: (0, 0))] * parts,
        out_specs=spec,
        out_shape=jax.ShapeDtypeStruct(shape, BF),
        compiler_params=params(),
        cost_estimate=cost(
            2 * parts * count * width * width, 4 * parts * count * width + 2 * width * width
        ),
        name="out_grad",
    )(*inners, *grads).reshape(size, width, count_out)


def head_rows(weight, b, split):
    return weight[:, b].reshape(-1, weight.shape[-1]) if split else weight[b]


def out_kernel(
    split, place, came_ref, even_ref, odd_ref, x_ref, gi_ref, gf_ref, inner_ref, res_ref, mid_ref, acc
):
    i = pl.program_id(0)
    size, rows, cols = came_ref.shape
    width = size * cols
    count = width // size

    @pl.when(i == 0)
    def _():
        first = jnp.zeros((rows, 1), F32)
        second = jnp.zeros((rows, 1), F32)
        for b in range(size):
            part = came_ref[b].astype(F32)
            first += jnp.sum(part, axis=1, keepdims=True)
            second += jnp.sum(part * part, axis=1, keepdims=True)
        mean = first / width
        inverse = lax.rsqrt(second / width - mean * mean + EPSILON)
        for b in range(size):
            inner_ref[b] = ((came_ref[b].astype(F32) - mean) * inverse * gi_ref[b]).astype(BF)

    def piece(ref):
        total = jnp.zeros((rows, count), F32)
        for b in range(size):
            total += dot(inner_ref[b], head_rows(ref, b, split), NN)
        acc[place[i]] = total

    pl.when(i < size // 2)(lambda: piece(even_ref))
    pl.when(i >= size // 2)(lambda: piece(odd_ref))

    @pl.when(i == size - 1)
    def _():
        first = jnp.zeros((rows, 1), F32)
        second = jnp.zeros((rows, 1), F32)
        for b in range(size):
            here = slice(b * count, (b + 1) * count)
            part = acc[b] + x_ref[:, here].astype(F32)
            res_ref[:, here] = part
            first += jnp.sum(part, axis=1, keepdims=True)
            second += jnp.sum(part * part, axis=1, keepdims=True)
        mean = first / width
        inverse = lax.rsqrt(second / width - mean * mean + EPSILON)
        mid_ref[...] = ((res_ref[...] - mean) * inverse * gf_ref[...]).astype(BF)


def weight_views(pieces, size, cols, split):
    half, count = size // 2, pieces[0].shape[1]
    if split:
        shape = (cols // split, size, split, count)
    else:
        shape = (size, cols, count)
    zeros = (0,) * len(shape)
    views = [piece.reshape((half,) + shape) for piece in pieces]
    specs = [
        pl.BlockSpec((pl.squeezed,) + shape, lambda i, *_: (jnp.minimum(i, half - 1),) + zeros),
        pl.BlockSpec((pl.squeezed,) + shape, lambda i, *_: (jnp.maximum(i - half, 0),) + zeros),
    ]
    return views, specs


def out_project(place, came, pieces, rows, gain_inner, gain_ffn, split):
    size, count, cols = came.shape
    width = size * cols
    views, specs = weight_views(pieces, size, cols, split)
    blocks = pl.BlockSpec((size, count, cols), lambda i, *_: (0, 0, 0))
    flat = pl.BlockSpec((count, width), lambda i, *_: (0, 0))
    return pl.pallas_call(
        partial(out_kernel, split),
        grid_spec=pltpu.PrefetchScalarGridSpec(
            num_scalar_prefetch=1,
            grid=(size,),
            in_specs=[blocks]
            + specs
            + [
                flat,
                pl.BlockSpec((size, 1, cols), lambda i, *_: (0, 0, 0)),
                pl.BlockSpec((1, width), lambda i, *_: (0, 0)),
            ],
            out_specs=[blocks, flat, flat],
            scratch_shapes=[pltpu.VMEM((size, count, width // size), F32)],
        ),
        out_shape=[
            jax.ShapeDtypeStruct((size, count, cols), BF),
            jax.ShapeDtypeStruct((count, width), F32),
            jax.ShapeDtypeStruct((count, width), BF),
        ],
        compiler_params=params(),
        cost_estimate=cost(2 * count * width * width, 2 * width * width + 12 * count * width),
        name="out_project",
    )(place, came, *views, rows, gain_inner, gain_ffn)


def out_back_kernel(
    split, place, grad_ref, res_ref, cot_ref, came_ref, even_ref, odd_ref, gi_ref, gf_ref,
    rg_ref, ag_ref, back_ref, fg_ref, ig_ref, held, sent,
):
    i = pl.program_id(0)
    size, rows, cols = came_ref.shape
    width = size * cols
    count = width // size

    @pl.when(i == 0)
    def _():
        residual, grad = res_ref[...], grad_ref[...]
        mean = jnp.mean(residual, axis=1, keepdims=True)
        second = jnp.mean(residual * residual, axis=1, keepdims=True)
        inverse = lax.rsqrt(second - mean * mean + EPSILON)
        normal = (residual - mean) * inverse
        fg_ref[...] = jnp.sum(grad * normal, axis=0, keepdims=True)
        scaled = grad * gf_ref[...]
        back = inverse * (
            scaled
            - jnp.mean(scaled, axis=1, keepdims=True)
            - normal * jnp.mean(scaled * normal, axis=1, keepdims=True)
        )
        total = cot_ref[...].astype(F32) + back
        rg_ref[...] = total
        low = total.astype(BF)
        ag_ref[...] = low
        for b in range(size):
            sent[b] = low[:, b * count : (b + 1) * count]
        held[...] = jnp.zeros_like(held)

    def piece(ref):
        grad = sent[place[i]]
        for b in range(size):
            held[b] += dot(grad, head_rows(ref, b, split), NT)

    pl.when(i < size // 2)(lambda: piece(even_ref))
    pl.when(i >= size // 2)(lambda: piece(odd_ref))

    @pl.when(i == size - 1)
    def _():
        zero = jnp.zeros((rows, 1), F32)
        first, second = zero, zero
        for b in range(size):
            part = came_ref[b].astype(F32)
            first += jnp.sum(part, axis=1, keepdims=True)
            second += jnp.sum(part * part, axis=1, keepdims=True)
        mean = first / width
        inverse = lax.rsqrt(second / width - mean * mean + EPSILON)
        plain, cross = zero, zero
        for b in range(size):
            normal = (came_ref[b].astype(F32) - mean) * inverse
            grad = held[b]
            ig_ref[b] = jnp.sum(grad * normal, axis=0, keepdims=True)
            scaled = grad * gi_ref[b]
            plain += jnp.sum(scaled, axis=1, keepdims=True)
            cross += jnp.sum(scaled * normal, axis=1, keepdims=True)
        plain, cross = plain / width, cross / width
        for b in range(size):
            normal = (came_ref[b].astype(F32) - mean) * inverse
            back_ref[b] = (inverse * (held[b] * gi_ref[b] - plain - normal * cross)).astype(BF)


def out_back(place, grad, residual, cotangent, came, pieces, gain_inner, gain_ffn, split):
    size, count, cols = came.shape
    width = size * cols
    views, specs = weight_views(pieces, size, cols, split)
    blocks = pl.BlockSpec((size, count, cols), lambda i, *_: (0, 0, 0))
    flat = pl.BlockSpec((count, width), lambda i, *_: (0, 0))
    line = pl.BlockSpec((1, width), lambda i, *_: (0, 0))
    lines = pl.BlockSpec((size, 1, cols), lambda i, *_: (0, 0, 0))
    return pl.pallas_call(
        partial(out_back_kernel, split),
        grid_spec=pltpu.PrefetchScalarGridSpec(
            num_scalar_prefetch=1,
            grid=(size,),
            in_specs=[flat, flat, flat, blocks] + specs + [lines, line],
            out_specs=[flat, flat, blocks, line, lines],
            scratch_shapes=[
                pltpu.VMEM((size, count, cols), F32),
                pltpu.VMEM((size, count, width // size), BF),
            ],
        ),
        out_shape=[
            jax.ShapeDtypeStruct((count, width), F32),
            jax.ShapeDtypeStruct((count, width), BF),
            jax.ShapeDtypeStruct((size, count, cols), BF),
            jax.ShapeDtypeStruct((1, width), F32),
            jax.ShapeDtypeStruct((size, 1, cols), F32),
        ],
        compiler_params=params(),
        cost_estimate=cost(2 * count * width * width, 2 * width * width + 20 * count * width),
        name="out_back",
    )(place, grad, residual, cotangent, came, *views, gain_inner, gain_ffn)


def ffn_grad_kernel(c_ref, down_ref, g_ref, t_ref):
    t_ref[...] = (dot(c_ref[...], down_ref[...], NT) * g_ref[...]).astype(BF)


def ffn_grad(grads, down, gain):
    here, width = grads.shape
    cols = down.shape[0]
    tile = 256
    return pl.pallas_call(
        ffn_grad_kernel,
        grid=(here // tile,),
        in_specs=[
            pl.BlockSpec((tile, width), lambda i: (i, 0)),
            pl.BlockSpec((cols, width), lambda i: (0, 0)),
            pl.BlockSpec((1, cols), lambda i: (0, 0)),
        ],
        out_specs=pl.BlockSpec((tile, cols), lambda i: (i, 0)),
        out_shape=jax.ShapeDtypeStruct((here, cols), BF),
        compiler_params=params(),
        cost_estimate=cost(2 * here * width * cols, 2 * here * (width + cols) + 2 * width * cols),
        name="ffn_grad",
    )(grads, down, gain)


def ffn_in_kernel(given, *refs):
    if given:
        x_ref, t_in_ref, up_ref, a_ref, p_ref, s_ref = refs
    else:
        x_ref, c_ref, up_ref, down_ref, g_ref, a_ref, p_ref, s_ref, t_ref = refs
    parts, _, units = up_ref.shape
    sums = [0.0] * 4
    for k in range(parts):
        here = slice(k * units, (k + 1) * units)
        hidden = dot(x_ref[...], up_ref[k], NN)
        if given:
            scaled = t_in_ref[:, here].astype(F32)
        else:
            low = (dot(c_ref[...], down_ref[here, :], NT) * g_ref[:, here]).astype(BF)
            t_ref[:, here] = low
            scaled = low.astype(F32)
        share = 0.5 * (1.0 + lax.erf(hidden * (2.0**-0.5)))
        activated = hidden * share
        slope = share + hidden * jnp.exp(-0.5 * hidden * hidden) * ((2.0 * np.pi) ** -0.5)
        a_ref[:, here] = activated
        p_ref[:, here] = slope.astype(BF)
        for j, terms in enumerate((activated, activated * activated, scaled, scaled * activated)):
            sums[j] = sums[j] + jnp.sum(terms, axis=1, keepdims=True)
    for j in range(4):
        s_ref[:, j : j + 1] = sums[j]


def ffn_in(rows, up_parts, scaled=None, grads=None, down=None, gain=None):
    given = scaled is not None
    here, width = rows.shape
    parts, _, units = up_parts.shape
    cols = parts * units
    tile = 256
    wide = pl.BlockSpec((tile, width), lambda i: (i, 0))
    out = pl.BlockSpec((tile, cols), lambda i: (i, 0))
    up_spec = pl.BlockSpec(up_parts.shape, lambda i: (0, 0, 0))
    if given:
        arrays, specs = (rows, scaled, up_parts), [wide, out, up_spec]
    else:
        arrays = (rows, grads, up_parts, down, gain)
        specs = [
            wide,
            wide,
            up_spec,
            pl.BlockSpec((cols, width), lambda i: (0, 0)),
            pl.BlockSpec((1, cols), lambda i: (0, 0)),
        ]
    low = jax.ShapeDtypeStruct((here, cols), BF)
    outs = [jax.ShapeDtypeStruct((here, cols), F32), low, jax.ShapeDtypeStruct((here, 4), F32)]
    out_specs = [out, out, pl.BlockSpec((tile, 4), lambda i: (i, 0))]
    result = pl.pallas_call(
        partial(ffn_in_kernel, given),
        grid=(here // tile,),
        in_specs=specs,
        out_specs=out_specs if given else out_specs + [out],
        out_shape=outs if given else outs + [low],
        compiler_params=params(),
        cost_estimate=cost(
            (2 if given else 4) * here * width * cols,
            4 * here * width + 4 * width * cols + 8 * here * cols,
            2 * here * cols,
        ),
        name="ffn_in",
    )(*arrays)
    return result[0], result[1], scaled if given else result[3], result[2]


def ffn_out_kernel(
    a_ref, p_ref, t_ref, s_ref, g_ref, up_ref, down_ref, sq_ref, hg_ref, m_ref, o_ref, n_ref
):
    parts, _, units = up_ref.shape
    stats = s_ref[...]
    mean, inverse, plain, cross = (stats[:, k : k + 1] for k in range(4))
    normal = (a_ref[...] - mean) * inverse
    scaled = t_ref[...].astype(F32)
    squeezed = (normal * g_ref[...]).astype(BF)
    sq_ref[...] = squeezed
    grad = (p_ref[...].astype(F32) * (inverse * (scaled - plain - normal * cross))).astype(BF)
    hg_ref[...] = grad
    total = dot(grad[:, :units], up_ref[0], NT)
    for k in range(1, parts):
        total = total + dot(grad[:, k * units : (k + 1) * units], up_ref[k], NT)
    m_ref[...] = total.astype(BF)
    o_ref[...] = dot(squeezed, down_ref[...], NN).astype(BF)
    part = jnp.sum(scaled * normal, axis=0, keepdims=True)

    @pl.when(pl.program_id(0) == 0)
    def _():
        n_ref[...] = part

    @pl.when(pl.program_id(0) > 0)
    def _():
        n_ref[...] += part


def ffn_out(held, stats, gain, up_parts, down, offset):
    activated, slope, scaled = held
    here, cols = activated.shape
    width = down.shape[1]
    tile = 256
    shift = offset // tile
    out = pl.BlockSpec((tile, cols), lambda i: (i, 0))
    wide = pl.BlockSpec((tile, width), lambda i: (i, 0))
    return pl.pallas_call(
        ffn_out_kernel,
        grid=(here // tile,),
        in_specs=[
            out,
            out,
            out,
            pl.BlockSpec((tile, 4), lambda i: (i + shift, 0)),
            pl.BlockSpec((1, cols), lambda i: (0, 0)),
            pl.BlockSpec(up_parts.shape, lambda i: (0, 0, 0)),
            pl.BlockSpec((cols, width), lambda i: (0, 0)),
        ],
        out_specs=[out, out, wide, wide, pl.BlockSpec((1, cols), lambda i: (0, 0))],
        out_shape=[
            jax.ShapeDtypeStruct((here, cols), BF),
            jax.ShapeDtypeStruct((here, cols), BF),
            jax.ShapeDtypeStruct((here, width), BF),
            jax.ShapeDtypeStruct((here, width), BF),
            jax.ShapeDtypeStruct((1, cols), F32),
        ],
        compiler_params=params(),
        cost_estimate=cost(
            4 * here * width * cols, 12 * here * cols + 4 * width * cols + 4 * here * width
        ),
        name="ffn_out",
    )(activated, slope, scaled, stats, gain, up_parts, down)


def multiply_kernel(x_ref, w_ref, o_ref):
    o_ref[...] = dot(x_ref[...], w_ref[...], NN).astype(BF)


def multiply(rows, weights, offset, here):
    depth, width = weights.shape
    tile = 256
    shift = offset // tile
    return pl.pallas_call(
        multiply_kernel,
        grid=(here // tile,),
        in_specs=[
            pl.BlockSpec((tile, depth), lambda i: (i + shift, 0)),
            pl.BlockSpec((depth, width), lambda i: (0, 0)),
        ],
        out_specs=pl.BlockSpec((tile, width), lambda i: (i, 0)),
        out_shape=jax.ShapeDtypeStruct((here, width), BF),
        compiler_params=params(),
        cost_estimate=cost(2 * here * width * depth, 2 * (here * width + here * depth + depth * width)),
        name="multiply",
    )(rows, weights)


def grads_kernel(weighted, *refs):
    outs = 2 if weighted else 1
    ins = refs[:-outs]
    parts = len(ins) // 2
    total = dot(ins[0][...], ins[parts][...], TN)
    for k in range(1, parts):
        total = total + dot(ins[k][...], ins[parts + k][...], TN)
    refs[-outs][...] = total.astype(BF)
    if weighted:
        refs[-1][...] = jnp.sum(total * ins[-1][...].astype(F32), axis=0, keepdims=True)


def weight_grad(lefts, rights, offsets, weights=None):
    cols, width, here = lefts[0].shape[1], rights[0].shape[1], rights[0].shape[0]
    tile = 512
    count = len(lefts)

    def left_spec(offset):
        return pl.BlockSpec((here, cols), lambda i: (offset // here, 0))

    out_specs = [pl.BlockSpec((cols, tile), lambda i: (0, i))]
    out_shape = [jax.ShapeDtypeStruct((cols, width), BF)]
    extra, extra_specs = (), []
    if weights is not None:
        out_specs.append(pl.BlockSpec((1, tile), lambda i: (0, i)))
        out_shape.append(jax.ShapeDtypeStruct((1, width), F32))
        extra, extra_specs = (weights,), [pl.BlockSpec((cols, tile), lambda i: (0, i))]
    return pl.pallas_call(
        partial(grads_kernel, weights is not None),
        grid=(width // tile,),
        in_specs=[left_spec(offset) for offset in offsets]
        + [pl.BlockSpec((here, tile), lambda i: (0, i))] * count
        + extra_specs,
        out_specs=out_specs,
        out_shape=out_shape,
        compiler_params=params(),
        cost_estimate=cost(
            2 * count * here * width * cols, 2 * (count * here * (width + cols) + cols * width)
        ),
        name="weight_grad",
    )(*lefts, *rights, *extra)


def head_mask(shape, head, heads, turned):
    lane = lax.broadcasted_iota(jnp.int32, shape, 1)
    if turned:
        return (lane // HALF) % heads == head
    return lane // HEAD_DIM == head


def attend_kernel(first, q_ref, k_ref, v_ref, start_ref, o_ref, low_ref, lse_ref, scores, vcat):
    i = pl.program_id(0)
    rows, cols = q_ref.shape
    heads = cols // HEAD_DIM
    blocks = k_ref.shape[0] // rows

    @pl.when(i == 0)
    def _():
        for b in range(blocks):
            value = v_ref[b * rows : (b + 1) * rows, :]
            for h in range(heads):
                vcat[b, h * rows : (h + 1) * rows, :] = jnp.where(
                    head_mask((rows, cols), h, heads, False), value, jnp.zeros_like(value)
                )

    query = q_ref[...]
    parts = [
        jnp.where(head_mask((rows, cols), h, heads, True), query, jnp.zeros_like(query))
        for h in range(heads)
    ]
    start = start_ref[...]
    low = first[i]
    place = i * rows + lax.broadcasted_iota(jnp.int32, (rows, rows), 0)
    lane = lax.broadcasted_iota(jnp.int32, (rows, rows), 1)

    def score_block(j, tops):
        column = j * rows + lane
        keep = (column <= place) & (column >= start)
        key = k_ref[pl.ds(pl.multiple_of(j * rows, rows), rows), :]
        new = []
        for h in range(heads):
            score = jnp.where(keep, dot(parts[h], key, NT), MASKED_SCORE)
            scores[j, h] = score
            new.append(jnp.maximum(tops[h], jnp.max(score, axis=1, keepdims=True)))
        return tuple(new)

    tops = lax.fori_loop(
        low, i + 1, score_block, tuple(jnp.full((rows, 1), MASKED_SCORE, F32) for _ in range(heads))
    )

    def value_block(j, carry):
        sums, total = carry
        chances, new = [], []
        for h in range(heads):
            chance = jnp.exp(scores[j, h] - tops[h])
            new.append(sums[h] + jnp.sum(chance, axis=1, keepdims=True))
            chances.append(chance.astype(BF))
        total = total + dot(jnp.concatenate(chances, axis=1), vcat[j], NN)
        return tuple(new), total

    sums, total = lax.fori_loop(
        low,
        i + 1,
        value_block,
        (tuple(jnp.zeros((rows, 1), F32) for _ in range(heads)), jnp.zeros((rows, cols), F32)),
    )
    scale = jnp.zeros((rows, cols), F32)
    for h in range(heads):
        scale = jnp.where(head_mask((rows, cols), h, heads, False), 1.0 / sums[h], scale)
        lse_ref[:, h : h + 1] = tops[h] + jnp.log(sums[h])
    result = total * scale
    o_ref[...] = result
    low_ref[...] = result.astype(BF)


def attend(first, query, key, value, start_column, count):
    length, cols = query.shape
    heads = cols // HEAD_DIM
    size = length // count
    whole = pl.BlockSpec((length, cols), lambda i, first: (0, 0))
    return pl.pallas_call(
        attend_kernel,
        grid_spec=pltpu.PrefetchScalarGridSpec(
            num_scalar_prefetch=1,
            grid=(size,),
            in_specs=[
                pl.BlockSpec((count, cols), lambda i, first: (i, 0)),
                whole,
                whole,
                pl.BlockSpec((count, 1), lambda i, first: (i, 0)),
            ],
            out_specs=[
                pl.BlockSpec((count, cols), lambda i, first: (i, 0)),
                pl.BlockSpec((count, cols), lambda i, first: (i, 0)),
                pl.BlockSpec((count, heads), lambda i, first: (i, 0)),
            ],
            scratch_shapes=[
                pltpu.VMEM((size, heads, count, count), F32),
                pltpu.VMEM((size, heads * count, cols), BF),
            ],
        ),
        out_shape=[
            jax.ShapeDtypeStruct((length, cols), F32),
            jax.ShapeDtypeStruct((length, cols), BF),
            jax.ShapeDtypeStruct((length, heads), F32),
        ],
        compiler_params=params(),
        cost_estimate=cost(18 * length * length * cols, 10 * length * cols),
        name="attend",
    )(first, query, key, value, start_column)


def attend_back_kernel(
    first, spot, q_ref, k_ref, v_ref, do_ref, lse_ref, delta_ref, start_ref,
    cq_ref, sq_ref, ck_ref, sk_ref, out_ref, kcat, dk_ref, dv_ref,
):
    i = pl.program_id(0)
    rows, cols = q_ref.shape
    half = cols // 2
    heads = cols // HEAD_DIM
    blocks = k_ref.shape[0] // rows

    @pl.when(i == 0)
    def _():
        dk_ref[...] = jnp.zeros_like(dk_ref)
        dv_ref[...] = jnp.zeros_like(dv_ref)
        for b in range(blocks):
            key = k_ref[b * rows : (b + 1) * rows, :]
            for h in range(heads):
                kcat[b, h * rows : (h + 1) * rows, :] = jnp.where(
                    head_mask((rows, cols), h, heads, True), key, jnp.zeros_like(key)
                )

    query, grad = q_ref[...], do_ref[...]
    parts = [
        jnp.where(head_mask((rows, cols), h, heads, True), query, jnp.zeros_like(query))
        for h in range(heads)
    ]
    grads = [
        jnp.where(head_mask((rows, cols), h, heads, False), grad, jnp.zeros_like(grad))
        for h in range(heads)
    ]
    query_stack = jnp.concatenate(parts, axis=0)
    grad_stack = jnp.concatenate(grads, axis=0)
    start = start_ref[...]
    place = i * rows + lax.broadcasted_iota(jnp.int32, (rows, rows), 1)
    line = lax.broadcasted_iota(jnp.int32, (rows, rows), 0)

    def block(j, total):
        where = pl.ds(pl.multiple_of(j * rows, rows), rows)
        column = j * rows + line
        keep = (column <= place) & (column >= start)
        key, value = k_ref[where, :], v_ref[where, :]
        chances, slopes = [], []
        for h in range(heads):
            score = jnp.where(keep, dot(key, parts[h], NT), MASKED_SCORE)
            chance = jnp.exp(score - lse_ref[h : h + 1, :])
            product = dot(value, grads[h], NT)
            slopes.append((chance * (product - delta_ref[h : h + 1, :])).astype(BF))
            chances.append(chance.astype(BF))
        slope = jnp.concatenate(slopes, axis=1)
        dk_ref[where, :] += dot(slope, query_stack, NN)
        dv_ref[where, :] += dot(jnp.concatenate(chances, axis=1), grad_stack, NN)
        return total + dot(jnp.concatenate(slopes, axis=0), kcat[j], TN)

    total = lax.fori_loop(first[i], i + 1, block, jnp.zeros((rows, cols), F32))
    here = pl.ds(pl.multiple_of(i * rows, rows), rows)
    target = pl.ds(pl.multiple_of(spot[i] * rows, rows), rows)
    cq, sq = cq_ref[here, :], sq_ref[here, :]
    d1, d2 = total[:, :half], total[:, half:]
    out_ref[target, :half] = (d1 * cq + d2 * sq).astype(BF)
    out_ref[target, half:cols] = (d2 * cq - d1 * sq).astype(BF)

    @pl.when(i == pl.num_programs(0) - 1)
    def _():
        def finish(j, carry):
            where = pl.ds(pl.multiple_of(j * rows, rows), rows)
            goal = pl.ds(pl.multiple_of(spot[j] * rows, rows), rows)
            ck, sk = ck_ref[where, :], sk_ref[where, :]
            k1, k2 = dk_ref[where, :half], dk_ref[where, half:]
            out_ref[goal, cols : cols + half] = (k1 * ck + k2 * sk).astype(BF)
            out_ref[goal, cols + half : 2 * cols] = (k2 * ck - k1 * sk).astype(BF)
            out_ref[goal, 2 * cols :] = dv_ref[where, :].astype(BF)
            return carry

        lax.fori_loop(0, blocks, finish, 0)


def attend_back(first, spot, query, key, value, grad, lse, delta, start_row, tables, count):
    length, cols = query.shape
    heads = cols // HEAD_DIM
    size = length // count
    whole = pl.BlockSpec((length, cols), lambda i, *_: (0, 0))
    table = pl.BlockSpec((length, cols // 2), lambda i, *_: (0, 0))
    rows = pl.BlockSpec((count, cols), lambda i, *_: (i, 0))
    line = pl.BlockSpec((pl.squeezed, heads, count), lambda i, *_: (i, 0, 0))
    return pl.pallas_call(
        attend_back_kernel,
        grid_spec=pltpu.PrefetchScalarGridSpec(
            num_scalar_prefetch=2,
            grid=(size,),
            in_specs=[
                rows,
                whole,
                whole,
                rows,
                line,
                line,
                pl.BlockSpec((pl.squeezed, 1, count), lambda i, *_: (i, 0, 0)),
                table,
                table,
                table,
                table,
            ],
            out_specs=pl.BlockSpec((length, 3 * cols), lambda i, *_: (0, 0)),
            scratch_shapes=[
                pltpu.VMEM((size, heads * count, cols), BF),
                pltpu.VMEM((length, cols), F32),
                pltpu.VMEM((length, cols), F32),
            ],
        ),
        out_shape=jax.ShapeDtypeStruct((length, 3 * cols), BF),
        compiler_params=params(),
        cost_estimate=cost(24 * length * length * cols, 20 * length * cols),
        name="attend_back",
    )(first, spot, query, key, value, grad, lse, delta, start_row, *tables)


def xpos_tables(heads, scale, positions):
    pair_index = (jnp.arange(HALF * heads) % HALF).astype(F32)
    frequency = 10000.0 ** (-pair_index / HALF)
    angles = positions[:, None] * frequency[None, :]
    zeta_base = (pair_index / HALF + 0.4) / 1.4
    growth = zeta_base[None, :] ** ((positions[:, None] - SEQ_LEN // 2) / SCALE_BASE)
    cosine, sine = jnp.cos(angles), jnp.sin(angles)
    return cosine * growth * scale, sine * growth * scale, cosine / growth, sine / growth


def on_device(
    layer_input,
    segment_ids,
    cotangent,
    projections,
    output_weight,
    up_weight,
    down_weight,
    norm_gains,
    hidden_gain,
    decays,
    average_projections,
    average_output,
    average_up,
    average_down,
    average_gains,
    average_hidden,
):
    size = lax.axis_size("seq")
    groups = lax.axis_size("tensor")
    me = lax.axis_index("seq")
    group = lax.axis_index("tensor")
    chunks, count, width = layer_input.shape
    length = segment_ids.shape[1]
    block_cols = projections.shape[2]
    heads = width // HEAD_DIM
    per_block = block_cols // HEAD_DIM
    mine = heads // size
    cols = mine * HEAD_DIM
    even_split = per_block % size == 0
    units = up_weight.shape[1] // size
    hidden_cols = units * groups
    hidden_total = hidden_cols * size

    each = per_block // size if even_split else 0
    split = each * HEAD_DIM

    def to_order(rows):
        if not even_split:
            return rows
        shaped = rows.reshape((groups, size, split) + rows.shape[1:])
        return jnp.swapaxes(shaped, 0, 1).reshape(rows.shape)

    def from_order(rows):
        if not even_split:
            return rows
        shaped = rows.reshape((size, groups, split) + rows.shape[1:])
        return jnp.swapaxes(shaped, 0, 1).reshape(rows.shape)

    line = Line()
    masks = np.concatenate([np.arange(0, size, 2), np.arange(1, size, 2)]).astype(np.int32)
    place = (jnp.asarray(masks) ^ me).astype(jnp.int32)
    middle = length // 2
    halves = (0, 1)

    gains_all = lax.all_gather(norm_gains, "seq", axis=1, tiled=True).astype(F32)
    gain_attn, gain_ffn = gains_all[0], gains_all[2][None]
    gain_inner = to_order(gains_all[1]).reshape(size, 1, cols)
    inputs = [layer_input[c].astype(F32) for c in range(chunks)]
    normed = [row_norm(rows) for rows in inputs]
    sent_in = [(normed[c][0] * gain_attn).astype(BF) for c in range(chunks)]

    turned = projections.transpose(1, 2, 0)
    if even_split:
        sent = turned.reshape(3, size, split, count).transpose(1, 0, 2, 3)
        came = lax.all_to_all(sent, "seq", 0, 0, tiled=True)
        raw = lax.all_gather(came, "tensor", axis=0, tiled=False)
    else:
        wide = lax.all_gather(turned, "tensor", axis=1, tiled=True)
        sent = wide.reshape(3, size, cols, count).transpose(1, 0, 2, 3)
        came = lax.all_to_all(sent, "seq", 0, 0, tiled=True)
        raw = came[None]
    proj, proj_plain = arrange(raw)
    tall = lax.all_gather(after(output_weight, came), "tensor", axis=0, tiled=True)

    def swapped(kind):
        if kind == "up":
            sent = line.put(up_weight).reshape(count, size, units).transpose(1, 0, 2)
            return lax.all_to_all(sent, "seq", 0, 0, tiled=True).reshape(width, units)
        sent = line.put(down_weight).reshape(size, units, count)
        came = lax.all_to_all(sent, "seq", 0, 0, tiled=True)
        return came.transpose(1, 0, 2).reshape(units, width)

    gain_hidden = jnp.zeros((groups, units), BF)
    for k in range(groups):
        part = hidden_gain
        if k:
            part = lax.ppermute(part, "tensor", [(i, (i - k) % groups) for i in range(groups)])
        gain_hidden = lax.dynamic_update_slice(
            gain_hidden, part.reshape(1, units), ((group + k) % groups, 0)
        )
    gain_hidden = gain_hidden.astype(F32).reshape(1, hidden_cols)

    blocks = jnp.arange(size, dtype=jnp.int32) ^ me
    spot = (blocks & 1) * (size // 2) + (blocks >> 1)
    segments = lax.dynamic_slice_in_dim(segment_ids, group * chunks, chunks, 0)
    starts = jnp.sum((segments[:, None, :] < segments[:, :, None]).astype(jnp.int32), axis=2)
    firsts = starts.reshape(chunks, size, count)[:, :, 0] // count

    rows_of = {}

    def projected(c, h):
        before = rows_of.get(c) or [jnp.zeros((length, cols), BF) for _ in range(3)]
        rows_of[c] = project(
            line.enter(place[h * (size // 2) : (h + 1) * (size // 2)]),
            ins[c].halves[h],
            proj_plain,
            tables_turn,
            count,
            before,
        )
        line.mark(rows_of[c][0])

    def attention(c):
        attended, low, lse = attend(
            line.enter(firsts[c]), *rows_of[c], starts[c][:, None], count
        )
        line.mark(lse)
        came = lax.all_to_all(low.reshape(size, count, cols), "seq", 0, 0, tiled=True)
        return rows_of[c], attended, lse, came

    def mixed(c):
        result = out_project(
            line.enter(place),
            kept[c][3],
            pieces.halves,
            layer_input[c],
            gain_inner,
            gain_ffn,
            split,
        )
        line.mark(result[1])
        return result

    ins = [Gather(line, sent_in[0])]
    line.mark(ins[0].pieces[-1])
    ins[0].corner()
    ins.append(Gather(line, sent_in[1]))
    came_up = swapped("up")
    line.note(gain_hidden)
    turn = line.enter(jnp.arange(SEQ_LEN, dtype=F32))
    tables_turn = xpos_tables(mine, FACTOR, turn)
    line.mark(tables_turn[0])
    ins[0].core()
    line.note(came_up)
    came_down = swapped("down")
    up_parts = lax.all_gather(after(came_up, tall), "tensor", axis=0, tiled=False)
    proj, proj_plain = arrange(line.enter(raw))
    line.mark(proj)
    ins[1].corner()
    line.note(came_down)
    projected(0, 0)
    pieces = Gather(line, tall)
    projected(0, 1)
    ins[1].core()
    down = lax.all_gather(line.put(came_down), "tensor", axis=0, tiled=True)
    kept = [attention(0)]
    pieces.corner()
    cots = [Gather(line, cotangent[0])]
    projected(1, 0)
    projected(1, 1)
    pieces.core()
    kept.append(attention(1))
    cots[0].corner()
    line.note(kept[0][3])
    outs = [mixed(0)]
    cots[0].core()
    mids = [Gather(line, outs[0][2])]
    line.note(kept[1][3])
    outs.append(mixed(1))
    cots.append(Gather(line, cotangent[1]))

    def graded(c, h):
        scaled = ffn_grad(cots[c].halves[h], down, line.enter(gain_hidden))
        line.mark(scaled)
        return scaled

    def entered(c, h, scaled=None):
        if scaled is None:
            result = ffn_in(
                mids[c].halves[h], up_parts, None, cots[c].halves[h], down, line.enter(gain_hidden)
            )
        else:
            result = ffn_in(mids[c].halves[h], up_parts, line.enter(scaled))
        line.mark(result[3])
        return result

    def summed(held):
        stats = jnp.concatenate([held[h][3] for h in halves]).reshape(size, count, 4)
        return BlockSum(line, stats.transpose(0, 2, 1))

    def row_stats(sums):
        stats = sums.total() / hidden_total
        mean, second, plain, cross = (stats[:, k] for k in range(4))
        inverse = lax.rsqrt(second - mean * mean + EPSILON)
        cross = inverse * (cross - mean * plain)
        return jnp.stack([mean, inverse, plain, cross], axis=-1).reshape(length, 4)

    def left(c, h):
        result = ffn_out(
            held[c][h][:3], stats[c], line.enter(gain_hidden), up_parts, down, h * middle
        )
        line.mark(result[4])
        return result

    scaled0 = [graded(0, 0)]
    mids[0].corner()
    mids.append(Gather(line, outs[1][2]))
    scaled0.append(graded(0, 1))
    mids[0].core()
    cots[1].corner()
    held = [[entered(0, 0, scaled0[0])]]
    cots[1].core()
    mids[1].corner()
    held[0].append(entered(0, 1, scaled0[1]))
    mids[1].core()
    sums = [summed(held[0])]
    held.append([entered(1, 0)])
    sums[0].more()
    held[1].append(entered(1, 1))
    sums[0].more()
    sums.append(summed(held[1]))
    stats = [row_stats(sums[0])]
    done = [[None, None] for _ in range(chunks)]
    done[0][1] = left(0, 1)
    sums[1].more()
    mid_sums = [Scatter(line, done[0][1][2], count)]
    done[0][0] = left(0, 0)
    mid_sums[0].corner(done[0][0][2])
    sums[1].more()
    stats.append(row_stats(sums[1]))
    done[1][1] = left(1, 1)
    mid_sums[0].near()
    mid_sums.append(Scatter(line, done[1][1][2], count))
    done[1][0] = left(1, 0)
    mid_sums[1].corner(done[1][0][2])
    out_sums = [Scatter(line, done[0][1][3], count)]
    hidden_gain_grad = sum(done[c][h][4] for c in range(chunks) for h in halves)
    hidden_gain_grad = (hidden_gain_grad / gain_hidden).reshape(groups, units)
    down_grad = weight_grad(
        [line.enter(done[c][h][0]) for c in range(chunks) for h in halves],
        [cots[c].halves[h] for c in range(chunks) for h in halves],
        [0] * 4,
    )[0]
    line.mark(down_grad)
    scatter = partial(lax.psum_scatter, axis_name="tensor", scatter_dimension=0, tiled=True)
    down_own = scatter(down_grad)

    def back_out(c):
        residual_grad, attn_grad, sent, ffn_gain, inner_gain = out_back(
            line.enter(place),
            mid_sums[c].total(),
            outs[c][1],
            cotangent[c],
            kept[c][3],
            pieces.halves,
            gain_inner,
            gain_ffn,
            split,
        )
        line.mark(sent)
        grad = lax.all_to_all(sent, "seq", 0, 0, tiled=True).reshape(length, cols)
        return residual_grad, attn_grad, grad, ffn_gain[0], inner_gain.reshape(width)

    def back_attention(c):
        turned_rows, attended, lse, came = kept[c]
        grad = backs[c][2]
        delta = jnp.sum((grad.astype(F32) * attended).reshape(length, mine, HEAD_DIM), axis=2)
        slope = attend_back(
            line.enter(firsts[c]),
            spot,
            *turned_rows,
            grad,
            lse.reshape(size, count, mine).transpose(0, 2, 1),
            delta.reshape(size, count, mine).transpose(0, 2, 1),
            starts[c].reshape(size, 1, count),
            tables_turn,
            count,
        )
        line.mark(slope)
        return slope

    def times(rows, weights, offset):
        result = multiply(line.enter(rows), weights, offset, middle)
        line.mark(result)
        return result

    mid_sums[1].near()
    backs = [back_out(0)]
    out_sums[0].corner(done[0][0][3])
    out_sums.append(Scatter(line, done[1][1][3], count))
    up_grad = weight_grad(
        [line.enter(done[c][h][1]) for c in range(chunks) for h in halves],
        [mids[c].halves[h] for c in range(chunks) for h in halves],
        [0] * 4,
    )[0]
    line.mark(up_grad)
    up_own = scatter(up_grad)
    out_sums[0].near()
    backs.append(back_out(1))
    line.note(backs[0][2])
    output_grad = out_grad(
        [line.enter(outs[c][0]) for c in range(chunks)], [back[1] for back in backs], split
    )
    line.mark(output_grad)
    output_own = scatter(
        lax.psum_scatter(output_grad, "seq", scatter_dimension=0, tiled=True).reshape(width, count)
    )
    out_sums[1].corner(done[1][0][3])
    slopes = [back_attention(0)]
    out_sums[1].near()
    line.note(down_own, backs[1][2])
    odd = times(slopes[0], proj, middle)
    in_sums = [Scatter(line, odd, count)]
    even = times(slopes[0], proj, 0)
    in_sums[0].corner(even)
    slopes.append(back_attention(1))
    in_sums[0].near()
    line.note(up_own)
    odd = times(slopes[1], proj, middle)
    in_sums.append(Scatter(line, odd, count))
    even = times(slopes[1], proj, 0)
    in_sums[1].corner(even)
    proj_grad, attn_gain = weight_grad(
        [line.enter(slopes[c]) for c in range(chunks) for h in halves],
        [ins[c].halves[h] for c in range(chunks) for h in halves],
        [h * middle for c in range(chunks) for h in halves],
        proj,
    )
    line.mark(proj_grad)
    in_sums[1].near()

    outputs = [outs[c][1] + out_sums[c].total() for c in range(chunks)]
    input_grads = [
        backs[c][0] + row_norm_back(in_sums[c].total() * gain_attn, *normed[c])
        for c in range(chunks)
    ]
    gain_terms = jnp.stack(
        [
            attn_gain[0] / gain_attn,
            from_order(sum(back[4] for back in backs)),
            sum(back[3] for back in backs),
        ]
    )
    gains_grad = lax.psum(
        lax.psum_scatter(gain_terms, "seq", scatter_dimension=1, tiled=True), "tensor"
    )

    part = down_own.reshape(units, size, count).transpose(1, 0, 2)
    down_final = lax.all_to_all(part, "seq", 0, 0, tiled=True).reshape(size * units, count)
    part = up_own.reshape(units, size, count).transpose(1, 0, 2)
    part = lax.all_to_all(part, "seq", 0, 0, tiled=True)
    up_final = part.transpose(2, 0, 1).reshape(count, size * units)
    output_final = output_own
    part = proj_grad
    turned_heads = part[: 2 * cols].reshape(2, 2, mine, HALF, width).transpose(0, 2, 1, 3, 4)
    part = jnp.concatenate([turned_heads.reshape(2, cols, width), part[None, 2 * cols :]])
    if even_split:
        part = part.reshape(3, groups, split, width).transpose(1, 0, 2, 3)
        part = scatter(part.reshape(3 * cols, width))
        part = part.reshape(3, split, size, count).transpose(2, 0, 1, 3)
        part = lax.all_to_all(part, "seq", 0, 0, tiled=True)
        proj_final = part.transpose(3, 1, 0, 2).reshape(count, 3, block_cols)
    else:
        part = lax.psum(part, "tensor").reshape(3, cols, size, count).transpose(2, 0, 1, 3)
        part = lax.all_to_all(part, "seq", 0, 0, tiled=True)
        part = part.transpose(3, 1, 0, 2).reshape(count, 3, width)
        proj_final = lax.dynamic_slice_in_dim(part, group * block_cols, block_cols, 2)
    hidden_final = lax.psum_scatter(
        hidden_gain_grad, "tensor", scatter_dimension=0, tiled=True
    )

    grads = (
        proj_final.astype(F32),
        output_final.astype(F32),
        up_final.astype(F32),
        down_final.astype(F32),
        gains_grad.astype(F32),
        hidden_final.astype(F32),
    )
    averages = (
        average_projections,
        average_output,
        average_up,
        average_down,
        average_gains,
        average_hidden,
    )
    updated = tuple(
        decays[i] * averages[i] + (1.0 - decays[i]) * grads[i] for i in range(6)
    )
    return (jnp.stack(outputs).astype(BF), jnp.stack(input_grads)) + grads + updated


def solution(mesh):
    weights = (P("seq", None, "tensor"), P("tensor", "seq"), P("seq", "tensor"), P("tensor", "seq"))
    gains = (P(None, "seq"), P("tensor", "seq"))
    rows = P("tensor", "seq", None)
    return jax.shard_map(
        on_device,
        mesh=mesh,
        in_specs=(rows, P(), rows) + weights + gains + (P(),) + weights + gains,
        out_specs=(rows, rows) + weights + gains + weights + gains,
        check_vma=False,
    )
```

```python
from functools import partial

import jax
import jax.numpy as jnp
import numpy as np
from jax import lax
from jax.experimental import pallas as pl
from jax.experimental.pallas import tpu as pltpu
from jax.sharding import PartitionSpec as P

HEAD_DIM = 64
HALF = HEAD_DIM // 2
SEQ_LEN = 2048
SCALE_BASE = 512
EPSILON = 1e-05
MASKED_SCORE = -1e30
FACTOR = HEAD_DIM ** (-0.5)
BF = jnp.bfloat16
F32 = jnp.float32
SCALE = 8
VMEM_LIMIT = 56 * 1024 * 1024


def swap(block, bit):
    size = lax.axis_size("seq")
    return lax.ppermute(block, "seq", [(i, i ^ bit) for i in range(size)])


def after(array, *others):
    return lax.optimization_barrier((array,) + others)[0]


class Line:
    def __init__(self):
        self.last, self.noted = (), ()

    def put(self, array):
        return after(array, *self.last) if self.last else array

    def note(self, *arrays):
        self.noted += arrays

    def enter(self, array):
        return after(array, *self.last, *self.noted) if self.last + self.noted else array

    def mark(self, *arrays):
        self.last, self.noted = arrays, ()


def join_kernel(*refs):
    parts, out_ref, held, came, left = refs[:-4], refs[-4], refs[-3], refs[-2], refs[-1]
    spots, at = [], 0
    for part in parts:
        spots.append(pl.ds(at, part.shape[0]))
        at += part.shape[0]
    ins = [
        pltpu.make_async_copy(part, held.at[spot], came.at[k])
        for k, (part, spot) in enumerate(zip(parts, spots))
    ]
    outs = [
        pltpu.make_async_copy(held.at[spot], out_ref.at[spot], left.at[k])
        for k, spot in enumerate(spots)
    ]
    for copy in ins:
        copy.start()
    for k, copy in enumerate(ins):
        copy.wait()
        outs[k].start()
    for copy in outs:
        copy.wait()


def join(parts):
    rows, width = sum(part.shape[0] for part in parts), parts[0].shape[1]
    if any(part.shape[0] % 16 for part in parts) or width % 128:
        return jnp.concatenate(parts)
    return pl.pallas_call(
        join_kernel,
        in_specs=[pl.BlockSpec(memory_space=pl.ANY)] * len(parts),
        out_specs=pl.BlockSpec(memory_space=pl.ANY),
        out_shape=jax.ShapeDtypeStruct((rows, width), parts[0].dtype),
        scratch_shapes=[
            pltpu.VMEM((rows, width), parts[0].dtype),
            pltpu.SemaphoreType.DMA((len(parts),)),
            pltpu.SemaphoreType.DMA((len(parts),)),
        ],
        compiler_params=params(),
        cost_estimate=cost(0, 4 * rows * width),
        name="join",
    )(*parts)


class Gather:
    def __init__(self, line, rows):
        self.line = line
        self.size = lax.axis_size("seq")
        self.rows = line.put(rows)
        self.pieces = [self.rows]
        if self.size == 8:
            self.pieces += [swap(self.rows, 2), swap(self.rows, 4)]
        line.note(self.rows)

    def corner(self):
        if self.size == 8:
            half = self.rows.shape[0] // 2
            across = self.line.put(self.pieces[1])[:half]
            along = self.line.put(self.pieces[2])[half:]
            self.pieces += [swap(across, 4), swap(along, 2)]
            self.line.note(across, along)
        return self

    def core(self):
        even = self.line.put(self.pieces[0])
        if self.size == 8:
            even = join([even] + self.pieces[1:])
        else:
            bit = 2
            while bit < self.size:
                even = jnp.concatenate([even, swap(even, bit)])
                bit *= 2
        self.halves = (even, swap(even, 1))
        self.line.note(even)
        return self


class Scatter:
    def __init__(self, line, odd, count):
        self.line, self.count = line, count
        self.size = lax.axis_size("seq")
        self.other = swap(odd, 1)

    def block(self, k, start, stop):
        here = slice(k * self.count + start, k * self.count + stop)
        return self.even[here].astype(F32) + self.other[here].astype(F32)

    def corner(self, even):
        self.even = self.line.put(even)
        if self.size == 8:
            half = self.count // 2
            low = self.block(3, 0, half).astype(BF)
            high = self.block(3, half, self.count).astype(BF)
            self.low, self.high = swap(low, 4), swap(high, 2)
            self.line.note(low, high)
        return self

    def near(self):
        if self.size == 8:
            half = self.count // 2
            low, high = self.line.put(self.low), self.line.put(self.high)
            across = [self.block(1, 0, half) + low.astype(F32), self.block(1, half, self.count)]
            along = [self.block(2, 0, half), self.block(2, half, self.count) + high.astype(F32)]
            across = jnp.concatenate(across).astype(BF)
            along = jnp.concatenate(along).astype(BF)
            self.parts = [swap(across, 2), swap(along, 4)]
            self.line.note(across, along)
        return self

    def total(self):
        if self.size == 8:
            return self.block(0, 0, self.count) + sum(part.astype(F32) for part in self.parts)
        total, bit = self.even.astype(F32) + self.other.astype(F32), self.size // 2
        while bit > 1:
            middle = total.shape[0] // 2
            total = total[:middle] + swap(total[middle:].astype(BF), bit).astype(F32)
            bit //= 2
        return total


class BlockSum:
    def __init__(self, line, stats):
        self.line, self.stats, self.bit = line, line.put(stats), 1
        self.size = stats.shape[0]
        self.send()

    def send(self):
        self.other = swap(self.stats, self.bit)
        self.line.note(self.stats)

    def add(self):
        shift = (self.bit & 1) * (self.size // 2) + (self.bit >> 1)
        other = self.line.put(self.other)
        self.stats = self.stats + jnp.stack([other[i ^ shift] for i in range(self.size)])
        self.bit *= 2

    def more(self):
        self.add()
        if self.bit < self.size:
            self.send()

    def total(self):
        while self.bit < self.size:
            self.add()
            if self.bit < self.size:
                self.send()
        return self.stats


def row_norm(features):
    mean = jnp.mean(features, axis=-1, keepdims=True)
    second = jnp.mean(features * features, axis=-1, keepdims=True)
    inverse = lax.rsqrt(second - mean * mean + EPSILON)
    return (features - mean) * inverse, inverse


def row_norm_back(scaled, normed, inverse):
    return inverse * (
        scaled
        - jnp.mean(scaled, axis=-1, keepdims=True)
        - normed * jnp.mean(scaled * normed, axis=-1, keepdims=True)
    )


def dot(a, b, dims):
    return lax.dot_general(a, b, (dims, ((), ())), preferred_element_type=F32)


NN = ((1,), (0,))
NT = ((1,), (1,))
TN = ((0,), (0,))


def params():
    return pltpu.CompilerParams(vmem_limit_bytes=VMEM_LIMIT)


def cost(flops, moved, special=0):
    return pl.CostEstimate(
        flops=int(flops * SCALE), bytes_accessed=int(moved * SCALE), transcendentals=int(special * SCALE)
    )


def qkv_kernel(
    place, x_ref, w_ref, cq_ref, sq_ref, ck_ref, sk_ref, qa, ka, va, q_ref, k_ref, v_ref
):
    cols = q_ref.shape[1]
    half = cols // 2
    full = dot(x_ref[...], w_ref[...], NN)
    q1, q2 = full[:, :half], full[:, half:cols]
    k1, k2 = full[:, cols : cols + half], full[:, cols + half : 2 * cols]
    cq, sq, ck, sk = cq_ref[...], sq_ref[...], ck_ref[...], sk_ref[...]
    q_ref[:, :half] = (q1 * cq - q2 * sq).astype(BF)
    q_ref[:, half:] = (q2 * cq + q1 * sq).astype(BF)
    k_ref[:, :half] = (k1 * ck - k2 * sk).astype(BF)
    k_ref[:, half:] = (k2 * ck + k1 * sk).astype(BF)
    v_ref[...] = full[:, 2 * cols :].astype(BF)


def project(place, rows, weights, tables, count, before):
    here, width = rows.shape
    cols = weights.shape[1] // 3
    length = tables[0].shape[0]
    table = pl.BlockSpec((count, cols // 2), lambda i, place: (place[i], 0))
    out = pl.BlockSpec((count, cols), lambda i, place: (place[i], 0))
    held = pl.BlockSpec(memory_space=pl.ANY)
    return pl.pallas_call(
        qkv_kernel,
        grid_spec=pltpu.PrefetchScalarGridSpec(
            num_scalar_prefetch=1,
            grid=(here // count,),
            in_specs=[
                pl.BlockSpec((count, width), lambda i, place: (i, 0)),
                pl.BlockSpec((width, 3 * cols), lambda i, place: (0, 0)),
                table,
                table,
                table,
                table,
                held,
                held,
                held,
            ],
            out_specs=[out, out, out],
        ),
        out_shape=[jax.ShapeDtypeStruct((length, cols), BF)] * 3,
        input_output_aliases={7: 0, 8: 1, 9: 2},
        compiler_params=params(),
        cost_estimate=cost(
            2 * here * width * 3 * cols, 2 * (here * width + 3 * cols * width + 3 * here * cols)
        ),
        name="project",
    )(place, rows, weights, *tables, *before)


def turned_row(kind, head, heads):
    first = kind * heads * HEAD_DIM
    if kind == 2:
        return first + head * HEAD_DIM, first + head * HEAD_DIM + HALF
    return first + head * HALF, first + (heads + head) * HALF


def arrange_kernel(raw_ref, turned_ref, plain_ref):
    parts, size, _, split, count = raw_ref.shape
    each = split // HEAD_DIM
    for kind in range(3):
        for t in range(parts):
            for j in range(each):
                starts = turned_row(kind, t * each + j, parts * each)
                for b in range(size):
                    for h in range(2):
                        here = slice(j * HEAD_DIM + h * HALF, j * HEAD_DIM + (h + 1) * HALF)
                        turned_ref[starts[h] : starts[h] + HALF, b * count : (b + 1) * count] = (
                            raw_ref[t, b, kind, here, :]
                        )
    plain_ref[...] = turned_ref[...].T


def arrange(raw):
    parts, size, _, split, count = raw.shape
    cols, width = parts * split, size * count
    if count % 128:
        proj = raw.transpose(2, 0, 3, 1, 4).reshape(3, cols, width)
        heads = proj[:2].reshape(2, cols // HEAD_DIM, 2, HALF, width).transpose(0, 2, 1, 3, 4)
        turned = jnp.concatenate([heads.reshape(2 * cols, width), proj[2]])
        return turned, turned.T
    return pl.pallas_call(
        arrange_kernel,
        out_shape=[
            jax.ShapeDtypeStruct((3 * cols, width), BF),
            jax.ShapeDtypeStruct((width, 3 * cols), BF),
        ],
        compiler_params=params(),
        cost_estimate=cost(0, 18 * cols * width),
        name="arrange",
    )(raw)


def out_grad_kernel(*refs):
    out_ref = refs[-1]
    parts = (len(refs) - 1) // 2
    total = dot(refs[0][...], refs[parts][...], TN)
    for k in range(1, parts):
        total = total + dot(refs[k][...], refs[parts + k][...], TN)
    low = total.astype(BF)
    count = out_ref.shape[-1]
    for b in range(out_ref.shape[0]):
        out_ref[b] = low[:, b * count : (b + 1) * count].reshape(out_ref.shape[1:])


def out_grad(inners, grads, split):
    size, count, cols = inners[0].shape
    width = size * cols
    count_out = width // size
    if split:
        shape = (size, cols // split, size, split, count_out)
        spec = pl.BlockSpec(
            (size, cols // split, pl.squeezed, split, count_out), lambda i: (0, 0, i, 0, 0)
        )
    else:
        shape = (size, size, cols, count_out)
        spec = pl.BlockSpec((size, pl.squeezed, cols, count_out), lambda i: (0, i, 0, 0))
    parts = len(inners)
    return pl.pallas_call(
        out_grad_kernel,
        grid=(size,),
        in_specs=[pl.BlockSpec((pl.squeezed, count, cols), lambda i: (i, 0, 0))] * parts
        + [pl.BlockSpec((count, width), lambda i: (0, 0))] * parts,
        out_specs=spec,
        out_shape=jax.ShapeDtypeStruct(shape, BF),
        compiler_params=params(),
        cost_estimate=cost(
            2 * parts * count * width * width, 4 * parts * count * width + 2 * width * width
        ),
        name="out_grad",
    )(*inners, *grads).reshape(size, width, count_out)


def head_rows(weight, b, split):
    return weight[:, b].reshape(-1, weight.shape[-1]) if split else weight[b]


def out_kernel(
    split, place, came_ref, even_ref, odd_ref, x_ref, gi_ref, gf_ref, inner_ref, res_ref, mid_ref, acc
):
    i = pl.program_id(0)
    size, rows, cols = came_ref.shape
    width = size * cols
    count = width // size

    @pl.when(i == 0)
    def _():
        first = jnp.zeros((rows, 1), F32)
        second = jnp.zeros((rows, 1), F32)
        for b in range(size):
            part = came_ref[b].astype(F32)
            first += jnp.sum(part, axis=1, keepdims=True)
            second += jnp.sum(part * part, axis=1, keepdims=True)
        mean = first / width
        inverse = lax.rsqrt(second / width - mean * mean + EPSILON)
        for b in range(size):
            inner_ref[b] = ((came_ref[b].astype(F32) - mean) * inverse * gi_ref[b]).astype(BF)

    def piece(ref):
        total = jnp.zeros((rows, count), F32)
        for b in range(size):
            total += dot(inner_ref[b], head_rows(ref, b, split), NN)
        acc[place[i]] = total

    pl.when(i < size // 2)(lambda: piece(even_ref))
    pl.when(i >= size // 2)(lambda: piece(odd_ref))

    @pl.when(i == size - 1)
    def _():
        first = jnp.zeros((rows, 1), F32)
        second = jnp.zeros((rows, 1), F32)
        for b in range(size):
            here = slice(b * count, (b + 1) * count)
            part = acc[b] + x_ref[:, here].astype(F32)
            res_ref[:, here] = part
            first += jnp.sum(part, axis=1, keepdims=True)
            second += jnp.sum(part * part, axis=1, keepdims=True)
        mean = first / width
        inverse = lax.rsqrt(second / width - mean * mean + EPSILON)
        mid_ref[...] = ((res_ref[...] - mean) * inverse * gf_ref[...]).astype(BF)


def weight_views(pieces, size, cols, split):
    half, count = size // 2, pieces[0].shape[1]
    if split:
        shape = (cols // split, size, split, count)
    else:
        shape = (size, cols, count)
    zeros = (0,) * len(shape)
    views = [piece.reshape((half,) + shape) for piece in pieces]
    specs = [
        pl.BlockSpec((pl.squeezed,) + shape, lambda i, *_: (jnp.minimum(i, half - 1),) + zeros),
        pl.BlockSpec((pl.squeezed,) + shape, lambda i, *_: (jnp.maximum(i - half, 0),) + zeros),
    ]
    return views, specs


def out_project(place, came, pieces, rows, gain_inner, gain_ffn, split):
    size, count, cols = came.shape
    width = size * cols
    views, specs = weight_views(pieces, size, cols, split)
    blocks = pl.BlockSpec((size, count, cols), lambda i, *_: (0, 0, 0))
    flat = pl.BlockSpec((count, width), lambda i, *_: (0, 0))
    return pl.pallas_call(
        partial(out_kernel, split),
        grid_spec=pltpu.PrefetchScalarGridSpec(
            num_scalar_prefetch=1,
            grid=(size,),
            in_specs=[blocks]
            + specs
            + [
                flat,
                pl.BlockSpec((size, 1, cols), lambda i, *_: (0, 0, 0)),
                pl.BlockSpec((1, width), lambda i, *_: (0, 0)),
            ],
            out_specs=[blocks, flat, flat],
            scratch_shapes=[pltpu.VMEM((size, count, width // size), F32)],
        ),
        out_shape=[
            jax.ShapeDtypeStruct((size, count, cols), BF),
            jax.ShapeDtypeStruct((count, width), F32),
            jax.ShapeDtypeStruct((count, width), BF),
        ],
        compiler_params=params(),
        cost_estimate=cost(2 * count * width * width, 2 * width * width + 12 * count * width),
        name="out_project",
    )(place, came, *views, rows, gain_inner, gain_ffn)


def out_back_kernel(
    split, place, grad_ref, res_ref, cot_ref, came_ref, even_ref, odd_ref, gi_ref, gf_ref,
    rg_ref, ag_ref, back_ref, fg_ref, ig_ref, held, sent,
):
    i = pl.program_id(0)
    size, rows, cols = came_ref.shape
    width = size * cols
    count = width // size

    @pl.when(i == 0)
    def _():
        residual, grad = res_ref[...], grad_ref[...]
        mean = jnp.mean(residual, axis=1, keepdims=True)
        second = jnp.mean(residual * residual, axis=1, keepdims=True)
        inverse = lax.rsqrt(second - mean * mean + EPSILON)
        normal = (residual - mean) * inverse
        fg_ref[...] = jnp.sum(grad * normal, axis=0, keepdims=True)
        scaled = grad * gf_ref[...]
        back = inverse * (
            scaled
            - jnp.mean(scaled, axis=1, keepdims=True)
            - normal * jnp.mean(scaled * normal, axis=1, keepdims=True)
        )
        total = cot_ref[...].astype(F32) + back
        rg_ref[...] = total
        low = total.astype(BF)
        ag_ref[...] = low
        for b in range(size):
            sent[b] = low[:, b * count : (b + 1) * count]
        held[...] = jnp.zeros_like(held)

    def piece(ref):
        grad = sent[place[i]]
        for b in range(size):
            held[b] += dot(grad, head_rows(ref, b, split), NT)

    pl.when(i < size // 2)(lambda: piece(even_ref))
    pl.when(i >= size // 2)(lambda: piece(odd_ref))

    @pl.when(i == size - 1)
    def _():
        zero = jnp.zeros((rows, 1), F32)
        first, second = zero, zero
        for b in range(size):
            part = came_ref[b].astype(F32)
            first += jnp.sum(part, axis=1, keepdims=True)
            second += jnp.sum(part * part, axis=1, keepdims=True)
        mean = first / width
        inverse = lax.rsqrt(second / width - mean * mean + EPSILON)
        plain, cross = zero, zero
        for b in range(size):
            normal = (came_ref[b].astype(F32) - mean) * inverse
            grad = held[b]
            ig_ref[b] = jnp.sum(grad * normal, axis=0, keepdims=True)
            scaled = grad * gi_ref[b]
            plain += jnp.sum(scaled, axis=1, keepdims=True)
            cross += jnp.sum(scaled * normal, axis=1, keepdims=True)
        plain, cross = plain / width, cross / width
        for b in range(size):
            normal = (came_ref[b].astype(F32) - mean) * inverse
            back_ref[b] = (inverse * (held[b] * gi_ref[b] - plain - normal * cross)).astype(BF)


def out_back(place, grad, residual, cotangent, came, pieces, gain_inner, gain_ffn, split):
    size, count, cols = came.shape
    width = size * cols
    views, specs = weight_views(pieces, size, cols, split)
    blocks = pl.BlockSpec((size, count, cols), lambda i, *_: (0, 0, 0))
    flat = pl.BlockSpec((count, width), lambda i, *_: (0, 0))
    line = pl.BlockSpec((1, width), lambda i, *_: (0, 0))
    lines = pl.BlockSpec((size, 1, cols), lambda i, *_: (0, 0, 0))
    return pl.pallas_call(
        partial(out_back_kernel, split),
        grid_spec=pltpu.PrefetchScalarGridSpec(
            num_scalar_prefetch=1,
            grid=(size,),
            in_specs=[flat, flat, flat, blocks] + specs + [lines, line],
            out_specs=[flat, flat, blocks, line, lines],
            scratch_shapes=[
                pltpu.VMEM((size, count, cols), F32),
                pltpu.VMEM((size, count, width // size), BF),
            ],
        ),
        out_shape=[
            jax.ShapeDtypeStruct((count, width), F32),
            jax.ShapeDtypeStruct((count, width), BF),
            jax.ShapeDtypeStruct((size, count, cols), BF),
            jax.ShapeDtypeStruct((1, width), F32),
            jax.ShapeDtypeStruct((size, 1, cols), F32),
        ],
        compiler_params=params(),
        cost_estimate=cost(2 * count * width * width, 2 * width * width + 20 * count * width),
        name="out_back",
    )(place, grad, residual, cotangent, came, *views, gain_inner, gain_ffn)


def ffn_grad_kernel(c_ref, down_ref, g_ref, t_ref):
    t_ref[...] = (dot(c_ref[...], down_ref[...], NT) * g_ref[...]).astype(BF)


def ffn_grad(grads, down, gain):
    here, width = grads.shape
    cols = down.shape[0]
    tile = 256
    return pl.pallas_call(
        ffn_grad_kernel,
        grid=(here // tile,),
        in_specs=[
            pl.BlockSpec((tile, width), lambda i: (i, 0)),
            pl.BlockSpec((cols, width), lambda i: (0, 0)),
            pl.BlockSpec((1, cols), lambda i: (0, 0)),
        ],
        out_specs=pl.BlockSpec((tile, cols), lambda i: (i, 0)),
        out_shape=jax.ShapeDtypeStruct((here, cols), BF),
        compiler_params=params(),
        cost_estimate=cost(2 * here * width * cols, 2 * here * (width + cols) + 2 * width * cols),
        name="ffn_grad",
    )(grads, down, gain)


def ffn_in_kernel(given, *refs):
    if given:
        x_ref, t_in_ref, up_ref, a_ref, p_ref, s_ref = refs
    else:
        x_ref, c_ref, up_ref, down_ref, g_ref, a_ref, p_ref, s_ref, t_ref = refs
    parts, _, units = up_ref.shape
    sums = [0.0] * 4
    for k in range(parts):
        here = slice(k * units, (k + 1) * units)
        hidden = dot(x_ref[...], up_ref[k], NN)
        if given:
            scaled = t_in_ref[:, here].astype(F32)
        else:
            low = (dot(c_ref[...], down_ref[here, :], NT) * g_ref[:, here]).astype(BF)
            t_ref[:, here] = low
            scaled = low.astype(F32)
        share = 0.5 * (1.0 + lax.erf(hidden * (2.0**-0.5)))
        activated = hidden * share
        slope = share + hidden * jnp.exp(-0.5 * hidden * hidden) * ((2.0 * np.pi) ** -0.5)
        a_ref[:, here] = activated
        p_ref[:, here] = slope.astype(BF)
        for j, terms in enumerate((activated, activated * activated, scaled, scaled * activated)):
            sums[j] = sums[j] + jnp.sum(terms, axis=1, keepdims=True)
    for j in range(4):
        s_ref[:, j : j + 1] = sums[j]


def ffn_in(rows, up_parts, scaled=None, grads=None, down=None, gain=None):
    given = scaled is not None
    here, width = rows.shape
    parts, _, units = up_parts.shape
    cols = parts * units
    tile = 256
    wide = pl.BlockSpec((tile, width), lambda i: (i, 0))
    out = pl.BlockSpec((tile, cols), lambda i: (i, 0))
    up_spec = pl.BlockSpec(up_parts.shape, lambda i: (0, 0, 0))
    if given:
        arrays, specs = (rows, scaled, up_parts), [wide, out, up_spec]
    else:
        arrays = (rows, grads, up_parts, down, gain)
        specs = [
            wide,
            wide,
            up_spec,
            pl.BlockSpec((cols, width), lambda i: (0, 0)),
            pl.BlockSpec((1, cols), lambda i: (0, 0)),
        ]
    low = jax.ShapeDtypeStruct((here, cols), BF)
    outs = [jax.ShapeDtypeStruct((here, cols), F32), low, jax.ShapeDtypeStruct((here, 4), F32)]
    out_specs = [out, out, pl.BlockSpec((tile, 4), lambda i: (i, 0))]
    result = pl.pallas_call(
        partial(ffn_in_kernel, given),
        grid=(here // tile,),
        in_specs=specs,
        out_specs=out_specs if given else out_specs + [out],
        out_shape=outs if given else outs + [low],
        compiler_params=params(),
        cost_estimate=cost(
            (2 if given else 4) * here * width * cols,
            4 * here * width + 4 * width * cols + 8 * here * cols,
            2 * here * cols,
        ),
        name="ffn_in",
    )(*arrays)
    return result[0], result[1], scaled if given else result[3], result[2]


def ffn_out_kernel(
    a_ref, p_ref, t_ref, s_ref, g_ref, up_ref, down_ref, sq_ref, hg_ref, m_ref, o_ref, n_ref
):
    parts, _, units = up_ref.shape
    stats = s_ref[...]
    mean, inverse, plain, cross = (stats[:, k : k + 1] for k in range(4))
    normal = (a_ref[...] - mean) * inverse
    scaled = t_ref[...].astype(F32)
    squeezed = (normal * g_ref[...]).astype(BF)
    sq_ref[...] = squeezed
    grad = (p_ref[...].astype(F32) * (inverse * (scaled - plain - normal * cross))).astype(BF)
    hg_ref[...] = grad
    total = dot(grad[:, :units], up_ref[0], NT)
    for k in range(1, parts):
        total = total + dot(grad[:, k * units : (k + 1) * units], up_ref[k], NT)
    m_ref[...] = total.astype(BF)
    o_ref[...] = dot(squeezed, down_ref[...], NN).astype(BF)
    part = jnp.sum(scaled * normal, axis=0, keepdims=True)

    @pl.when(pl.program_id(0) == 0)
    def _():
        n_ref[...] = part

    @pl.when(pl.program_id(0) > 0)
    def _():
        n_ref[...] += part


def ffn_out(held, stats, gain, up_parts, down, offset):
    activated, slope, scaled = held
    here, cols = activated.shape
    width = down.shape[1]
    tile = 256
    shift = offset // tile
    out = pl.BlockSpec((tile, cols), lambda i: (i, 0))
    wide = pl.BlockSpec((tile, width), lambda i: (i, 0))
    return pl.pallas_call(
        ffn_out_kernel,
        grid=(here // tile,),
        in_specs=[
            out,
            out,
            out,
            pl.BlockSpec((tile, 4), lambda i: (i + shift, 0)),
            pl.BlockSpec((1, cols), lambda i: (0, 0)),
            pl.BlockSpec(up_parts.shape, lambda i: (0, 0, 0)),
            pl.BlockSpec((cols, width), lambda i: (0, 0)),
        ],
        out_specs=[out, out, wide, wide, pl.BlockSpec((1, cols), lambda i: (0, 0))],
        out_shape=[
            jax.ShapeDtypeStruct((here, cols), BF),
            jax.ShapeDtypeStruct((here, cols), BF),
            jax.ShapeDtypeStruct((here, width), BF),
            jax.ShapeDtypeStruct((here, width), BF),
            jax.ShapeDtypeStruct((1, cols), F32),
        ],
        compiler_params=params(),
        cost_estimate=cost(
            4 * here * width * cols, 12 * here * cols + 4 * width * cols + 4 * here * width
        ),
        name="ffn_out",
    )(activated, slope, scaled, stats, gain, up_parts, down)


def multiply_kernel(x_ref, w_ref, o_ref):
    o_ref[...] = dot(x_ref[...], w_ref[...], NN).astype(BF)


def multiply(rows, weights, offset, here):
    depth, width = weights.shape
    tile = 256
    shift = offset // tile
    return pl.pallas_call(
        multiply_kernel,
        grid=(here // tile,),
        in_specs=[
            pl.BlockSpec((tile, depth), lambda i: (i + shift, 0)),
            pl.BlockSpec((depth, width), lambda i: (0, 0)),
        ],
        out_specs=pl.BlockSpec((tile, width), lambda i: (i, 0)),
        out_shape=jax.ShapeDtypeStruct((here, width), BF),
        compiler_params=params(),
        cost_estimate=cost(2 * here * width * depth, 2 * (here * width + here * depth + depth * width)),
        name="multiply",
    )(rows, weights)


def grads_kernel(weighted, *refs):
    outs = 2 if weighted else 1
    ins = refs[:-outs]
    parts = len(ins) // 2
    total = dot(ins[0][...], ins[parts][...], TN)
    for k in range(1, parts):
        total = total + dot(ins[k][...], ins[parts + k][...], TN)
    refs[-outs][...] = total.astype(BF)
    if weighted:
        refs[-1][...] = jnp.sum(total * ins[-1][...].astype(F32), axis=0, keepdims=True)


def weight_grad(lefts, rights, offsets, weights=None):
    cols, width, here = lefts[0].shape[1], rights[0].shape[1], rights[0].shape[0]
    tile = 512
    count = len(lefts)

    def left_spec(offset):
        return pl.BlockSpec((here, cols), lambda i: (offset // here, 0))

    out_specs = [pl.BlockSpec((cols, tile), lambda i: (0, i))]
    out_shape = [jax.ShapeDtypeStruct((cols, width), BF)]
    extra, extra_specs = (), []
    if weights is not None:
        out_specs.append(pl.BlockSpec((1, tile), lambda i: (0, i)))
        out_shape.append(jax.ShapeDtypeStruct((1, width), F32))
        extra, extra_specs = (weights,), [pl.BlockSpec((cols, tile), lambda i: (0, i))]
    return pl.pallas_call(
        partial(grads_kernel, weights is not None),
        grid=(width // tile,),
        in_specs=[left_spec(offset) for offset in offsets]
        + [pl.BlockSpec((here, tile), lambda i: (0, i))] * count
        + extra_specs,
        out_specs=out_specs,
        out_shape=out_shape,
        compiler_params=params(),
        cost_estimate=cost(
            2 * count * here * width * cols, 2 * (count * here * (width + cols) + cols * width)
        ),
        name="weight_grad",
    )(*lefts, *rights, *extra)


def head_mask(shape, head, heads, turned):
    lane = lax.broadcasted_iota(jnp.int32, shape, 1)
    if turned:
        return (lane // HALF) % heads == head
    return lane // HEAD_DIM == head


def attend_kernel(first, q_ref, k_ref, v_ref, start_ref, o_ref, low_ref, lse_ref, scores, vcat):
    i = pl.program_id(0)
    rows, cols = q_ref.shape
    heads = cols // HEAD_DIM
    blocks = k_ref.shape[0] // rows

    @pl.when(i == 0)
    def _():
        for b in range(blocks):
            value = v_ref[b * rows : (b + 1) * rows, :]
            for h in range(heads):
                vcat[b, h * rows : (h + 1) * rows, :] = jnp.where(
                    head_mask((rows, cols), h, heads, False), value, jnp.zeros_like(value)
                )

    query = q_ref[...]
    parts = [
        jnp.where(head_mask((rows, cols), h, heads, True), query, jnp.zeros_like(query))
        for h in range(heads)
    ]
    start = start_ref[...]
    low = first[i]
    place = i * rows + lax.broadcasted_iota(jnp.int32, (rows, rows), 0)
    lane = lax.broadcasted_iota(jnp.int32, (rows, rows), 1)

    def score_block(j, tops):
        column = j * rows + lane
        keep = (column <= place) & (column >= start)
        key = k_ref[pl.ds(pl.multiple_of(j * rows, rows), rows), :]
        new = []
        for h in range(heads):
            score = jnp.where(keep, dot(parts[h], key, NT), MASKED_SCORE)
            scores[j, h] = score
            new.append(jnp.maximum(tops[h], jnp.max(score, axis=1, keepdims=True)))
        return tuple(new)

    tops = lax.fori_loop(
        low, i + 1, score_block, tuple(jnp.full((rows, 1), MASKED_SCORE, F32) for _ in range(heads))
    )

    def value_block(j, carry):
        sums, total = carry
        chances, new = [], []
        for h in range(heads):
            chance = jnp.exp(scores[j, h] - tops[h])
            new.append(sums[h] + jnp.sum(chance, axis=1, keepdims=True))
            chances.append(chance.astype(BF))
        total = total + dot(jnp.concatenate(chances, axis=1), vcat[j], NN)
        return tuple(new), total

    sums, total = lax.fori_loop(
        low,
        i + 1,
        value_block,
        (tuple(jnp.zeros((rows, 1), F32) for _ in range(heads)), jnp.zeros((rows, cols), F32)),
    )
    scale = jnp.zeros((rows, cols), F32)
    for h in range(heads):
        scale = jnp.where(head_mask((rows, cols), h, heads, False), 1.0 / sums[h], scale)
        lse_ref[:, h : h + 1] = tops[h] + jnp.log(sums[h])
    result = total * scale
    o_ref[...] = result
    low_ref[...] = result.astype(BF)


def attend(first, query, key, value, start_column, count):
    length, cols = query.shape
    heads = cols // HEAD_DIM
    size = length // count
    whole = pl.BlockSpec((length, cols), lambda i, first: (0, 0))
    return pl.pallas_call(
        attend_kernel,
        grid_spec=pltpu.PrefetchScalarGridSpec(
            num_scalar_prefetch=1,
            grid=(size,),
            in_specs=[
                pl.BlockSpec((count, cols), lambda i, first: (i, 0)),
                whole,
                whole,
                pl.BlockSpec((count, 1), lambda i, first: (i, 0)),
            ],
            out_specs=[
                pl.BlockSpec((count, cols), lambda i, first: (i, 0)),
                pl.BlockSpec((count, cols), lambda i, first: (i, 0)),
                pl.BlockSpec((count, heads), lambda i, first: (i, 0)),
            ],
            scratch_shapes=[
                pltpu.VMEM((size, heads, count, count), F32),
                pltpu.VMEM((size, heads * count, cols), BF),
            ],
        ),
        out_shape=[
            jax.ShapeDtypeStruct((length, cols), F32),
            jax.ShapeDtypeStruct((length, cols), BF),
            jax.ShapeDtypeStruct((length, heads), F32),
        ],
        compiler_params=params(),
        cost_estimate=cost(18 * length * length * cols, 10 * length * cols),
        name="attend",
    )(first, query, key, value, start_column)


def attend_back_kernel(
    first, spot, q_ref, k_ref, v_ref, do_ref, lse_ref, delta_ref, start_ref,
    cq_ref, sq_ref, ck_ref, sk_ref, out_ref, kcat, dk_ref, dv_ref,
):
    i = pl.program_id(0)
    rows, cols = q_ref.shape
    half = cols // 2
    heads = cols // HEAD_DIM
    blocks = k_ref.shape[0] // rows

    @pl.when(i == 0)
    def _():
        dk_ref[...] = jnp.zeros_like(dk_ref)
        dv_ref[...] = jnp.zeros_like(dv_ref)
        for b in range(blocks):
            key = k_ref[b * rows : (b + 1) * rows, :]
            for h in range(heads):
                kcat[b, h * rows : (h + 1) * rows, :] = jnp.where(
                    head_mask((rows, cols), h, heads, True), key, jnp.zeros_like(key)
                )

    query, grad = q_ref[...], do_ref[...]
    parts = [
        jnp.where(head_mask((rows, cols), h, heads, True), query, jnp.zeros_like(query))
        for h in range(heads)
    ]
    grads = [
        jnp.where(head_mask((rows, cols), h, heads, False), grad, jnp.zeros_like(grad))
        for h in range(heads)
    ]
    query_stack = jnp.concatenate(parts, axis=0)
    grad_stack = jnp.concatenate(grads, axis=0)
    start = start_ref[...]
    place = i * rows + lax.broadcasted_iota(jnp.int32, (rows, rows), 1)
    line = lax.broadcasted_iota(jnp.int32, (rows, rows), 0)

    def block(j, total):
        where = pl.ds(pl.multiple_of(j * rows, rows), rows)
        column = j * rows + line
        keep = (column <= place) & (column >= start)
        key, value = k_ref[where, :], v_ref[where, :]
        chances, slopes = [], []
        for h in range(heads):
            score = jnp.where(keep, dot(key, parts[h], NT), MASKED_SCORE)
            chance = jnp.exp(score - lse_ref[h : h + 1, :])
            product = dot(value, grads[h], NT)
            slopes.append((chance * (product - delta_ref[h : h + 1, :])).astype(BF))
            chances.append(chance.astype(BF))
        slope = jnp.concatenate(slopes, axis=1)
        dk_ref[where, :] += dot(slope, query_stack, NN)
        dv_ref[where, :] += dot(jnp.concatenate(chances, axis=1), grad_stack, NN)
        return total + dot(jnp.concatenate(slopes, axis=0), kcat[j], TN)

    total = lax.fori_loop(first[i], i + 1, block, jnp.zeros((rows, cols), F32))
    here = pl.ds(pl.multiple_of(i * rows, rows), rows)
    target = pl.ds(pl.multiple_of(spot[i] * rows, rows), rows)
    cq, sq = cq_ref[here, :], sq_ref[here, :]
    d1, d2 = total[:, :half], total[:, half:]
    out_ref[target, :half] = (d1 * cq + d2 * sq).astype(BF)
    out_ref[target, half:cols] = (d2 * cq - d1 * sq).astype(BF)

    @pl.when(i == pl.num_programs(0) - 1)
    def _():
        def finish(j, carry):
            where = pl.ds(pl.multiple_of(j * rows, rows), rows)
            goal = pl.ds(pl.multiple_of(spot[j] * rows, rows), rows)
            ck, sk = ck_ref[where, :], sk_ref[where, :]
            k1, k2 = dk_ref[where, :half], dk_ref[where, half:]
            out_ref[goal, cols : cols + half] = (k1 * ck + k2 * sk).astype(BF)
            out_ref[goal, cols + half : 2 * cols] = (k2 * ck - k1 * sk).astype(BF)
            out_ref[goal, 2 * cols :] = dv_ref[where, :].astype(BF)
            return carry

        lax.fori_loop(0, blocks, finish, 0)


def attend_back(first, spot, query, key, value, grad, lse, delta, start_row, tables, count):
    length, cols = query.shape
    heads = cols // HEAD_DIM
    size = length // count
    whole = pl.BlockSpec((length, cols), lambda i, *_: (0, 0))
    table = pl.BlockSpec((length, cols // 2), lambda i, *_: (0, 0))
    rows = pl.BlockSpec((count, cols), lambda i, *_: (i, 0))
    line = pl.BlockSpec((pl.squeezed, heads, count), lambda i, *_: (i, 0, 0))
    return pl.pallas_call(
        attend_back_kernel,
        grid_spec=pltpu.PrefetchScalarGridSpec(
            num_scalar_prefetch=2,
            grid=(size,),
            in_specs=[
                rows,
                whole,
                whole,
                rows,
                line,
                line,
                pl.BlockSpec((pl.squeezed, 1, count), lambda i, *_: (i, 0, 0)),
                table,
                table,
                table,
                table,
            ],
            out_specs=pl.BlockSpec((length, 3 * cols), lambda i, *_: (0, 0)),
            scratch_shapes=[
                pltpu.VMEM((size, heads * count, cols), BF),
                pltpu.VMEM((length, cols), F32),
                pltpu.VMEM((length, cols), F32),
            ],
        ),
        out_shape=jax.ShapeDtypeStruct((length, 3 * cols), BF),
        compiler_params=params(),
        cost_estimate=cost(24 * length * length * cols, 20 * length * cols),
        name="attend_back",
    )(first, spot, query, key, value, grad, lse, delta, start_row, *tables)


def xpos_tables(heads, scale, positions):
    pair_index = (jnp.arange(HALF * heads) % HALF).astype(F32)
    frequency = 10000.0 ** (-pair_index / HALF)
    angles = positions[:, None] * frequency[None, :]
    zeta_base = (pair_index / HALF + 0.4) / 1.4
    growth = zeta_base[None, :] ** ((positions[:, None] - SEQ_LEN // 2) / SCALE_BASE)
    cosine, sine = jnp.cos(angles), jnp.sin(angles)
    return cosine * growth * scale, sine * growth * scale, cosine / growth, sine / growth


def on_device(
    layer_input,
    segment_ids,
    cotangent,
    projections,
    output_weight,
    up_weight,
    down_weight,
    norm_gains,
    hidden_gain,
    decays,
    average_projections,
    average_output,
    average_up,
    average_down,
    average_gains,
    average_hidden,
):
    size = lax.axis_size("seq")
    groups = lax.axis_size("tensor")
    me = lax.axis_index("seq")
    group = lax.axis_index("tensor")
    chunks, count, width = layer_input.shape
    length = segment_ids.shape[1]
    block_cols = projections.shape[2]
    heads = width // HEAD_DIM
    per_block = block_cols // HEAD_DIM
    mine = heads // size
    cols = mine * HEAD_DIM
    even_split = per_block % size == 0
    units = up_weight.shape[1] // size
    hidden_cols = units * groups
    hidden_total = hidden_cols * size

    each = per_block // size if even_split else 0
    split = each * HEAD_DIM

    def to_order(rows):
        if not even_split:
            return rows
        shaped = rows.reshape((groups, size, split) + rows.shape[1:])
        return jnp.swapaxes(shaped, 0, 1).reshape(rows.shape)

    def from_order(rows):
        if not even_split:
            return rows
        shaped = rows.reshape((size, groups, split) + rows.shape[1:])
        return jnp.swapaxes(shaped, 0, 1).reshape(rows.shape)

    line = Line()
    masks = np.concatenate([np.arange(0, size, 2), np.arange(1, size, 2)]).astype(np.int32)
    place = (jnp.asarray(masks) ^ me).astype(jnp.int32)
    middle = length // 2
    halves = (0, 1)

    gains_all = lax.all_gather(norm_gains, "seq", axis=1, tiled=True).astype(F32)
    gain_attn, gain_ffn = gains_all[0], gains_all[2][None]
    gain_inner = to_order(gains_all[1]).reshape(size, 1, cols)
    inputs = [layer_input[c].astype(F32) for c in range(chunks)]
    normed = [row_norm(rows) for rows in inputs]
    sent_in = [(normed[c][0] * gain_attn).astype(BF) for c in range(chunks)]

    turned = projections.transpose(1, 2, 0)
    if even_split:
        sent = turned.reshape(3, size, split, count).transpose(1, 0, 2, 3)
        came = lax.all_to_all(sent, "seq", 0, 0, tiled=True)
        raw = lax.all_gather(came, "tensor", axis=0, tiled=False)
    else:
        wide = lax.all_gather(turned, "tensor", axis=1, tiled=True)
        sent = wide.reshape(3, size, cols, count).transpose(1, 0, 2, 3)
        came = lax.all_to_all(sent, "seq", 0, 0, tiled=True)
        raw = came[None]
    proj, proj_plain = arrange(raw)
    tall = lax.all_gather(after(output_weight, came), "tensor", axis=0, tiled=True)

    def swapped(kind):
        if kind == "up":
            sent = line.put(up_weight).reshape(count, size, units).transpose(1, 0, 2)
            return lax.all_to_all(sent, "seq", 0, 0, tiled=True).reshape(width, units)
        sent = line.put(down_weight).reshape(size, units, count)
        came = lax.all_to_all(sent, "seq", 0, 0, tiled=True)
        return came.transpose(1, 0, 2).reshape(units, width)

    gain_hidden = jnp.zeros((groups, units), BF)
    for k in range(groups):
        part = hidden_gain
        if k:
            part = lax.ppermute(part, "tensor", [(i, (i - k) % groups) for i in range(groups)])
        gain_hidden = lax.dynamic_update_slice(
            gain_hidden, part.reshape(1, units), ((group + k) % groups, 0)
        )
    gain_hidden = gain_hidden.astype(F32).reshape(1, hidden_cols)

    blocks = jnp.arange(size, dtype=jnp.int32) ^ me
    spot = (blocks & 1) * (size // 2) + (blocks >> 1)
    segments = lax.dynamic_slice_in_dim(segment_ids, group * chunks, chunks, 0)
    starts = jnp.sum((segments[:, None, :] < segments[:, :, None]).astype(jnp.int32), axis=2)
    firsts = starts.reshape(chunks, size, count)[:, :, 0] // count

    rows_of = {}

    def projected(c, h):
        before = rows_of.get(c) or [jnp.zeros((length, cols), BF) for _ in range(3)]
        rows_of[c] = project(
            line.enter(place[h * (size // 2) : (h + 1) * (size // 2)]),
            ins[c].halves[h],
            proj_plain,
            tables_turn,
            count,
            before,
        )
        line.mark(rows_of[c][0])

    def attention(c):
        attended, low, lse = attend(
            line.enter(firsts[c]), *rows_of[c], starts[c][:, None], count
        )
        line.mark(lse)
        came = lax.all_to_all(low.reshape(size, count, cols), "seq", 0, 0, tiled=True)
        return rows_of[c], attended, lse, came

    def mixed(c):
        result = out_project(
            line.enter(place),
            kept[c][3],
            pieces.halves,
            layer_input[c],
            gain_inner,
            gain_ffn,
            split,
        )
        line.mark(result[1])
        return result

    ins = [Gather(line, sent_in[0])]
    line.mark(ins[0].pieces[-1])
    ins[0].corner()
    ins.append(Gather(line, sent_in[1]))
    came_up = swapped("up")
    line.note(gain_hidden)
    turn = line.enter(jnp.arange(SEQ_LEN, dtype=F32))
    tables_turn = xpos_tables(mine, FACTOR, turn)
    line.mark(tables_turn[0])
    ins[0].core()
    line.note(came_up)
    came_down = swapped("down")
    up_parts = lax.all_gather(after(came_up, tall), "tensor", axis=0, tiled=False)
    proj, proj_plain = arrange(line.enter(raw))
    line.mark(proj)
    ins[1].corner()
    line.note(came_down)
    projected(0, 0)
    pieces = Gather(line, tall)
    projected(0, 1)
    ins[1].core()
    down = lax.all_gather(line.put(came_down), "tensor", axis=0, tiled=True)
    kept = [attention(0)]
    pieces.corner()
    cots = [Gather(line, cotangent[0])]
    projected(1, 0)
    projected(1, 1)
    pieces.core()
    kept.append(attention(1))
    cots[0].corner()
    line.note(kept[0][3])
    outs = [mixed(0)]
    cots[0].core()
    mids = [Gather(line, outs[0][2])]
    line.note(kept[1][3])
    outs.append(mixed(1))
    cots.append(Gather(line, cotangent[1]))

    def graded(c, h):
        scaled = ffn_grad(cots[c].halves[h], down, line.enter(gain_hidden))
        line.mark(scaled)
        return scaled

    def entered(c, h, scaled=None):
        if scaled is None:
            result = ffn_in(
                mids[c].halves[h], up_parts, None, cots[c].halves[h], down, line.enter(gain_hidden)
            )
        else:
            result = ffn_in(mids[c].halves[h], up_parts, line.enter(scaled))
        line.mark(result[3])
        return result

    def summed(held):
        stats = jnp.concatenate([held[h][3] for h in halves]).reshape(size, count, 4)
        return BlockSum(line, stats.transpose(0, 2, 1))

    def row_stats(sums):
        stats = sums.total() / hidden_total
        mean, second, plain, cross = (stats[:, k] for k in range(4))
        inverse = lax.rsqrt(second - mean * mean + EPSILON)
        cross = inverse * (cross - mean * plain)
        return jnp.stack([mean, inverse, plain, cross], axis=-1).reshape(length, 4)

    def left(c, h):
        result = ffn_out(
            held[c][h][:3], stats[c], line.enter(gain_hidden), up_parts, down, h * middle
        )
        line.mark(result[4])
        return result

    scaled0 = [graded(0, 0)]
    mids[0].corner()
    mids.append(Gather(line, outs[1][2]))
    scaled0.append(graded(0, 1))
    mids[0].core()
    cots[1].corner()
    held = [[entered(0, 0, scaled0[0])]]
    cots[1].core()
    mids[1].corner()
    held[0].append(entered(0, 1, scaled0[1]))
    mids[1].core()
    sums = [summed(held[0])]
    held.append([entered(1, 0)])
    sums[0].more()
    held[1].append(entered(1, 1))
    sums[0].more()
    sums.append(summed(held[1]))
    stats = [row_stats(sums[0])]
    done = [[None, None] for _ in range(chunks)]
    done[0][1] = left(0, 1)
    sums[1].more()
    mid_sums = [Scatter(line, done[0][1][2], count)]
    done[0][0] = left(0, 0)
    mid_sums[0].corner(done[0][0][2])
    sums[1].more()
    stats.append(row_stats(sums[1]))
    done[1][1] = left(1, 1)
    mid_sums[0].near()
    mid_sums.append(Scatter(line, done[1][1][2], count))
    done[1][0] = left(1, 0)
    mid_sums[1].corner(done[1][0][2])
    out_sums = [Scatter(line, done[0][1][3], count)]
    hidden_gain_grad = sum(done[c][h][4] for c in range(chunks) for h in halves)
    hidden_gain_grad = (hidden_gain_grad / gain_hidden).reshape(groups, units)
    down_grad = weight_grad(
        [line.enter(done[c][h][0]) for c in range(chunks) for h in halves],
        [cots[c].halves[h] for c in range(chunks) for h in halves],
        [0] * 4,
    )[0]
    line.mark(down_grad)
    scatter = partial(lax.psum_scatter, axis_name="tensor", scatter_dimension=0, tiled=True)
    down_own = scatter(down_grad)

    def back_out(c):
        residual_grad, attn_grad, sent, ffn_gain, inner_gain = out_back(
            line.enter(place),
            mid_sums[c].total(),
            outs[c][1],
            cotangent[c],
            kept[c][3],
            pieces.halves,
            gain_inner,
            gain_ffn,
            split,
        )
        line.mark(sent)
        grad = lax.all_to_all(sent, "seq", 0, 0, tiled=True).reshape(length, cols)
        return residual_grad, attn_grad, grad, ffn_gain[0], inner_gain.reshape(width)

    def back_attention(c):
        turned_rows, attended, lse, came = kept[c]
        grad = backs[c][2]
        delta = jnp.sum((grad.astype(F32) * attended).reshape(length, mine, HEAD_DIM), axis=2)
        slope = attend_back(
            line.enter(firsts[c]),
            spot,
            *turned_rows,
            grad,
            lse.reshape(size, count, mine).transpose(0, 2, 1),
            delta.reshape(size, count, mine).transpose(0, 2, 1),
            starts[c].reshape(size, 1, count),
            tables_turn,
            count,
        )
        line.mark(slope)
        return slope

    def times(rows, weights, offset):
        result = multiply(line.enter(rows), weights, offset, middle)
        line.mark(result)
        return result

    mid_sums[1].near()
    backs = [back_out(0)]
    out_sums[0].corner(done[0][0][3])
    out_sums.append(Scatter(line, done[1][1][3], count))
    up_grad = weight_grad(
        [line.enter(done[c][h][1]) for c in range(chunks) for h in halves],
        [mids[c].halves[h] for c in range(chunks) for h in halves],
        [0] * 4,
    )[0]
    line.mark(up_grad)
    up_own = scatter(up_grad)
    out_sums[0].near()
    backs.append(back_out(1))
    line.note(backs[0][2])
    output_grad = out_grad(
        [line.enter(outs[c][0]) for c in range(chunks)], [back[1] for back in backs], split
    )
    line.mark(output_grad)
    output_own = scatter(
        lax.psum_scatter(output_grad, "seq", scatter_dimension=0, tiled=True).reshape(width, count)
    )
    out_sums[1].corner(done[1][0][3])
    slopes = [back_attention(0)]
    out_sums[1].near()
    line.note(down_own, backs[1][2])
    odd = times(slopes[0], proj, middle)
    in_sums = [Scatter(line, odd, count)]
    even = times(slopes[0], proj, 0)
    in_sums[0].corner(even)
    slopes.append(back_attention(1))
    in_sums[0].near()
    line.note(up_own)
    odd = times(slopes[1], proj, middle)
    in_sums.append(Scatter(line, odd, count))
    even = times(slopes[1], proj, 0)
    in_sums[1].corner(even)
    proj_grad, attn_gain = weight_grad(
        [line.enter(slopes[c]) for c in range(chunks) for h in halves],
        [ins[c].halves[h] for c in range(chunks) for h in halves],
        [h * middle for c in range(chunks) for h in halves],
        proj,
    )
    line.mark(proj_grad)
    in_sums[1].near()

    outputs = [outs[c][1] + out_sums[c].total() for c in range(chunks)]
    input_grads = [
        backs[c][0] + row_norm_back(in_sums[c].total() * gain_attn, *normed[c])
        for c in range(chunks)
    ]
    gain_terms = jnp.stack(
        [
            attn_gain[0] / gain_attn,
            from_order(sum(back[4] for back in backs)),
            sum(back[3] for back in backs),
        ]
    )
    gains_grad = lax.psum(
        lax.psum_scatter(gain_terms, "seq", scatter_dimension=1, tiled=True), "tensor"
    )

    part = down_own.reshape(units, size, count).transpose(1, 0, 2)
    down_final = lax.all_to_all(part, "seq", 0, 0, tiled=True).reshape(size * units, count)
    part = up_own.reshape(units, size, count).transpose(1, 0, 2)
    part = lax.all_to_all(part, "seq", 0, 0, tiled=True)
    up_final = part.transpose(2, 0, 1).reshape(count, size * units)
    output_final = output_own
    part = proj_grad
    turned_heads = part[: 2 * cols].reshape(2, 2, mine, HALF, width).transpose(0, 2, 1, 3, 4)
    part = jnp.concatenate([turned_heads.reshape(2, cols, width), part[None, 2 * cols :]])
    if even_split:
        part = part.reshape(3, groups, split, width).transpose(1, 0, 2, 3)
        part = scatter(part.reshape(3 * cols, width))
        part = part.reshape(3, split, size, count).transpose(2, 0, 1, 3)
        part = lax.all_to_all(part, "seq", 0, 0, tiled=True)
        proj_final = part.transpose(3, 1, 0, 2).reshape(count, 3, block_cols)
    else:
        part = lax.psum(part, "tensor").reshape(3, cols, size, count).transpose(2, 0, 1, 3)
        part = lax.all_to_all(part, "seq", 0, 0, tiled=True)
        part = part.transpose(3, 1, 0, 2).reshape(count, 3, width)
        proj_final = lax.dynamic_slice_in_dim(part, group * block_cols, block_cols, 2)
    hidden_final = lax.psum_scatter(
        hidden_gain_grad, "tensor", scatter_dimension=0, tiled=True
    )

    grads = (
        proj_final.astype(F32),
        output_final.astype(F32),
        up_final.astype(F32),
        down_final.astype(F32),
        gains_grad.astype(F32),
        hidden_final.astype(F32),
    )
    averages = (
        average_projections,
        average_output,
        average_up,
        average_down,
        average_gains,
        average_hidden,
    )
    updated = tuple(
        decays[i] * averages[i] + (1.0 - decays[i]) * grads[i] for i in range(6)
    )
    return (jnp.stack(outputs).astype(BF), jnp.stack(input_grads)) + grads + updated


def solution(mesh):
    weights = (P("seq", None, "tensor"), P("tensor", "seq"), P("seq", "tensor"), P("tensor", "seq"))
    gains = (P(None, "seq"), P("tensor", "seq"))
    rows = P("tensor", "seq", None)
    return jax.shard_map(
        on_device,
        mesh=mesh,
        in_specs=(rows, P(), rows) + weights + gains + (P(),) + weights + gains,
        out_specs=(rows, rows) + weights + gains + weights + gains,
        check_vma=False,
    )
```
